32 devices in a mesh: groups: 2 (over y), dp: 4 (over z), tensor: 4 (over x, core).
Axes of the slice: x: 2, y: 2, z: 4, core: 2. Of those that a mesh axis runs over, the one named last changes fastest.
Arguments:
- tokens: bfloat16 [3584, 4096], P(('groups', 'dp'), 'tensor'), parts along dimension 0, may hold values from -6 to 6
- frozen: bfloat16 [4096, 15360], P('dp', 'tensor'), may hold values from -0.09375 to 0.09375
- delta: bfloat16 [16, 128, 128], P('tensor'), may hold values from -0.5 to 0.5
- block_rows: int32 [16], P('tensor'), may hold values from 0 to 31, as said below
- block_cols: int32 [16], P('tensor'), may hold values from 0 to 119, as said below
- owners: int32 [16, 1], P('tensor'), may hold values from 0 to 3; in each aligned block of 4 rows (0 to 3, 4 to 7, ...) at most 2 rows name the same one
- d_out: bfloat16 [3584, 15360], P(('groups', 'dp'), 'tensor'), parts along dimension 0, may hold values from -6 to 6
Outputs:
- activated: bfloat16 [3584, 15360], P(('groups', 'dp'), 'tensor'), parts along dimension 0
- d_tokens: bfloat16 [3584, 4096], P(('groups', 'dp'), 'tensor'), parts along dimension 0
- block_grads: float32 [4, 16, 128, 128], P('tensor', ('groups', 'dp')), parts along dimension 1
The draws below stay inside these ranges and needn't reach their ends.
There are 2 independent parts, one for each index of `groups`. The reference program is written for one: setup_inputs(seed, part) draws one part's arguments, and reference() takes and returns one part's arrays. A program takes and returns all parts, laid end to end along the dimension named above; an argument that names none is the same for every part. Nothing has to cross between parts.
Inputs may be any that keep to these rules, and one draw needn't show every extreme that they name: The blocks 4 j to 4 j + 3 are distinct in (block_rows, block_cols) within that range of blocks. The blocks 4 j to 4 j + 3 have block_cols in j * (30) to (j + 1) * 30 - 1. `owners`: among the 4 blocks 4 j to 4 j + 3 no index is named more than 2 times; in some such range one is named exactly 2 times.
All inputs are finite; a program needn't handle non-finite values.
Results may differ from the reference program's by a relative error of at most 0.012.
Values may be sent and summed in bfloat16 or wider, within the bound.
No kernel may reach another device: no remote copies, remote signals or barrier semaphores. Data moves between devices by JAX's collectives and lax.ppermute only.
A program may use at most 192 MiB of HBM per device.

```python
import math
import jax
import jax.numpy as jnp
import numpy as np
from jax import lax

D = 4096
FF = 15360
BS = 128
CAP = 2
TOKENS = 1792
NBT = 4
BLOCKS = 16
N_DP = 4
N_TENSOR = 4


def block_cells(key):
    cell_count = D // BS * (FF // (BS * N_TENSOR))
    slab_keys = jax.random.split(key, N_TENSOR + 1)
    middle = jax.random.randint(slab_keys[N_TENSOR], (N_TENSOR,), 0, cell_count).astype(jnp.int32)
    slab_ids = jnp.arange(N_TENSOR, dtype=jnp.int32)
    forced = jnp.where(slab_ids == 0, 0, jnp.where(slab_ids == N_TENSOR - 1, cell_count - 1, middle)).astype(jnp.int32)
    forced = jnp.where(slab_ids == 0, 0, forced).astype(jnp.int32)

    def choose(slab_key, first_cell):
        others = jax.random.permutation(slab_key, cell_count - 1)[:NBT].astype(jnp.int32)
        others = (first_cell + 1 + others) % cell_count
        return others.at[0].set(first_cell)
    return jax.vmap(choose)(slab_keys[:N_TENSOR], forced).astype(jnp.int32)


def draw_block_rows(key, part):
    picked = block_cells(key)
    per_slab = FF // (BS * N_TENSOR)
    return (picked // per_slab).reshape(-1).astype(jnp.int32)


def draw_block_cols(key, part):
    picked = block_cells(key)
    per_slab = FF // (BS * N_TENSOR)
    slab_ids = jnp.arange(N_TENSOR, dtype=jnp.int32)[:, None]
    return (slab_ids * per_slab + picked % per_slab).reshape(-1).astype(jnp.int32)


def block_scale(key, extent, pieces, smallest, high):
    factor_of, own = 1.0, jax.random.fold_in(key, 6)
    for dim, parts in pieces:
        heights = jnp.exp(jax.random.uniform(jax.random.fold_in(own, dim), (parts,), jnp.float32, smallest / len(pieces), high / len(pieces)))
        factor_of = factor_of * jnp.repeat(heights, extent[dim] // parts).reshape([-1 if axis == dim else 1 for axis in range(len(extent))])
    return factor_of


def assign_block(stream_key, own, number, rows, count, top, limit, lean):
    ranking = jax.random.permutation(stream_key, count)
    heavy_load, usual = portions_of(count, rows * top, limit, lean, True), portions_of(count, rows * top, limit, lean, False)
    places = jnp.arange(count)

    def named(tallies, rotation):
        used = int((tallies > 0).sum())
        fixed = max(1, used // 4)
        passed = fixed + (places - fixed + rotation * (used - fixed)) % max(1, count - fixed)
        return jnp.zeros((count,), jnp.int32).at[ranking[jnp.where(places < fixed, places, passed)]].set(jnp.asarray(tallies, jnp.int32))

    tallies = jnp.where(number % 4 == 0, named(heavy_load, number // 4), named(usual, number - number // 4 - 1))
    mixed = jax.random.permutation(jax.random.fold_in(own, 3), count)
    donor, receiver = mixed[0:count // 2 * 2:2], mixed[1:count // 2 * 2:2]
    room = jnp.minimum(tallies[donor] - 1, limit - tallies[receiver]) // 2
    room = jnp.where((donor == ranking[0]) | (receiver == ranking[0]) | (tallies[receiver] == 0), 0, jnp.maximum(room, 0))
    passed = jax.random.randint(jax.random.fold_in(own, 4), (count // 2,), 0, 1 << 20) % (room + 1)
    tallies = tallies.at[donor].add(-passed).at[receiver].add(passed)
    labels = jnp.searchsorted(jnp.cumsum(tallies), jnp.arange(rows * top), side="right").astype(jnp.int32)
    grid = labels.reshape(top, rows).T
    grid = grid[jax.random.permutation(jax.random.fold_in(own, 1), rows)]
    rotation = jax.random.randint(jax.random.fold_in(own, 2), (rows, 1), 0, top)
    return jnp.take_along_axis(grid, (jnp.arange(top)[None, :] + rotation) % top, axis=1)


def portions_of(count, total, bound, slope, full):
    portions = [(1 << 20) // math.isqrt(grade ** slope) + 1 for grade in range(1, count + 1)]
    largest = bound if full else min(bound, max(-(-total // count), total * portions[0] // sum(portions)))
    least = 1 if total - largest >= count - 1 else 0
    holding, rest = [largest] + [least] * (count - 1), total - largest - least * (count - 1)
    while rest > 0:
        movable = [i for i in range(1, count) if holding[i] < largest] or [i for i in range(1, count) if holding[i] < bound]
        mass, remaining = sum([portions[i] for i in movable]), rest
        for i in movable:
            extra = min(bound - holding[i], max(1, remaining * portions[i] // mass), rest)
            holding[i] = holding[i] + extra
            rest = rest - extra
    return np.array(holding)


def bell_draw(stream_key, dims, scale, reach, cuts=(), kind=jnp.bfloat16):
    entries = scale * jax.random.normal(stream_key, dims, jnp.float32)
    if cuts:
        entries = entries * block_scale(stream_key, dims, cuts, -0.22, 0.18)
    return jnp.clip(entries, -reach, reach).astype(kind)


def setup_inputs(seed: int = 0, part: int = 0) -> dict:
    splits = jax.random.split(jax.random.key(seed), 8)
    part_splits = jax.random.split(jax.random.fold_in(splits[7], part), 8)
    tokens = bell_draw(part_splits[0], (TOKENS, D), 1.0, 6.0, ((0, 4), (1, 4)))
    frozen = bell_draw(splits[1], (D, FF), D ** -0.5, 0.09375, ((0, 4), (1, 4)))
    delta = bell_draw(splits[2], (BLOCKS, BS, BS), BS ** -0.5, 0.5, ((0, 4),))
    block_rows = draw_block_rows(jax.random.fold_in(splits[7], 71), part)
    block_cols = draw_block_cols(jax.random.fold_in(splits[7], 71), part)
    owners_keys = jax.random.split(jax.random.fold_in(splits[5], 1), BLOCKS // NBT)
    owners_turns = jax.random.permutation(jax.random.fold_in(splits[5], 3), BLOCKS // NBT)
    owners = jax.vmap(lambda own, number: assign_block(jax.random.fold_in(splits[5], 2), own, number, NBT, N_DP, 1, CAP, 2))(owners_keys, owners_turns).reshape((BLOCKS, 1))
    d_out = bell_draw(part_splits[6], (TOKENS, FF), 1.0, 6.0, ((0, 4), (1, 4)))
    return dict(tokens=tokens, frozen=frozen, delta=delta, block_rows=block_rows, block_cols=block_cols, owners=owners, d_out=d_out)


def reference(tokens, frozen, delta, block_rows, block_cols, owners, d_out):
    rows_total = tokens.shape[0]
    x_blocks = jnp.take(tokens.reshape(rows_total, D // BS, BS), block_rows, axis=1).astype(jnp.float32)
    delta_wide = delta.astype(jnp.float32)
    preact = jnp.dot(tokens, frozen, preferred_element_type=jnp.float32)
    contrib = jnp.einsum("tnk,nkc->tnc", x_blocks, delta_wide, precision=lax.Precision.HIGHEST)
    preact = preact.reshape(rows_total, FF // BS, BS).at[:, block_cols].add(contrib).reshape(rows_total, FF)
    squash = jax.nn.sigmoid(preact)
    activated = (preact * squash).astype(jnp.bfloat16)
    d_pre = (d_out.astype(jnp.float32) * squash * (1.0 + preact * (1.0 - squash))).astype(jnp.bfloat16)
    dy_blocks = jnp.take(d_pre.reshape(rows_total, FF // BS, BS), block_cols, axis=1).astype(jnp.float32)
    back_rows = jnp.einsum("tnc,nkc->tnk", dy_blocks, delta_wide, precision=lax.Precision.HIGHEST)
    slab_width = FF // N_TENSOR

    def slab_term(total, slab_index):
        start = (slab_index * slab_width).astype(jnp.int32)
        slab_grad = lax.dynamic_slice_in_dim(d_pre, start, slab_width, 1)
        slab_weight = lax.dynamic_slice_in_dim(frozen, start, slab_width, 1)
        partial_rows = lax.dot_general(slab_grad, slab_weight, (((1,), (1,)), ((), ())), preferred_element_type=jnp.float32)
        first_block = (slab_index * NBT).astype(jnp.int32)
        slab_back = lax.dynamic_slice_in_dim(back_rows, first_block, NBT, 1)
        slab_rows = lax.dynamic_slice_in_dim(block_rows, first_block, NBT, 0)
        partial_rows = partial_rows.reshape(rows_total, D // BS, BS).at[:, slab_rows].add(slab_back).reshape(rows_total, D)
        rounded = lax.optimization_barrier(partial_rows.astype(jnp.bfloat16))
        return total + rounded.astype(total.dtype), None

    d_rows, unused = lax.scan(slab_term, jnp.zeros((rows_total, D), jnp.float32), jnp.arange(N_TENSOR, dtype=jnp.int32))
    d_tokens = d_rows.astype(jnp.bfloat16)
    block_grad = jnp.einsum("tnk,tnc->nkc", x_blocks, dy_blocks, precision=lax.Precision.HIGHEST) * (TOKENS ** -0.5)
    owner_ids = owners[:, 0]
    block_ids = jnp.arange(BLOCKS, dtype=jnp.int32)
    shard_ids = block_ids // NBT
    earlier = (owner_ids[None, :] == owner_ids[:, None]) & (shard_ids[None, :] == shard_ids[:, None]) & (block_ids[None, :] < block_ids[:, None])
    slot_ids = owner_ids * CAP + jnp.sum(earlier.astype(jnp.int32), axis=1)
    block_grads = jnp.zeros((N_TENSOR, N_DP * CAP, BS, BS), jnp.float32).at[shard_ids, slot_ids].set(block_grad)
    return activated, d_tokens, block_grads
```

```python
import jax
import jax.numpy as jnp
from jax import lax
from jax.sharding import PartitionSpec as P

CAP = 2
BF = jnp.bfloat16
F32 = jnp.float32


def swap(array, axis, bit):
    size = lax.axis_size(axis)
    return lax.ppermute(array, axis, [(i, i ^ bit) for i in range(size)])


def merge_blocks(weight, delta, first_rows, first_cols):
    size = delta.shape[1]
    for n in range(delta.shape[0]):
        row, col = first_rows[n], first_cols[n]
        inside = (row >= 0) & (row < weight.shape[0]) & (col >= 0) & (col < weight.shape[1])
        at = (jnp.clip(row, 0, weight.shape[0] - size), jnp.clip(col, 0, weight.shape[1] - size))
        old = lax.dynamic_slice(weight, at, (size, size))
        new = (old.astype(F32) + delta[n].astype(F32)).astype(BF)
        weight = lax.dynamic_update_slice(weight, jnp.where(inside, new, old), at)
    return weight


def split_sizes(width, unit):
    blocks = width // unit
    if width % unit or blocks < 8:
        return [width]
    sizes = []
    for parts in (5, 4, 3, 2):
        take = -(-blocks // parts) if parts > 2 else blocks // 2 + blocks % 2
        sizes.append(take * unit)
        blocks -= take
    sizes.append(blocks * unit)
    return [s for s in sizes if s]


def local(tokens, frozen, delta, block_rows, block_cols, owners, d_out):
    group, me_dp, me_t = (lax.axis_index(a) for a in ("groups", "dp", "tensor"))
    n_dp, n_tensor = lax.axis_size("dp"), lax.axis_size("tensor")
    rows, feats = tokens.shape
    block_count, bs = delta.shape[0], delta.shape[1]
    slab = frozen.shape[1]
    half = slab // 2
    width = feats * n_tensor
    mine, theirs = group * half, (1 - group) * half

    first_rows = block_rows * bs - me_dp * frozen.shape[0]
    slab_cols = block_cols * bs - me_t * slab
    if half % bs == 0:
        weight = lax.dynamic_slice(frozen, (0, mine), (frozen.shape[0], half))
        weight = merge_blocks(weight, delta, first_rows, slab_cols - mine)
    else:
        weight = merge_blocks(frozen, delta, first_rows, slab_cols)
        weight = lax.dynamic_slice(weight, (0, mine), (frozen.shape[0], half))

    x_two = jnp.concatenate([tokens, swap(tokens, "groups", 1)], axis=0)
    if n_tensor == 4:
        own, other = x_two, swap(x_two, "tensor", 2)
        own_c, other_c = swap(own, "tensor", 1), swap(other, "tensor", 1)
        x_full = jnp.zeros((2 * rows, width), BF)
        for bit, part in ((0, own), (2, other), (1, own_c), (3, other_c)):
            x_full = lax.dynamic_update_slice(x_full, part, (0, (me_t ^ bit) * feats))
    else:
        x_full = lax.all_gather(x_two, "tensor", axis=1, tiled=True)

    give = lax.dynamic_slice(d_out, (0, theirs), (rows, half))
    keep = lax.dynamic_slice(d_out, (0, mine), (rows, half))
    d_two = jnp.concatenate([keep, swap(give, "groups", 1)], axis=0)

    sizes = split_sizes(half, bs)
    activated = jnp.zeros((rows, slab), BF)
    d_rows = None
    slopes = []
    history = []
    first = 0
    for number, size in enumerate(sizes):
        shard = weight[:, first : first + size]
        if number >= 2:
            shard, history[number - 2] = lax.optimization_barrier((shard, history[number - 2]))
        segment = lax.all_gather(shard, "dp", axis=0, tiled=True)
        preact = jnp.dot(x_full, segment, preferred_element_type=F32)
        squash = jax.nn.sigmoid(preact)
        act = (preact * squash).astype(BF)
        d_slope = (
            d_two[:, first : first + size].astype(F32) * squash * (1.0 + preact * (1.0 - squash))
        ).astype(BF)
        slopes.append(d_slope)
        back = swap(act[rows:], "groups", 1)
        activated = lax.dynamic_update_slice(activated, act[:rows], (0, mine + first))
        activated = lax.dynamic_update_slice(activated, back, (0, theirs + first))
        term = lax.dot_general(
            d_slope, segment, (((1,), (1,)), ((), ())), preferred_element_type=F32
        )
        d_rows = term if d_rows is None else d_rows + term
        history.append(d_slope)
        first += size

    if n_tensor == 4:
        parts = d_rows.reshape(2 * rows, 2, 2, feats)
        core = me_t % 2
        side = me_t // 2
        send = lax.dynamic_slice_in_dim(parts, 1 - core, 1, 2)[:, :, 0].astype(BF)
        stay = lax.dynamic_slice_in_dim(parts, core, 1, 2)[:, :, 0]
        both = stay + swap(send, "tensor", 1).astype(F32)
        near = lax.dynamic_slice_in_dim(both, side, 1, 1)[:, 0]
        far = lax.dynamic_slice_in_dim(both, 1 - side, 1, 1)[:, 0]
        cut = rows // 2
        near_own, near_peer = near[:rows], near[rows:]
        far_own, far_peer = far[:rows], far[rows:].astype(BF)
        over_x = swap(far_peer[:cut], "tensor", 2).astype(F32)
        over_y = swap(far_peer[cut:], "groups", 1).astype(F32)
        near_peer = jnp.concatenate([near_peer[:cut] + over_x, near_peer[cut:]], axis=0)
        far_own = jnp.concatenate([far_own[:cut], far_own[cut:] + over_y], axis=0)
        from_y = swap(near_peer.astype(BF), "groups", 1).astype(F32)
        from_x = swap(far_own.astype(BF), "tensor", 2).astype(F32)
        d_tokens = (near_own + from_x + from_y).astype(BF)
    else:
        summed = lax.psum_scatter(d_rows.astype(BF), "tensor", scatter_dimension=1, tiled=True)
        d_tokens = (
            summed[:rows].astype(F32) + swap(summed[rows:], "groups", 1).astype(F32)
        ).astype(BF)

    d_pre = jnp.concatenate(
        [jnp.zeros((2 * rows, bs), BF)] + slopes + [jnp.zeros((2 * rows, bs), BF)], axis=1
    )
    starts = jnp.clip(slab_cols - mine + bs, 0, half + bs)
    dy = jnp.stack(
        [lax.dynamic_slice(d_pre, (0, starts[n]), (2 * rows, bs)) for n in range(block_count)]
    ).reshape(block_count, 2, rows, bs)
    xb = jnp.stack(
        [
            lax.dynamic_slice(x_full, (0, block_rows[n] * bs), (2 * rows, bs))
            for n in range(block_count)
        ]
    ).reshape(block_count, 2, rows, bs)
    grads = jnp.einsum("ngtk,ngtc->gnkc", xb, dy, preferred_element_type=F32)
    grads = grads[0] + swap(grads[1].astype(BF), "groups", 1).astype(F32)
    norm = float(rows * n_dp) ** (-0.5)
    everyone = lax.all_gather(grads.astype(BF), "dp", axis=0)
    total = jnp.sum(everyone.astype(F32), axis=0) * norm
    owner_ids = owners[:, 0]
    order = jnp.arange(block_count, dtype=jnp.int32)
    earlier = (owner_ids[None, :] == owner_ids[:, None]) & (order[None, :] < order[:, None])
    rank = jnp.sum(earlier.astype(jnp.int32), axis=1)
    wanted = (owner_ids[None, :] == me_dp) & (
        rank[None, :] == jnp.arange(CAP, dtype=jnp.int32)[:, None]
    )
    bucket = jnp.sum(jnp.where(wanted[:, :, None, None], total[None], 0.0), axis=1)
    return (activated, d_tokens, bucket[None])


def solution(mesh):
    in_specs = (
        P(("groups", "dp"), "tensor"),
        P("dp", "tensor"),
        P("tensor", None, None),
        P("tensor"),
        P("tensor"),
        P("tensor", None),
        P(("groups", "dp"), "tensor"),
    )
    out_specs = (
        P(("groups", "dp"), "tensor"),
        P(("groups", "dp"), "tensor"),
        P("tensor", ("groups", "dp"), None, None),
    )
    return jax.shard_map(local, mesh=mesh, in_specs=in_specs, out_specs=out_specs, check_vma=False)
```

```python
import functools

import jax
import jax.numpy as jnp
from jax import lax
from jax.experimental import pallas as pl
from jax.experimental.pallas import tpu as pltpu
from jax.sharding import PartitionSpec as P

CAP = 2
BF = jnp.bfloat16
F32 = jnp.float32
VMEM_BYTES = 56 * 2**20


def swap(array, axis, bit):
    size = lax.axis_size(axis)
    return lax.ppermute(array, axis, [(i, i ^ bit) for i in range(size)])


def params():
    return pltpu.CompilerParams(vmem_limit_bytes=VMEM_BYTES)


def forward_kernel(n_x, n_w, first, blocks, bs, meta, *refs):
    x_refs, w_refs = refs[:n_x], refs[n_x : n_x + n_w]
    delta_ref, d_ref, act_ref, slope_ref, acc = refs[n_x + n_w :]
    feats = x_refs[0].shape[1]
    width = acc.shape[1]
    total = None
    for k in range(n_x):
        part = meta[k]
        if n_w == 1:
            weight = w_refs[0][pl.ds(pl.multiple_of(part * feats, feats), feats), :]
        else:
            weight = w_refs[k][...]
        term = jnp.dot(x_refs[k][...], weight, preferred_element_type=F32)
        total = term if total is None else total + term
    acc[...] = total
    for n in range(blocks):
        row, col = meta[8 + 2 * n], meta[9 + 2 * n] - first
        here = (col >= 0) & (col < width)
        for k in range(n_x):
            offset = row - meta[k] * feats

            @pl.when(here & (offset >= 0) & (offset < feats))
            def _():
                cols = pl.ds(pl.multiple_of(col, bs), bs)
                xs = x_refs[k][:, pl.ds(pl.multiple_of(offset, bs), bs)]
                acc[:, cols] += jnp.dot(xs, delta_ref[n], preferred_element_type=F32)

    preact = acc[...]
    squash = jax.nn.sigmoid(preact)
    act_ref[0] = (preact * squash).astype(BF)
    slope_ref[...] = (
        d_ref[...].astype(F32) * squash * (1.0 + preact * (1.0 - squash))
    ).astype(BF)


def forward(meta, xs, ws, delta, d_piece, first, groups_of):
    rows, width = d_piece.shape
    feats = xs[0].shape[1]
    tile = rows // groups_of
    blocks, bs = delta.shape[0], delta.shape[1]
    flops = 2 * rows * feats * len(xs) * width
    return pl.pallas_call(
        functools.partial(forward_kernel, len(xs), len(ws), first, blocks, bs),
        grid_spec=pltpu.PrefetchScalarGridSpec(
            num_scalar_prefetch=1,
            grid=(groups_of,),
            in_specs=[pl.BlockSpec((tile, feats), lambda i, m: (i, 0)) for _ in xs]
            + [
                pl.BlockSpec(w.shape, lambda i, m: (0, 0), pipeline_mode=pl.Buffered(1))
                for w in ws
            ]
            + [
                pl.BlockSpec(delta.shape, lambda i, m: (0, 0, 0)),
                pl.BlockSpec((tile, width), lambda i, m: (i, 0)),
            ],
            out_specs=[
                pl.BlockSpec((1, tile, width), lambda i, m: (i, 0, 0)),
                pl.BlockSpec((tile, width), lambda i, m: (i, 0)),
            ],
            scratch_shapes=[pltpu.VMEM((tile, width), F32)],
        ),
        out_shape=[
            jax.ShapeDtypeStruct((groups_of, tile, width), BF),
            jax.ShapeDtypeStruct((rows, width), BF),
        ],
        compiler_params=params(),
        cost_estimate=pl.CostEstimate(
            flops=flops, bytes_accessed=2 * (rows + width) * feats * len(xs), transcendentals=0
        ),
    )(meta, *xs, *ws, delta, d_piece)


def backward_kernel(firsts, blocks, bs, meta, *refs):
    n = len(firsts)
    slopes, w_refs = refs[:n], refs[n : 2 * n]
    delta_ref, out_ref, acc = refs[2 * n :]
    size = acc.shape[1]
    base = meta[0] * (size * pl.num_programs(0)) + pl.program_id(0) * size
    total = None
    for p in range(n):
        term = lax.dot_general(
            slopes[p][...], w_refs[p][...], (((1,), (1,)), ((), ())), preferred_element_type=F32
        )
        total = term if total is None else total + term
    acc[...] = total
    for b in range(blocks):
        row = meta[8 + 2 * b] - base
        for p in range(n):
            col = meta[9 + 2 * b] - firsts[p]

            @pl.when((row >= 0) & (row < size) & (col >= 0) & (col < slopes[p].shape[1]))
            def _():
                ds = slopes[p][:, pl.ds(pl.multiple_of(col, bs), bs)]
                acc[:, pl.ds(pl.multiple_of(row, bs), bs)] += lax.dot_general(
                    ds, delta_ref[b], (((1,), (1,)), ((), ())), preferred_element_type=F32
                )

    out_ref[...] = acc[...].astype(out_ref.dtype)


def backward(meta, slopes, ws, delta, firsts, feats, out_type):
    rows = slopes[0].shape[0]
    blocks, bs = delta.shape[0], delta.shape[1]
    tiles = 4
    size = feats // tiles
    width = sum(s.shape[1] for s in slopes)
    return pl.pallas_call(
        functools.partial(backward_kernel, firsts, blocks, bs),
        grid_spec=pltpu.PrefetchScalarGridSpec(
            num_scalar_prefetch=1,
            grid=(tiles,),
            in_specs=[
                pl.BlockSpec(s.shape, lambda i, m: (0, 0), pipeline_mode=pl.Buffered(1))
                for s in slopes
            ]
            + [
                pl.BlockSpec((size, w.shape[1]), lambda i, m: (m[0] * tiles + i, 0)) for w in ws
            ]
            + [pl.BlockSpec(delta.shape, lambda i, m: (0, 0, 0))],
            out_specs=pl.BlockSpec((rows, size), lambda i, m: (0, i)),
            scratch_shapes=[pltpu.VMEM((rows, size), F32)],
        ),
        out_shape=jax.ShapeDtypeStruct((rows, feats), out_type),
        compiler_params=params(),
        cost_estimate=pl.CostEstimate(
            flops=2 * rows * feats * width,
            bytes_accessed=2 * (rows + feats) * width,
            transcendentals=0,
        ),
    )(meta, *slopes, *ws, delta)


def slot_ranks(owners):
    owner_ids = owners[:, 0]
    order = jnp.arange(owner_ids.shape[0], dtype=jnp.int32)
    earlier = (owner_ids[None, :] == owner_ids[:, None]) & (order[None, :] < order[:, None])
    rank = jnp.sum(earlier.astype(jnp.int32), axis=1)
    return (owner_ids[None, :] == lax.axis_index("dp")) & (
        rank[None, :] == jnp.arange(CAP, dtype=jnp.int32)[:, None]
    )


def pick_slots(owners, total):
    wanted = slot_ranks(owners)
    return jnp.sum(jnp.where(wanted[:, :, None, None], total[None], 0.0), axis=1)[None]


def tie(*values):
    return lax.optimization_barrier(values)


def piece_sizes(half, bs):
    blocks = half // bs
    if blocks < 12:
        return [half]
    last = 4
    rest = blocks - last
    return [(rest - rest // 2) * bs, rest // 2 * bs, last * bs]


def local(tokens, frozen, delta, block_rows, block_cols, owners, d_out):
    group, me_dp, me_t = (lax.axis_index(a) for a in ("groups", "dp", "tensor"))
    n_dp, n_tensor = lax.axis_size("dp"), lax.axis_size("tensor")
    rows, feats = tokens.shape
    blocks, bs = delta.shape[0], delta.shape[1]
    slab = frozen.shape[1]
    half = slab // 2
    mine, theirs = group * half, (1 - group) * half
    sizes = piece_sizes(half, bs)
    firsts = [sum(sizes[:p]) for p in range(len(sizes))]
    block_cols_here = block_cols * bs - me_t * slab - mine
    block_info = jnp.stack([block_rows * bs, block_cols_here], axis=1).reshape(-1)
    parts = [me_t ^ k for k in range(4)]

    def meta_of(*head):
        lead = jnp.stack(list(head) + [jnp.int32(0)] * (8 - len(head)))
        return jnp.concatenate([lead, block_info]).astype(jnp.int32)

    gathered = []
    for first, size in zip(firsts, sizes):
        shard = lax.dynamic_slice(frozen, (0, mine + first), (frozen.shape[0], size))
        gathered.append(lax.all_gather(shard, "dp", axis=0, tiled=True))

    peer = swap(tokens, "groups", 1)
    own_x = swap(tokens, "tensor", 2)
    peer_x = swap(peer, "tensor", 2)
    near_x = jnp.concatenate([tokens, peer], axis=0)
    far_x = jnp.concatenate([own_x, peer_x], axis=0)
    xs = [near_x, swap(near_x, "tensor", 1), far_x, swap(far_x, "tensor", 1)]

    order = peer_x
    d_pieces = []
    for first, size in zip(firsts, sizes):
        give = lax.dynamic_slice(d_out, (0, theirs + first), (rows, size))
        keep = lax.dynamic_slice(d_out, (0, mine + first), (rows, size))
        give, order = tie(give, order)
        got = swap(give, "groups", 1)
        order = got
        d_pieces.append(jnp.concatenate([keep, got], axis=0))

    activated = jnp.zeros((rows, slab), BF)
    slopes = []
    meta = meta_of(*parts)
    for first, size, weight, d_piece in zip(firsts, sizes, gathered, d_pieces):
        act, slope = forward(meta, xs, [weight], delta, d_piece, first, 2)
        slopes.append(slope)
        back = swap(act[1], "groups", 1)
        activated = lax.dynamic_update_slice(activated, act[0], (0, mine + first))
        activated = lax.dynamic_update_slice(activated, back, (0, theirs + first))

    def back_of(bit, out_type, wait=None):
        m = meta_of(me_t ^ bit)
        if wait is not None:
            m, wait = tie(m, wait)
        return backward(m, slopes, gathered, delta, firsts, feats, out_type)

    far_give = back_of(3, BF)
    far_got = swap(far_give, "tensor", 1)
    far_stay = back_of(2, F32, far_give)
    near_give = back_of(1, BF, far_stay)
    near_got = swap(near_give, "tensor", 1)
    near_stay = back_of(0, F32, near_give)
    cut = rows // 2
    far_peer = (far_stay[rows:] + far_got[rows:].astype(F32)).astype(BF)
    over_x = swap(far_peer[:cut], "tensor", 2)
    over_y = swap(far_peer[cut:], "groups", 1)
    far_own = far_stay[:rows] + far_got[:rows].astype(F32)
    far_own = jnp.concatenate([far_own[:cut], far_own[cut:] + over_y.astype(F32)], 0).astype(BF)
    from_x = swap(far_own, "tensor", 2)
    near_peer = near_stay[rows:] + near_got[rows:].astype(F32)
    near_peer = jnp.concatenate([near_peer[:cut] + over_x.astype(F32), near_peer[cut:]], 0)
    from_y = swap(near_peer.astype(BF), "groups", 1)
    near_own = near_stay[:rows] + near_got[:rows].astype(F32)
    d_tokens = (near_own + from_x.astype(F32) + from_y.astype(F32)).astype(BF)

    grads = []
    for n in range(blocks):
        dy = jnp.zeros((2 * rows, bs), BF)
        for first, size, slope in zip(firsts, sizes, slopes):
            col = block_cols_here[n] - first
            cut_out = lax.dynamic_slice(slope, (0, jnp.clip(col, 0, size - bs)), (2 * rows, bs))
            dy = jnp.where((col >= 0) & (col < size), cut_out, dy)
        xb = jnp.zeros((2 * rows, bs), BF)
        for k in range(4):
            off = block_rows[n] * bs - parts[k] * feats
            cut_out = lax.dynamic_slice(xs[k], (0, jnp.clip(off, 0, feats - bs)), (2 * rows, bs))
            xb = jnp.where((off >= 0) & (off < feats), cut_out, xb)
        xb, dy = xb.reshape(2, rows, bs), dy.reshape(2, rows, bs)
        grads.append(jnp.einsum("gtk,gtc->gkc", xb, dy, preferred_element_type=F32))
    grads = jnp.stack(grads, axis=1)
    grads = grads[0] + swap(grads[1].astype(BF), "groups", 1).astype(F32)
    bit = 1
    while bit < n_dp:
        grads = grads + swap(grads.astype(BF), "dp", bit).astype(F32)
        bit *= 2
    norm = float(rows * n_dp) ** (-0.5)
    return (activated, d_tokens, pick_slots(owners, grads * norm))


def local_any(tokens, frozen, delta, block_rows, block_cols, owners, d_out):
    me_dp, me_t, n_dp = lax.axis_index("dp"), lax.axis_index("tensor"), lax.axis_size("dp")
    rows = tokens.shape[0]
    blocks, bs = delta.shape[0], delta.shape[1]
    slab = frozen.shape[1]
    x_full = lax.all_gather(tokens, "tensor", axis=1, tiled=True)
    weight = lax.all_gather(frozen, "dp", axis=0, tiled=True)
    width = x_full.shape[1]
    row_pick = (block_rows[:, None] == jnp.arange(width // bs)[None, :]).astype(F32)
    cols_here = block_cols - me_t * (slab // bs)
    col_pick = (cols_here[:, None] == jnp.arange(slab // bs)[None, :]).astype(F32)
    highest = lax.Precision.HIGHEST
    xb = jnp.take(x_full.reshape(rows, width // bs, bs), block_rows, axis=1)
    contrib = jnp.einsum("tnk,nkc->tnc", xb, delta, preferred_element_type=F32)
    add = jnp.einsum("tnc,nm->tmc", contrib, col_pick, precision=highest).reshape(rows, slab)
    preact = jnp.dot(x_full, weight, preferred_element_type=F32) + add
    squash = jax.nn.sigmoid(preact)
    activated = (preact * squash).astype(BF)
    d_pre = (d_out.astype(F32) * squash * (1.0 + preact * (1.0 - squash))).astype(BF)
    d_rows = lax.dot_general(
        d_pre, weight, (((1,), (1,)), ((), ())), preferred_element_type=F32
    )
    dy = jnp.take(d_pre.reshape(rows, slab // bs, bs), cols_here, axis=1)
    back = jnp.einsum("tnc,nkc->tnk", dy, delta, preferred_element_type=F32)
    back = jnp.einsum("tnk,nr->trk", back, row_pick, precision=highest).reshape(rows, width)
    d_tokens = lax.psum_scatter(
        (d_rows + back).astype(BF), "tensor", scatter_dimension=1, tiled=True
    )
    grads = jnp.einsum("tnk,tnc->nkc", xb, dy, preferred_element_type=F32)
    everyone = lax.all_gather(grads.astype(BF), "dp", axis=0).astype(F32)
    norm = float(rows * n_dp) ** (-0.5)
    return (activated, d_tokens, pick_slots(owners, jnp.sum(everyone, axis=0) * norm))


def solution(mesh):
    sizes = dict(mesh.shape)
    small = sizes["groups"] == 2 and sizes["dp"] == 4 and sizes["tensor"] == 4
    body = local if small else local_any
    in_specs = (
        P(("groups", "dp"), "tensor"),
        P("dp", "tensor"),
        P("tensor", None, None),
        P("tensor"),
        P("tensor"),
        P("tensor", None),
        P(("groups", "dp"), "tensor"),
    )
    out_specs = (
        P(("groups", "dp"), "tensor"),
        P(("groups", "dp"), "tensor"),
        P("tensor", ("groups", "dp"), None, None),
    )
    return jax.shard_map(body, mesh=mesh, in_specs=in_specs, out_specs=out_specs, check_vma=False)
```

```python
import functools

import jax
import jax.numpy as jnp
from jax import lax
from jax.experimental import pallas as pl
from jax.experimental.pallas import tpu as pltpu
from jax.sharding import PartitionSpec as P

CAP = 2
BF = jnp.bfloat16
F32 = jnp.float32
VMEM_BYTES = 56 * 2**20


def swap(array, axis, bit):
    size = lax.axis_size(axis)
    return lax.ppermute(array, axis, [(i, i ^ bit) for i in range(size)])


def params():
    return pltpu.CompilerParams(vmem_limit_bytes=VMEM_BYTES)


def forward_kernel(first, blocks, bs, meta, x_ref, w_ref, delta_ref, d_ref, act_ref, slope_ref, acc):
    width = acc.shape[1]
    total = None
    for s in range(w_ref.shape[0]):
        term = jnp.dot(x_ref[meta[s]], w_ref[s], preferred_element_type=F32)
        total = term if total is None else total + term
    acc[...] = total
    for n in range(blocks):
        col = meta[11 + 4 * n] - first

        @pl.when((col >= 0) & (col < width))
        def _():
            cols = pl.ds(pl.multiple_of(col, bs), bs)
            rows = pl.ds(pl.multiple_of(meta[10 + 4 * n], bs), bs)
            xs = x_ref[meta[8 + 4 * n], :, rows]
            acc[:, cols] += jnp.dot(xs, delta_ref[n], preferred_element_type=F32)

    preact = acc[...]
    squash = jax.nn.sigmoid(preact)
    act_ref[0] = (preact * squash).astype(BF)
    slope_ref[...] = (
        d_ref[...].astype(F32) * squash * (1.0 + preact * (1.0 - squash))
    ).astype(BF)


def forward(meta, x4, w4, delta, d_piece, first, groups_of):
    rows, width = d_piece.shape
    slots, feats = w4.shape[0], w4.shape[1]
    tile = rows // groups_of
    blocks, bs = delta.shape[0], delta.shape[1]
    return pl.pallas_call(
        functools.partial(forward_kernel, first, blocks, bs),
        grid_spec=pltpu.PrefetchScalarGridSpec(
            num_scalar_prefetch=1,
            grid=(groups_of,),
            in_specs=[
                pl.BlockSpec((slots, tile, feats), lambda i, m: (0, i, 0)),
                pl.BlockSpec(w4.shape, lambda i, m: (0, 0, 0), pipeline_mode=pl.Buffered(1)),
                pl.BlockSpec(delta.shape, lambda i, m: (0, 0, 0)),
                pl.BlockSpec((tile, width), lambda i, m: (i, 0)),
            ],
            out_specs=[
                pl.BlockSpec((1, tile, width), lambda i, m: (i, 0, 0)),
                pl.BlockSpec((tile, width), lambda i, m: (i, 0)),
            ],
            scratch_shapes=[pltpu.VMEM((tile, width), F32)],
        ),
        out_shape=[
            jax.ShapeDtypeStruct((groups_of, tile, width), BF),
            jax.ShapeDtypeStruct((rows, width), BF),
        ],
        compiler_params=params(),
        cost_estimate=pl.CostEstimate(
            flops=2 * rows * feats * slots * width,
            bytes_accessed=2 * (rows + width) * feats * slots,
            transcendentals=0,
        ),
    )(meta, x4, w4, delta, d_piece)


def backward_kernel(firsts, blocks, bs, has_acc, meta, *refs):
    n = len(firsts)
    slopes, w_refs = refs[:n], refs[n : 2 * n]
    delta_ref = refs[2 * n]
    acc_in = refs[2 * n + 1] if has_acc else None
    outs, acc = refs[2 * n + 1 + has_acc : -1], refs[-1]
    size = acc.shape[1]
    slot = meta[4] + pl.program_id(0)
    base = pl.program_id(1) * size
    total = acc_in[0] if has_acc else None
    for p in range(n):
        term = lax.dot_general(
            slopes[p][...], w_refs[p][0], (((1,), (1,)), ((), ())), preferred_element_type=F32
        )
        total = term if total is None else total + term
    acc[...] = total
    for b in range(blocks):
        row = meta[10 + 4 * b] - base
        for p in range(n):
            col = meta[11 + 4 * b] - firsts[p]
            inside = (row >= 0) & (row < size) & (col >= 0) & (col < slopes[p].shape[1])

            @pl.when(inside & (meta[9 + 4 * b] == slot))
            def _():
                ds = slopes[p][:, pl.ds(pl.multiple_of(col, bs), bs)]
                acc[:, pl.ds(pl.multiple_of(row, bs), bs)] += lax.dot_general(
                    ds, delta_ref[b], (((1,), (1,)), ((), ())), preferred_element_type=F32
                )

    if len(outs) == 1:
        outs[0][0] = acc[...]
    else:
        cut = outs[0].shape[0]
        outs[0][...] = acc[:cut].astype(outs[0].dtype)
        outs[1][...] = acc[cut:].astype(outs[1].dtype)


def backward(meta, slopes, ws, delta, firsts, acc, out_type):
    rows = slopes[0].shape[0]
    slots, feats = ws[0].shape[0], ws[0].shape[1]
    blocks, bs = delta.shape[0], delta.shape[1]
    tiles = 2
    size = feats // tiles
    width = sum(s.shape[1] for s in slopes)
    every = out_type is None
    steps = slots if every else 1
    whole = pl.BlockSpec((1, rows, size), lambda s, i, m: (m[4] + s, 0, i))
    half = pl.BlockSpec((rows // 2, size), lambda s, i, m: (0, i))
    if every:
        out_specs = [whole]
        out_shape = [jax.ShapeDtypeStruct((slots, rows, feats), F32)]
    else:
        out_specs = [half, half]
        out_shape = [jax.ShapeDtypeStruct((rows // 2, feats), out_type)] * 2
    return pl.pallas_call(
        functools.partial(backward_kernel, firsts, blocks, bs, acc is not None),
        grid_spec=pltpu.PrefetchScalarGridSpec(
            num_scalar_prefetch=1,
            grid=(steps, tiles),
            in_specs=[
                pl.BlockSpec(s.shape, lambda s, i, m: (0, 0), pipeline_mode=pl.Buffered(1))
                for s in slopes
            ]
            + [
                pl.BlockSpec((1, size, w.shape[2]), lambda s, i, m: (m[4] + s, i, 0)) for w in ws
            ]
            + [pl.BlockSpec(delta.shape, lambda s, i, m: (0, 0, 0))]
            + ([] if acc is None else [whole]),
            out_specs=out_specs,
            scratch_shapes=[pltpu.VMEM((rows, size), F32)],
        ),
        out_shape=out_shape,
        compiler_params=params(),
        cost_estimate=pl.CostEstimate(
            flops=2 * rows * feats * width * steps,
            bytes_accessed=2 * (rows + feats) * width * steps,
            transcendentals=0,
        ),
    )(meta, *slopes, *ws, delta, *([] if acc is None else [acc]))


def slot_ranks(owners):
    owner_ids = owners[:, 0]
    order = jnp.arange(owner_ids.shape[0], dtype=jnp.int32)
    earlier = (owner_ids[None, :] == owner_ids[:, None]) & (order[None, :] < order[:, None])
    rank = jnp.sum(earlier.astype(jnp.int32), axis=1)
    return (owner_ids[None, :] == lax.axis_index("dp")) & (
        rank[None, :] == jnp.arange(CAP, dtype=jnp.int32)[:, None]
    )


def pick_slots(owners, total):
    wanted = slot_ranks(owners)
    return jnp.sum(jnp.where(wanted[:, :, None, None], total[None], 0.0), axis=1)[None]


def tie(value, *after):
    return lax.optimization_barrier((value,) + after)[0]


def piece_sizes(half, bs):
    blocks = half // bs
    last = max(blocks // 7, 1)
    sizes = []
    for left in (3, 2, 1):
        take = -(-(blocks - last - sum(sizes)) // left)
        sizes.append(take)
    return [s * bs for s in sizes + [last]]


def gather_line(shards):
    pairs = [(0, 1), (1, 0), (2, 3), (3, 2)]
    middle = [(1, 2), (2, 1)]
    outward = [(1, 0), (2, 3)]
    flights = []
    centre = []
    out = []

    def outer(value, route):
        if len(flights) >= 2:
            value = tie(value, flights[-2])
        got = lax.ppermute(value, "dp", route)
        flights.append(got)
        return got

    def inner(value):
        if len(centre) >= 2:
            value = tie(value, centre[-2])
        got = lax.ppermute(value, "dp", middle)
        centre.append(got)
        return got

    for shard in shards:
        a = outer(shard, pairs)
        b = inner(shard)
        c = inner(a)
        e = outer(b, outward)
        f = outer(c, outward)
        out.append(jnp.stack([shard, a, c + e, b + f]))
    return out


def local(tokens, frozen, delta, block_rows, block_cols, owners, d_out):
    group, me_dp, me_t = (lax.axis_index(a) for a in ("groups", "dp", "tensor"))
    n_dp = lax.axis_size("dp")
    rows, feats = tokens.shape
    blocks, bs = delta.shape[0], delta.shape[1]
    slab = frozen.shape[1]
    half = slab // 2
    mine, theirs = group * half, (1 - group) * half
    sizes = piece_sizes(half, bs)
    firsts = [sum(sizes[:p]) for p in range(len(sizes))]
    cols_here = block_cols * bs - me_t * slab - mine
    row_part = block_rows * bs // feats
    block_info = jnp.stack(
        [row_part ^ me_t, row_part ^ me_dp, block_rows * bs % feats, cols_here], axis=1
    ).reshape(-1)

    def meta_of(slot):
        head = [me_dp ^ me_t ^ s for s in range(4)] + [slot] + [jnp.int32(0)] * 3
        return jnp.concatenate([jnp.stack(head), block_info]).astype(jnp.int32)

    shards = [
        lax.dynamic_slice(frozen, (0, mine + first), (frozen.shape[0], size))
        for first, size in zip(firsts, sizes)
    ]
    gathered = gather_line(shards)

    peer = swap(tokens, "groups", 1)
    own_x = swap(tokens, "tensor", 2)
    peer_x = swap(peer, "tensor", 2)
    near_x = jnp.concatenate([tokens, peer], axis=0)
    far_x = jnp.concatenate([own_x, peer_x], axis=0)
    x4 = jnp.stack([near_x, swap(near_x, "tensor", 1), far_x, swap(far_x, "tensor", 1)])

    order = peer_x
    d_pieces = []
    for first, size in zip(firsts, sizes):
        give = lax.dynamic_slice(d_out, (0, theirs + first), (rows, size))
        keep = lax.dynamic_slice(d_out, (0, mine + first), (rows, size))
        got = swap(tie(give, order), "groups", 1)
        order = got
        d_pieces.append(jnp.concatenate([keep, got], axis=0))

    activated = jnp.zeros((rows, slab), BF)
    slopes = []
    meta = meta_of(jnp.int32(0))
    early = None
    for p, (first, size) in enumerate(zip(firsts, sizes)):
        if p == 3:
            meta = tie(meta, early)
        act, slope = forward(meta, x4, gathered[p], delta, d_pieces[p], first, 2)
        slopes.append(slope)
        back = swap(act[1], "groups", 1)
        activated = lax.dynamic_update_slice(activated, act[0], (0, mine + first))
        activated = lax.dynamic_update_slice(activated, back, (0, theirs + first))
        if p == 1:
            (early,) = backward(meta, slopes, gathered[:2], delta, firsts[:2], None, None)

    def back_of(bit, out_type, *wait):
        m = meta_of(me_t ^ bit ^ me_dp)
        if wait:
            m = tie(m, *wait)
        return backward(m, slopes[2:], gathered[2:], delta, firsts[2:], early, out_type)

    far_own_give, far_peer_give = back_of(3, BF)
    far_peer_got = swap(far_peer_give, "tensor", 1)
    far_own_got = swap(far_own_give, "tensor", 1)
    far_own, far_peer = back_of(2, F32, far_peer_give)
    near_own_give, near_peer_give = back_of(1, BF, far_own)
    near_peer_got = swap(near_peer_give, "tensor", 1)
    near_own_got = swap(near_own_give, "tensor", 1)
    near_own, near_peer = back_of(0, F32, near_peer_give)
    cut = rows // 2
    far_peer = (far_peer + far_peer_got.astype(F32)).astype(BF)
    over_x = swap(far_peer[:cut], "tensor", 2).astype(F32)
    over_y = swap(far_peer[cut:], "groups", 1).astype(F32)
    far_own = far_own + far_own_got.astype(F32)
    far_own = jnp.concatenate([far_own[:cut], far_own[cut:] + over_y], axis=0).astype(BF)
    from_x = swap(far_own, "tensor", 2)
    near_peer = near_peer + near_peer_got.astype(F32)
    near_peer = jnp.concatenate([near_peer[:cut] + over_x, near_peer[cut:]], axis=0).astype(BF)
    from_y = swap(near_peer, "groups", 1)
    near_own = near_own + near_own_got.astype(F32)
    d_tokens = (near_own + from_x.astype(F32) + from_y.astype(F32)).astype(BF)

    last_slope = tie(slopes[-1], near_own)
    grads = []
    for n in range(blocks):
        dy = jnp.zeros((2 * rows, bs), BF)
        for first, size, slope in zip(firsts, sizes, slopes[:-1] + [last_slope]):
            col = cols_here[n] - first
            cut_out = lax.dynamic_slice(slope, (0, jnp.clip(col, 0, size - bs)), (2 * rows, bs))
            dy = jnp.where((col >= 0) & (col < size), cut_out, dy)
        xb = lax.dynamic_slice(
            x4, (row_part[n] ^ me_t, 0, block_rows[n] * bs % feats), (1, 2 * rows, bs)
        )
        xb, dy = xb.reshape(2, rows, bs), dy.reshape(2, rows, bs)
        grads.append(jnp.einsum("gtk,gtc->gkc", xb, dy, preferred_element_type=F32))
    grads = jnp.stack(grads, axis=1)
    grads = grads[0] + swap(grads[1].astype(BF), "groups", 1).astype(F32)
    bit = 1
    while bit < n_dp:
        grads = grads + swap(grads.astype(BF), "dp", bit).astype(F32)
        bit *= 2
    norm = float(rows * n_dp) ** (-0.5)
    return (activated, d_tokens, pick_slots(owners, grads * norm))


def local_any(tokens, frozen, delta, block_rows, block_cols, owners, d_out):
    me_dp, me_t, n_dp = lax.axis_index("dp"), lax.axis_index("tensor"), lax.axis_size("dp")
    rows = tokens.shape[0]
    blocks, bs = delta.shape[0], delta.shape[1]
    slab = frozen.shape[1]
    x_full = lax.all_gather(tokens, "tensor", axis=1, tiled=True)
    weight = lax.all_gather(frozen, "dp", axis=0, tiled=True)
    width = x_full.shape[1]
    row_pick = (block_rows[:, None] == jnp.arange(width // bs)[None, :]).astype(F32)
    cols_here = block_cols - me_t * (slab // bs)
    col_pick = (cols_here[:, None] == jnp.arange(slab // bs)[None, :]).astype(F32)
    highest = lax.Precision.HIGHEST
    xb = jnp.take(x_full.reshape(rows, width // bs, bs), block_rows, axis=1)
    contrib = jnp.einsum("tnk,nkc->tnc", xb, delta, preferred_element_type=F32)
    add = jnp.einsum("tnc,nm->tmc", contrib, col_pick, precision=highest).reshape(rows, slab)
    preact = jnp.dot(x_full, weight, preferred_element_type=F32) + add
    squash = jax.nn.sigmoid(preact)
    activated = (preact * squash).astype(BF)
    d_pre = (d_out.astype(F32) * squash * (1.0 + preact * (1.0 - squash))).astype(BF)
    d_rows = lax.dot_general(
        d_pre, weight, (((1,), (1,)), ((), ())), preferred_element_type=F32
    )
    dy = jnp.take(d_pre.reshape(rows, slab // bs, bs), cols_here, axis=1)
    back = jnp.einsum("tnc,nkc->tnk", dy, delta, preferred_element_type=F32)
    back = jnp.einsum("tnk,nr->trk", back, row_pick, precision=highest).reshape(rows, width)
    d_tokens = lax.psum_scatter(
        (d_rows + back).astype(BF), "tensor", scatter_dimension=1, tiled=True
    )
    grads = jnp.einsum("tnk,tnc->nkc", xb, dy, preferred_element_type=F32)
    everyone = lax.all_gather(grads.astype(BF), "dp", axis=0).astype(F32)
    norm = float(rows * n_dp) ** (-0.5)
    return (activated, d_tokens, pick_slots(owners, jnp.sum(everyone, axis=0) * norm))


def solution(mesh):
    sizes = dict(mesh.shape)
    small = sizes["groups"] == 2 and sizes["dp"] == 4 and sizes["tensor"] == 4
    body = local if small else local_any
    in_specs = (
        P(("groups", "dp"), "tensor"),
        P("dp", "tensor"),
        P("tensor", None, None),
        P("tensor"),
        P("tensor"),
        P("tensor", None),
        P(("groups", "dp"), "tensor"),
    )
    out_specs = (
        P(("groups", "dp"), "tensor"),
        P(("groups", "dp"), "tensor"),
        P("tensor", ("groups", "dp"), None, None),
    )
    return jax.shard_map(body, mesh=mesh, in_specs=in_specs, out_specs=out_specs, check_vma=False)
```

```python
import functools

import jax
import jax.numpy as jnp
from jax import lax
from jax.experimental import pallas as pl
from jax.experimental.pallas import tpu as pltpu
from jax.sharding import PartitionSpec as P

CAP = 2
BF = jnp.bfloat16
F32 = jnp.float32
VMEM_BYTES = 56 * 2**20


def swap(array, axis, bit):
    size = lax.axis_size(axis)
    return lax.ppermute(array, axis, [(i, i ^ bit) for i in range(size)])


def params():
    return pltpu.CompilerParams(vmem_limit_bytes=VMEM_BYTES)


def forward_kernel(first, blocks, bs, meta, x_ref, w_ref, delta_ref, d_ref, act_ref, slope_ref, acc):
    width = acc.shape[1]
    total = None
    for s in range(w_ref.shape[0]):
        term = jnp.dot(x_ref[meta[s]], w_ref[s], preferred_element_type=F32)
        total = term if total is None else total + term
    acc[...] = total
    for n in range(blocks):
        col = meta[11 + 4 * n] - first

        @pl.when((col >= 0) & (col < width))
        def _():
            cols = pl.ds(pl.multiple_of(col, bs), bs)
            rows = pl.ds(pl.multiple_of(meta[10 + 4 * n], bs), bs)
            xs = x_ref[meta[8 + 4 * n], :, rows]
            acc[:, cols] += jnp.dot(xs, delta_ref[n], preferred_element_type=F32)

    preact = acc[...]
    squash = jax.nn.sigmoid(preact)
    act_ref[0] = (preact * squash).astype(BF)
    slope_ref[...] = (
        d_ref[...].astype(F32) * squash * (1.0 + preact * (1.0 - squash))
    ).astype(BF)


def forward(meta, x4, w4, delta, d_piece, first, groups_of):
    rows, width = d_piece.shape
    slots, feats = w4.shape[0], w4.shape[1]
    cuts = 2
    tile = rows // groups_of // cuts
    blocks, bs = delta.shape[0], delta.shape[1]
    return pl.pallas_call(
        functools.partial(forward_kernel, first, blocks, bs),
        grid_spec=pltpu.PrefetchScalarGridSpec(
            num_scalar_prefetch=1,
            grid=(groups_of * cuts,),
            in_specs=[
                pl.BlockSpec((slots, tile, feats), lambda i, m: (0, i, 0)),
                pl.BlockSpec(w4.shape, lambda i, m: (0, 0, 0), pipeline_mode=pl.Buffered(1)),
                pl.BlockSpec(delta.shape, lambda i, m: (0, 0, 0)),
                pl.BlockSpec((tile, width), lambda i, m: (i, 0)),
            ],
            out_specs=[
                pl.BlockSpec((1, tile, width), lambda i, m: (i // cuts, i % cuts, 0)),
                pl.BlockSpec((tile, width), lambda i, m: (i, 0)),
            ],
            scratch_shapes=[pltpu.VMEM((tile, width), F32)],
        ),
        out_shape=[
            jax.ShapeDtypeStruct((groups_of, rows // groups_of, width), BF),
            jax.ShapeDtypeStruct((rows, width), BF),
        ],
        compiler_params=params(),
        cost_estimate=pl.CostEstimate(
            flops=2 * rows * feats * slots * width,
            bytes_accessed=2 * (rows + width) * feats * slots,
            transcendentals=0,
        ),
    )(meta, x4, w4, delta, d_piece)


def backward_kernel(firsts, blocks, bs, has_acc, meta, *refs):
    n = len(firsts)
    slopes, w_refs = refs[:n], refs[n : 2 * n]
    delta_ref = refs[2 * n]
    acc_in = refs[2 * n + 1] if has_acc else None
    outs, acc = refs[2 * n + 1 + has_acc : -1], refs[-1]
    size = acc.shape[1]
    slot = meta[4] + pl.program_id(0)
    base = pl.program_id(1) * size
    total = acc_in[0] if has_acc else None
    for p in range(n):
        term = lax.dot_general(
            slopes[p][...], w_refs[p][0], (((1,), (1,)), ((), ())), preferred_element_type=F32
        )
        total = term if total is None else total + term
    acc[...] = total
    for b in range(blocks):
        row = meta[10 + 4 * b] - base
        for p in range(n):
            col = meta[11 + 4 * b] - firsts[p]
            inside = (row >= 0) & (row < size) & (col >= 0) & (col < slopes[p].shape[1])

            @pl.when(inside & (meta[9 + 4 * b] == slot))
            def _():
                ds = slopes[p][:, pl.ds(pl.multiple_of(col, bs), bs)]
                acc[:, pl.ds(pl.multiple_of(row, bs), bs)] += lax.dot_general(
                    ds, delta_ref[b], (((1,), (1,)), ((), ())), preferred_element_type=F32
                )

    if len(outs) == 1:
        outs[0][0] = acc[...]
    else:
        cut = outs[0].shape[0]
        outs[0][...] = acc[:cut].astype(outs[0].dtype)
        outs[1][...] = acc[cut:].astype(outs[1].dtype)


def weight_block(piece, step, tile, meta):
    return jnp.bitwise_xor(meta[4] + step, meta[5 + piece]), tile, 0


def backward(meta, slopes, ws, delta, firsts, acc, out_type):
    rows = slopes[0].shape[0]
    slots, feats = ws[0].shape[0], ws[0].shape[1]
    blocks, bs = delta.shape[0], delta.shape[1]
    tiles = 4
    size = feats // tiles
    width = sum(s.shape[1] for s in slopes)
    every = out_type is None
    steps = slots if every else 1
    whole = pl.BlockSpec((1, rows, size), lambda s, i, m: (m[4] + s, 0, i))
    half = pl.BlockSpec((rows // 2, size), lambda s, i, m: (0, i))
    if every:
        out_specs = [whole]
        out_shape = [jax.ShapeDtypeStruct((slots, rows, feats), F32)]
    else:
        out_specs = [half, half]
        out_shape = [jax.ShapeDtypeStruct((rows // 2, feats), out_type)] * 2
    return pl.pallas_call(
        functools.partial(backward_kernel, firsts, blocks, bs, acc is not None),
        grid_spec=pltpu.PrefetchScalarGridSpec(
            num_scalar_prefetch=1,
            grid=(steps, tiles),
            in_specs=[
                pl.BlockSpec(s.shape, lambda s, i, m: (0, 0), pipeline_mode=pl.Buffered(1))
                for s in slopes
            ]
            + [
                pl.BlockSpec((1, size, w.shape[2]), functools.partial(weight_block, p))
                for p, w in enumerate(ws)
            ]
            + [pl.BlockSpec(delta.shape, lambda s, i, m: (0, 0, 0))]
            + ([] if acc is None else [whole]),
            out_specs=out_specs,
            scratch_shapes=[pltpu.VMEM((rows, size), F32)],
        ),
        out_shape=out_shape,
        compiler_params=params(),
        cost_estimate=pl.CostEstimate(
            flops=2 * rows * feats * width * steps,
            bytes_accessed=2 * (rows + feats) * width * steps,
            transcendentals=0,
        ),
    )(meta, *slopes, *ws, delta, *([] if acc is None else [acc]))


def slot_ranks(owners):
    owner_ids = owners[:, 0]
    order = jnp.arange(owner_ids.shape[0], dtype=jnp.int32)
    earlier = (owner_ids[None, :] == owner_ids[:, None]) & (order[None, :] < order[:, None])
    rank = jnp.sum(earlier.astype(jnp.int32), axis=1)
    return (owner_ids[None, :] == lax.axis_index("dp")) & (
        rank[None, :] == jnp.arange(CAP, dtype=jnp.int32)[:, None]
    )


def pick_slots(owners, total):
    wanted = slot_ranks(owners)
    return jnp.sum(jnp.where(wanted[:, :, None, None], total[None], 0.0), axis=1)[None]


def tie(value, *after):
    return lax.optimization_barrier((value,) + after)[0]


def chain_line(shard):
    middle = [(1, 2), (2, 1)]
    outward = [(1, 0), (2, 3)]
    a = lax.ppermute(shard, "dp", [(0, 1), (1, 0), (2, 3), (3, 2)])
    b = lax.ppermute(shard, "dp", middle)
    c = lax.ppermute(a, "dp", middle)
    e = lax.ppermute(b, "dp", outward)
    f = lax.ppermute(c, "dp", outward)
    return jnp.stack([shard, a, c + e, b + f])


def piece_sizes(half, bs):
    blocks = half // bs
    chain, last = max(blocks // 3, 1), max(blocks // 5, 1)
    return [chain * bs, (blocks - chain - last) * bs, last * bs]


def local(tokens, frozen, delta, block_rows, block_cols, owners, d_out):
    group, me_dp, me_t = (lax.axis_index(a) for a in ("groups", "dp", "tensor"))
    n_dp = lax.axis_size("dp")
    rows, feats = tokens.shape
    blocks, bs = delta.shape[0], delta.shape[1]
    slab = frozen.shape[1]
    half = slab // 2
    mine, theirs = group * half, (1 - group) * half
    sizes = piece_sizes(half, bs)
    firsts = [sum(sizes[:p]) for p in range(len(sizes))]
    cols_here = block_cols * bs - me_t * slab - mine
    row_part = block_rows * bs // feats
    block_info = jnp.stack(
        [row_part ^ me_t, row_part, block_rows * bs % feats, cols_here], axis=1
    ).reshape(-1)
    zero = jnp.int32(0)

    def meta_of(mask, slot, *masks):
        head = [mask ^ me_t ^ s for s in range(4)] + [slot] + list(masks)
        head += [zero] * (8 - len(head))
        return jnp.concatenate([jnp.stack(head), block_info]).astype(jnp.int32)

    chain, first_shard, last_shard = [
        lax.dynamic_slice(frozen, (0, mine + first), (frozen.shape[0], size))
        for first, size in zip(firsts, sizes)
    ]
    gather_a = lax.all_gather(first_shard, "dp")
    chained = chain_line(chain)
    gather_b = lax.all_gather(tie(last_shard, gather_a, chained), "dp")
    gathered = [chained, gather_a, gather_b]
    masks = [me_dp, zero, zero]

    peer = swap(tokens, "groups", 1)
    own_x = swap(tokens, "tensor", 2)
    peer_x = swap(peer, "tensor", 2)
    near_x = jnp.concatenate([tokens, peer], axis=0)
    far_x = jnp.concatenate([own_x, peer_x], axis=0)
    x4 = jnp.stack([near_x, swap(near_x, "tensor", 1), far_x, swap(far_x, "tensor", 1)])

    order = peer_x
    d_pieces = []
    for first, size in zip(firsts, sizes):
        give = lax.dynamic_slice(d_out, (0, theirs + first), (rows, size))
        keep = lax.dynamic_slice(d_out, (0, mine + first), (rows, size))
        got = swap(tie(give, order), "groups", 1)
        order = got
        d_pieces.append(jnp.concatenate([keep, got], axis=0))

    activated = jnp.zeros((rows, slab), BF)
    slopes = []
    for p, (first, size) in enumerate(zip(firsts, sizes)):
        meta = meta_of(masks[p], zero)
        if p == 2:
            both = meta_of(zero, zero, *masks[:2])
            (early,) = backward(both, slopes, gathered[:2], delta, firsts[:2], None, None)
            meta = tie(meta, early, activated)
        act, slope = forward(meta, x4, gathered[p], delta, d_pieces[p], first, 2)
        slopes.append(slope)
        back = swap(act[1], "groups", 1)
        activated = lax.dynamic_update_slice(activated, act[0], (0, mine + first))
        activated = lax.dynamic_update_slice(activated, back, (0, theirs + first))

    def back_of(bit, out_type, *wait):
        m = meta_of(zero, me_t ^ bit, masks[2])
        if wait:
            m = tie(m, *wait)
        return backward(m, slopes[2:], gathered[2:], delta, firsts[2:], early, out_type)

    cut = rows // 2
    far_own_give, far_peer_give = back_of(3, BF)
    far_peer_got = swap(far_peer_give, "tensor", 1)
    far_own_got = swap(far_own_give, "tensor", 1)
    far_own, far_peer = back_of(2, F32, far_peer_give)
    far_peer = (far_peer + far_peer_got.astype(F32)).astype(BF)
    over_x = swap(far_peer[:cut], "tensor", 2)
    over_y = swap(far_peer[cut:], "groups", 1)
    near_own_give, near_peer_give = back_of(1, BF, far_peer)
    near_peer_got = swap(near_peer_give, "tensor", 1)
    near_own_got = swap(near_own_give, "tensor", 1)
    near_own, near_peer = back_of(0, F32, near_peer_give)

    last_slope = tie(slopes[-1], near_own)
    grads = []
    for n in range(blocks):
        dy = jnp.zeros((2 * rows, bs), BF)
        for first, size, slope in zip(firsts, sizes, slopes[:-1] + [last_slope]):
            col = cols_here[n] - first
            cut_out = lax.dynamic_slice(slope, (0, jnp.clip(col, 0, size - bs)), (2 * rows, bs))
            dy = jnp.where((col >= 0) & (col < size), cut_out, dy)
        xb = lax.dynamic_slice(
            x4, (row_part[n] ^ me_t, 0, block_rows[n] * bs % feats), (1, 2 * rows, bs)
        )
        xb, dy = xb.reshape(2, rows, bs), dy.reshape(2, rows, bs)
        grads.append(jnp.einsum("gtk,gtc->gkc", xb, dy, preferred_element_type=F32))
    grads = jnp.stack(grads, axis=1)
    grads_got = swap(grads[1].astype(BF), "groups", 1)

    far_own = far_own + far_own_got.astype(F32)
    far_own = jnp.concatenate([far_own[:cut], far_own[cut:] + over_y.astype(F32)], axis=0)
    from_x = swap(far_own.astype(BF), "tensor", 2)
    near_peer = near_peer + near_peer_got.astype(F32)
    near_peer = jnp.concatenate([near_peer[:cut] + over_x.astype(F32), near_peer[cut:]], axis=0)
    from_y = swap(near_peer.astype(BF), "groups", 1)
    grads = grads[0] + grads_got.astype(F32)
    sent = grads.astype(BF)
    shares = [swap(sent, "dp", bit) for bit in range(1, n_dp)]
    near_own = near_own + near_own_got.astype(F32)
    near_own = tie(near_own, *shares)
    d_tokens = (near_own + from_x.astype(F32) + from_y.astype(F32)).astype(BF)
    for share in shares:
        grads = grads + share.astype(F32)
    norm = float(rows * n_dp) ** (-0.5)
    return (activated, d_tokens, pick_slots(owners, grads * norm))


def local_any(tokens, frozen, delta, block_rows, block_cols, owners, d_out):
    me_dp, me_t, n_dp = lax.axis_index("dp"), lax.axis_index("tensor"), lax.axis_size("dp")
    rows = tokens.shape[0]
    blocks, bs = delta.shape[0], delta.shape[1]
    slab = frozen.shape[1]
    x_full = lax.all_gather(tokens, "tensor", axis=1, tiled=True)
    weight = lax.all_gather(frozen, "dp", axis=0, tiled=True)
    width = x_full.shape[1]
    row_pick = (block_rows[:, None] == jnp.arange(width // bs)[None, :]).astype(F32)
    cols_here = block_cols - me_t * (slab // bs)
    col_pick = (cols_here[:, None] == jnp.arange(slab // bs)[None, :]).astype(F32)
    highest = lax.Precision.HIGHEST
    xb = jnp.take(x_full.reshape(rows, width // bs, bs), block_rows, axis=1)
    contrib = jnp.einsum("tnk,nkc->tnc", xb, delta, preferred_element_type=F32)
    add = jnp.einsum("tnc,nm->tmc", contrib, col_pick, precision=highest).reshape(rows, slab)
    preact = jnp.dot(x_full, weight, preferred_element_type=F32) + add
    squash = jax.nn.sigmoid(preact)
    activated = (preact * squash).astype(BF)
    d_pre = (d_out.astype(F32) * squash * (1.0 + preact * (1.0 - squash))).astype(BF)
    d_rows = lax.dot_general(
        d_pre, weight, (((1,), (1,)), ((), ())), preferred_element_type=F32
    )
    dy = jnp.take(d_pre.reshape(rows, slab // bs, bs), cols_here, axis=1)
    back = jnp.einsum("tnc,nkc->tnk", dy, delta, preferred_element_type=F32)
    back = jnp.einsum("tnk,nr->trk", back, row_pick, precision=highest).reshape(rows, width)
    d_tokens = lax.psum_scatter(
        (d_rows + back).astype(BF), "tensor", scatter_dimension=1, tiled=True
    )
    grads = jnp.einsum("tnk,tnc->nkc", xb, dy, preferred_element_type=F32)
    everyone = lax.all_gather(grads.astype(BF), "dp", axis=0).astype(F32)
    norm = float(rows * n_dp) ** (-0.5)
    return (activated, d_tokens, pick_slots(owners, jnp.sum(everyone, axis=0) * norm))


def solution(mesh):
    sizes = dict(mesh.shape)
    small = sizes["groups"] == 2 and sizes["dp"] == 4 and sizes["tensor"] == 4
    body = local if small else local_any
    in_specs = (
        P(("groups", "dp"), "tensor"),
        P("dp", "tensor"),
        P("tensor", None, None),
        P("tensor"),
        P("tensor"),
        P("tensor", None),
        P(("groups", "dp"), "tensor"),
    )
    out_specs = (
        P(("groups", "dp"), "tensor"),
        P(("groups", "dp"), "tensor"),
        P("tensor", ("groups", "dp"), None, None),
    )
    return jax.shard_map(body, mesh=mesh, in_specs=in_specs, out_specs=out_specs, check_vma=False)
```

```python
import functools

import jax
import jax.numpy as jnp
from jax import lax
from jax.experimental import pallas as pl
from jax.experimental.pallas import tpu as pltpu
from jax.sharding import PartitionSpec as P

CAP = 2
BF = jnp.bfloat16
F32 = jnp.float32
VMEM_BYTES = 56 * 2**20


def swap(array, axis, bit):
    size = lax.axis_size(axis)
    return lax.ppermute(array, axis, [(i, i ^ bit) for i in range(size)])


def params():
    return pltpu.CompilerParams(vmem_limit_bytes=VMEM_BYTES)


PARTS, BLOCKS = 0, 4


def forward_kernel(first, blocks, bs, meta, x_ref, w_ref, delta_ref, d_ref, act_ref, slope_ref, acc):
    width = acc.shape[1]
    total = None
    for s in range(w_ref.shape[0]):
        term = jnp.dot(x_ref[meta[PARTS + s]], w_ref[s], preferred_element_type=F32)
        total = term if total is None else total + term
    acc[...] = total
    start = first + pl.program_id(0) * width
    for n in range(blocks):
        at = BLOCKS + 4 * n
        col = meta[at + 3] - start

        @pl.when((col >= 0) & (col < width))
        def _():
            cols = pl.ds(pl.multiple_of(col, bs), bs)
            rows = pl.ds(pl.multiple_of(meta[at + 2], bs), bs)
            xs = x_ref[meta[at], :, rows]
            acc[:, cols] += jnp.dot(xs, delta_ref[n], preferred_element_type=F32)

    preact = acc[...]
    squash = jax.nn.sigmoid(preact)
    act_ref[0] = (preact * squash).astype(BF)
    slope_ref[...] = (
        d_ref[...].astype(F32) * squash * (1.0 + preact * (1.0 - squash))
    ).astype(BF)


def forward(meta, x4, w4, delta, d_piece, first, groups_of):
    rows, width = d_piece.shape
    slots, feats = w4.shape[0], w4.shape[1]
    cuts = 2
    tile = rows // groups_of // cuts
    blocks, bs = delta.shape[0], delta.shape[1]
    wide = next(c for c in (512, 384, 256, 128, width) if width % c == 0)
    return pl.pallas_call(
        functools.partial(forward_kernel, first, blocks, bs),
        grid_spec=pltpu.PrefetchScalarGridSpec(
            num_scalar_prefetch=1,
            grid=(width // wide, groups_of * cuts),
            in_specs=[
                pl.BlockSpec((slots, tile, feats), lambda j, i, m: (0, i, 0)),
                pl.BlockSpec((slots, feats, wide), lambda j, i, m: (0, 0, j)),
                pl.BlockSpec(delta.shape, lambda j, i, m: (0, 0, 0)),
                pl.BlockSpec((tile, wide), lambda j, i, m: (i, j)),
            ],
            out_specs=[
                pl.BlockSpec((1, tile, wide), lambda j, i, m: (i // cuts, i % cuts, j)),
                pl.BlockSpec((tile, wide), lambda j, i, m: (i, j)),
            ],
            scratch_shapes=[pltpu.VMEM((tile, wide), F32)],
        ),
        out_shape=[
            jax.ShapeDtypeStruct((groups_of, rows // groups_of, width), BF),
            jax.ShapeDtypeStruct((rows, width), BF),
        ],
        compiler_params=params(),
        cost_estimate=pl.CostEstimate(
            flops=2 * rows * feats * slots * width,
            bytes_accessed=2 * (rows + width) * feats * slots,
            transcendentals=0,
        ),
    )(meta, x4, w4, delta, d_piece)


def backward_kernel(firsts, blocks, bs, has_acc, bit, meta, *refs):
    n = len(firsts)
    slopes, w_refs = refs[:n], refs[n : 2 * n]
    delta_ref = refs[2 * n]
    acc_in = refs[2 * n + 1] if has_acc else None
    outs, acc = refs[2 * n + 1 + has_acc : -1], refs[-1]
    size = acc.shape[1]
    slot = pl.program_id(0) if bit is None else meta[PARTS + bit]
    base = pl.program_id(1) * size
    total = acc_in[0] if has_acc else None
    for p in range(n):
        term = lax.dot_general(
            slopes[p][...], w_refs[p][0], (((1,), (1,)), ((), ())), preferred_element_type=F32
        )
        total = term if total is None else total + term
    acc[...] = total
    for b in range(blocks):
        at = BLOCKS + 4 * b
        row = meta[at + 2] - base
        for p in range(n):
            col = meta[at + 3] - firsts[p]
            inside = (row >= 0) & (row < size) & (col >= 0) & (col < slopes[p].shape[1])

            @pl.when(inside & (meta[at + 1] == slot))
            def _():
                ds = slopes[p][:, pl.ds(pl.multiple_of(col, bs), bs)]
                acc[:, pl.ds(pl.multiple_of(row, bs), bs)] += lax.dot_general(
                    ds, delta_ref[b], (((1,), (1,)), ((), ())), preferred_element_type=F32
                )

    if len(outs) == 1:
        outs[0][0] = acc[...]
    else:
        cut = outs[0].shape[0]
        outs[0][...] = acc[:cut].astype(outs[0].dtype)
        outs[1][...] = acc[cut:].astype(outs[1].dtype)


def backward(meta, slopes, ws, delta, firsts, acc, bit, out_type):
    rows = slopes[0].shape[0]
    slots, feats = ws[0].shape[0], ws[0].shape[1]
    blocks, bs = delta.shape[0], delta.shape[1]
    every = bit is None
    tiles = 4 if every else 2
    size = feats // tiles
    width = sum(s.shape[1] for s in slopes)
    steps = slots if every else 1

    def slot_of(step, meta):
        return step if every else meta[PARTS + bit]

    whole = pl.BlockSpec((1, rows, size), lambda s, i, m: (slot_of(s, m), 0, i))
    half = pl.BlockSpec((rows // 2, size), lambda s, i, m: (0, i))
    if every:
        out_specs = [whole]
        out_shape = [jax.ShapeDtypeStruct((slots, rows, feats), F32)]
    else:
        out_specs = [half, half]
        out_shape = [jax.ShapeDtypeStruct((rows // 2, feats), out_type)] * 2
    return pl.pallas_call(
        functools.partial(backward_kernel, firsts, blocks, bs, acc is not None, bit),
        grid_spec=pltpu.PrefetchScalarGridSpec(
            num_scalar_prefetch=1,
            grid=(steps, tiles),
            in_specs=[
                pl.BlockSpec(s.shape, lambda s, i, m: (0, 0), pipeline_mode=pl.Buffered(1))
                for s in slopes
            ]
            + [
                pl.BlockSpec((1, size, w.shape[2]), lambda s, i, m: (slot_of(s, m), i, 0))
                for w in ws
            ]
            + [pl.BlockSpec(delta.shape, lambda s, i, m: (0, 0, 0))]
            + ([] if acc is None else [whole]),
            out_specs=out_specs,
            scratch_shapes=[pltpu.VMEM((rows, size), F32)],
        ),
        out_shape=out_shape,
        compiler_params=params(),
        cost_estimate=pl.CostEstimate(
            flops=2 * rows * feats * width * steps if every else 1,
            bytes_accessed=2 * (rows + feats) * width * steps if every else 1,
            transcendentals=0,
        ),
    )(meta, *slopes, *ws, delta, *([] if acc is None else [acc]))


def grads_kernel(firsts, sizes, meta, x_ref, *refs):
    slopes, (own_ref, peer_ref) = refs[:-2], refs[-2:]
    col = meta[BLOCKS + 4 * pl.program_id(0) + 3]
    own_ref[...] = jnp.zeros_like(own_ref)
    peer_ref[...] = jnp.zeros_like(peer_ref)
    rows = x_ref.shape[1] // 2
    for first, size, slope in zip(firsts, sizes, slopes):

        @pl.when((col >= first) & (col < first + size))
        def _():
            dims = (((0,), (0,)), ((), ()))
            own_ref[0] = lax.dot_general(
                x_ref[0, :rows], slope[:rows], dims, preferred_element_type=F32
            )
            peer_ref[0] = lax.dot_general(
                x_ref[0, rows:], slope[rows:], dims, preferred_element_type=F32
            ).astype(BF)


def block_sums(meta, x4, slopes, firsts, blocks, bs):
    rows = x4.shape[1]
    sizes = [s.shape[1] for s in slopes]

    def slope_spec(first, size):
        def index(n, m):
            return 0, jnp.clip((m[BLOCKS + 4 * n + 3] - first) // bs, 0, size // bs - 1)

        return pl.BlockSpec((rows, bs), index)

    out = pl.BlockSpec((1, bs, bs), lambda n, m: (n, 0, 0))
    return pl.pallas_call(
        functools.partial(grads_kernel, firsts, sizes),
        grid_spec=pltpu.PrefetchScalarGridSpec(
            num_scalar_prefetch=1,
            grid=(blocks,),
            in_specs=[
                pl.BlockSpec(
                    (1, rows, bs),
                    lambda n, m: (m[BLOCKS + 4 * n], 0, m[BLOCKS + 4 * n + 2] // bs),
                )
            ]
            + [slope_spec(f, z) for f, z in zip(firsts, sizes)],
            out_specs=[out, out],
        ),
        out_shape=[
            jax.ShapeDtypeStruct((blocks, bs, bs), F32),
            jax.ShapeDtypeStruct((blocks, bs, bs), BF),
        ],
        compiler_params=params(),
        cost_estimate=pl.CostEstimate(
            flops=1, bytes_accessed=1, transcendentals=0
        ),
    )(meta, x4, *slopes)


def slot_ranks(owners):
    owner_ids = owners[:, 0]
    order = jnp.arange(owner_ids.shape[0], dtype=jnp.int32)
    earlier = (owner_ids[None, :] == owner_ids[:, None]) & (order[None, :] < order[:, None])
    rank = jnp.sum(earlier.astype(jnp.int32), axis=1)
    return (owner_ids[None, :] == lax.axis_index("dp")) & (
        rank[None, :] == jnp.arange(CAP, dtype=jnp.int32)[:, None]
    )


def pick_slots(owners, total):
    wanted = slot_ranks(owners)
    return jnp.sum(jnp.where(wanted[:, :, None, None], total[None], 0.0), axis=1)[None]


def tie(value, *after):
    return lax.optimization_barrier((value,) + after)[0]


def piece_sizes(half, bs):
    last = max(half // bs // 5, 1) * bs
    return [half - last, last]


def local(tokens, frozen, delta, block_rows, block_cols, owners, d_out):
    group, me_dp, me_t = (lax.axis_index(a) for a in ("groups", "dp", "tensor"))
    n_dp, n_t = lax.axis_size("dp"), lax.axis_size("tensor")
    rows, feats = tokens.shape
    blocks, bs = delta.shape[0], delta.shape[1]
    slab = frozen.shape[1]
    half = slab // 2
    mine, theirs = group * half, (1 - group) * half
    sizes = piece_sizes(half, bs)
    firsts = [sum(sizes[:p]) for p in range(len(sizes))]

    shards = [
        lax.dynamic_slice(frozen, (0, mine + first), (frozen.shape[0], size))
        for first, size in zip(firsts, sizes)
    ]
    gather_a = lax.all_gather(shards[0], "dp")
    gather_b = lax.all_gather(tie(shards[1], gather_a), "dp")
    gathered = [gather_a, gather_b]

    row_part = block_rows * bs // feats
    block_info = jnp.stack(
        [
            row_part ^ me_t,
            row_part,
            block_rows * bs - row_part * feats,
            block_cols * bs - (me_t * slab + mine),
        ],
        axis=1,
    )
    meta = jnp.concatenate([jnp.arange(n_t, dtype=jnp.int32) ^ me_t, block_info.reshape(-1)])

    peer = swap(tokens, "groups", 1)
    own_x = swap(tokens, "tensor", 2)
    peer_x = swap(peer, "tensor", 2)
    near_x = jnp.concatenate([tokens, peer], axis=0)
    far_x = jnp.concatenate([own_x, peer_x], axis=0)
    x4 = jnp.stack([near_x, swap(near_x, "tensor", 1), far_x, swap(far_x, "tensor", 1)])

    order = peer_x
    d_pieces = []
    for first, size in zip(firsts, sizes):
        give = lax.dynamic_slice(d_out, (0, theirs + first), (rows, size))
        keep = lax.dynamic_slice(d_out, (0, mine + first), (rows, size))
        got = swap(tie(give, order), "groups", 1)
        order = got
        d_pieces.append(jnp.concatenate([keep, got], axis=0))

    act_a, slope_a = forward(meta, x4, gather_a, delta, d_pieces[0], firsts[0], 2)
    back_a = swap(act_a[1], "groups", 1)
    (early,) = backward(meta, [slope_a], [gather_a], delta, firsts[:1], None, None, None)
    activated = jnp.zeros((rows, slab), BF)
    activated = lax.dynamic_update_slice(activated, act_a[0], (0, mine + firsts[0]))
    activated = lax.dynamic_update_slice(activated, back_a, (0, theirs + firsts[0]))

    delta_b = tie(delta, early, activated)
    act_b, slope_b = forward(meta, x4, gather_b, delta_b, d_pieces[1], firsts[1], 2)
    back_b = swap(act_b[1], "groups", 1)
    slopes = [slope_a, slope_b]

    def back_of(bit, out_type, *wait):
        d = tie(delta_b, *wait) if wait else delta_b
        return backward(meta, [slope_b], [gather_b], d, firsts[1:], early, bit, out_type)

    far_own_give, far_peer_give = back_of(3, BF)
    far_peer_got = swap(far_peer_give, "tensor", 1)
    far_own_got = swap(far_own_give, "tensor", 1)
    own_sum, peer_sum = block_sums(
        meta, x4, [slope_a, tie(slope_b, far_peer_give)], firsts, blocks, bs
    )
    sums = own_sum + swap(peer_sum, "groups", 1).astype(F32)
    shares = [swap(sums.astype(BF), "dp", bit) for bit in range(1, n_dp)]
    activated = lax.dynamic_update_slice(activated, act_b[0], (0, mine + firsts[1]))
    activated = lax.dynamic_update_slice(activated, back_b, (0, theirs + firsts[1]))
    far_own, far_peer = back_of(2, F32, far_peer_give, peer_sum)
    far_peer = (far_peer + far_peer_got.astype(F32)).astype(BF)
    diagonal = [(i, i ^ (n_t + 2)) for i in range(2 * n_t)]
    from_xy = lax.ppermute(far_peer, ("groups", "tensor"), diagonal)
    far_own = (far_own + far_own_got.astype(F32)).astype(BF)
    from_x = swap(far_own, "tensor", 2)
    near_own_give, near_peer_give = back_of(1, BF, far_peer, far_own, sums)
    near_peer_got = swap(near_peer_give, "tensor", 1)
    near_own_got = swap(near_own_give, "tensor", 1)
    near_own, near_peer = back_of(0, F32, near_peer_give, activated, *shares)
    near_peer = (near_peer + near_peer_got.astype(F32)).astype(BF)
    from_y = swap(near_peer, "groups", 1)
    near_own = near_own + near_own_got.astype(F32)
    d_tokens = near_own + from_y.astype(F32) + from_x.astype(F32) + from_xy.astype(F32)
    for share in shares:
        sums = sums + share.astype(F32)
    norm = float(rows * n_dp) ** (-0.5)
    return (activated, d_tokens.astype(BF), pick_slots(owners, sums * norm))


def local_any(tokens, frozen, delta, block_rows, block_cols, owners, d_out):
    me_dp, me_t, n_dp = lax.axis_index("dp"), lax.axis_index("tensor"), lax.axis_size("dp")
    rows = tokens.shape[0]
    blocks, bs = delta.shape[0], delta.shape[1]
    slab = frozen.shape[1]
    x_full = lax.all_gather(tokens, "tensor", axis=1, tiled=True)
    weight = lax.all_gather(frozen, "dp", axis=0, tiled=True)
    width = x_full.shape[1]
    row_pick = (block_rows[:, None] == jnp.arange(width // bs)[None, :]).astype(F32)
    cols_here = block_cols - me_t * (slab // bs)
    col_pick = (cols_here[:, None] == jnp.arange(slab // bs)[None, :]).astype(F32)
    highest = lax.Precision.HIGHEST
    xb = jnp.take(x_full.reshape(rows, width // bs, bs), block_rows, axis=1)
    contrib = jnp.einsum("tnk,nkc->tnc", xb, delta, preferred_element_type=F32)
    add = jnp.einsum("tnc,nm->tmc", contrib, col_pick, precision=highest).reshape(rows, slab)
    preact = jnp.dot(x_full, weight, preferred_element_type=F32) + add
    squash = jax.nn.sigmoid(preact)
    activated = (preact * squash).astype(BF)
    d_pre = (d_out.astype(F32) * squash * (1.0 + preact * (1.0 - squash))).astype(BF)
    d_rows = lax.dot_general(
        d_pre, weight, (((1,), (1,)), ((), ())), preferred_element_type=F32
    )
    dy = jnp.take(d_pre.reshape(rows, slab // bs, bs), cols_here, axis=1)
    back = jnp.einsum("tnc,nkc->tnk", dy, delta, preferred_element_type=F32)
    back = jnp.einsum("tnk,nr->trk", back, row_pick, precision=highest).reshape(rows, width)
    d_tokens = lax.psum_scatter(
        (d_rows + back).astype(BF), "tensor", scatter_dimension=1, tiled=True
    )
    grads = jnp.einsum("tnk,tnc->nkc", xb, dy, preferred_element_type=F32)
    everyone = lax.all_gather(grads.astype(BF), "dp", axis=0).astype(F32)
    norm = float(rows * n_dp) ** (-0.5)
    return (activated, d_tokens, pick_slots(owners, jnp.sum(everyone, axis=0) * norm))


def solution(mesh):
    sizes = dict(mesh.shape)
    small = sizes["groups"] == 2 and sizes["dp"] == 4 and sizes["tensor"] == 4
    body = local if small else local_any
    in_specs = (
        P(("groups", "dp"), "tensor"),
        P("dp", "tensor"),
        P("tensor", None, None),
        P("tensor"),
        P("tensor"),
        P("tensor", None),
        P(("groups", "dp"), "tensor"),
    )
    out_specs = (
        P(("groups", "dp"), "tensor"),
        P(("groups", "dp"), "tensor"),
        P("tensor", ("groups", "dp"), None, None),
    )
    return jax.shard_map(body, mesh=mesh, in_specs=in_specs, out_specs=out_specs, check_vma=False)
```

```python
import functools

import jax
import jax.numpy as jnp
from jax import lax
from jax.experimental import pallas as pl
from jax.experimental.pallas import tpu as pltpu
from jax.sharding import PartitionSpec as P

CAP = 2
BF = jnp.bfloat16
F32 = jnp.float32
VMEM_BYTES = 56 * 2**20


def swap(array, axis, bit):
    size = lax.axis_size(axis)
    return lax.ppermute(array, axis, [(i, i ^ bit) for i in range(size)])


def params():
    return pltpu.CompilerParams(vmem_limit_bytes=VMEM_BYTES)


PARTS, BLOCKS = 0, 4


def forward_kernel(
    first, blocks, bs, cuts, meta, x_ref, w_ref, delta_ref, d_ref, act_ref, slope_ref, sum_ref, acc
):
    width = acc.shape[1]
    group = pl.program_id(1) // cuts

    @pl.when((pl.program_id(0) == 0) & (pl.program_id(1) == 0))
    def _():
        sum_ref[...] = jnp.zeros_like(sum_ref)

    total = None
    for s in range(w_ref.shape[0]):
        term = jnp.dot(x_ref[meta[PARTS + s]], w_ref[s], preferred_element_type=F32)
        total = term if total is None else total + term
    acc[...] = total
    start = first + pl.program_id(0) * width
    for n in range(blocks):
        at = BLOCKS + 4 * n
        col = meta[at + 3] - start

        @pl.when((col >= 0) & (col < width))
        def _():
            cols = pl.ds(pl.multiple_of(col, bs), bs)
            rows = pl.ds(pl.multiple_of(meta[at + 2], bs), bs)
            xs = x_ref[meta[at], :, rows]
            acc[:, cols] += jnp.dot(xs, delta_ref[n], preferred_element_type=F32)

    preact = acc[...]
    squash = jax.nn.sigmoid(preact)
    act_ref[0] = (preact * squash).astype(BF)
    slope_ref[...] = (
        d_ref[...].astype(F32) * squash * (1.0 + preact * (1.0 - squash))
    ).astype(BF)
    for n in range(blocks):
        at = BLOCKS + 4 * n
        col = meta[at + 3] - start

        @pl.when((col >= 0) & (col < width))
        def _():
            rows = pl.ds(pl.multiple_of(meta[at + 2], bs), bs)
            ds = slope_ref[:, pl.ds(pl.multiple_of(col, bs), bs)]
            sum_ref[group, n] += lax.dot_general(
                x_ref[meta[at], :, rows], ds, (((0,), (0,)), ((), ())), preferred_element_type=F32
            )


def forward(meta, x4, w4, delta, d_piece, first, groups_of):
    rows, width = d_piece.shape
    slots, feats = w4.shape[0], w4.shape[1]
    cuts = 2
    tile = rows // groups_of // cuts
    blocks, bs = delta.shape[0], delta.shape[1]
    wide = next(c for c in (512, 384, 256, 128, width) if width % c == 0)
    return pl.pallas_call(
        functools.partial(forward_kernel, first, blocks, bs, cuts),
        grid_spec=pltpu.PrefetchScalarGridSpec(
            num_scalar_prefetch=1,
            grid=(width // wide, groups_of * cuts),
            in_specs=[
                pl.BlockSpec((slots, tile, feats), lambda j, i, m: (0, i, 0)),
                pl.BlockSpec((slots, feats, wide), lambda j, i, m: (0, 0, j)),
                pl.BlockSpec(delta.shape, lambda j, i, m: (0, 0, 0)),
                pl.BlockSpec((tile, wide), lambda j, i, m: (i, j)),
            ],
            out_specs=[
                pl.BlockSpec((1, tile, wide), lambda j, i, m: (i // cuts, i % cuts, j)),
                pl.BlockSpec((tile, wide), lambda j, i, m: (i, j)),
                pl.BlockSpec((groups_of, blocks, bs, bs), lambda j, i, m: (0, 0, 0, 0)),
            ],
            scratch_shapes=[pltpu.VMEM((tile, wide), F32)],
        ),
        out_shape=[
            jax.ShapeDtypeStruct((groups_of, rows // groups_of, width), BF),
            jax.ShapeDtypeStruct((rows, width), BF),
            jax.ShapeDtypeStruct((groups_of, blocks, bs, bs), F32),
        ],
        compiler_params=params(),
        cost_estimate=pl.CostEstimate(
            flops=2 * rows * feats * slots * width,
            bytes_accessed=2 * (rows + width) * feats * slots,
            transcendentals=0,
        ),
    )(meta, x4, w4, delta, d_piece)


def backward_kernel(firsts, blocks, bs, has_acc, bit, meta, *refs):
    n = len(firsts)
    slopes, w_refs = refs[:n], refs[n : 2 * n]
    delta_ref = refs[2 * n]
    acc_in = refs[2 * n + 1] if has_acc else None
    outs, acc = refs[2 * n + 1 + has_acc : -1], refs[-1]
    size = acc.shape[1]
    step = pl.program_id(0)
    slot = step if bit is None else meta[PARTS + bit - step]
    base = pl.program_id(1) * size
    total = acc_in[0] if has_acc else None
    for p in range(n):
        term = lax.dot_general(
            slopes[p][...], w_refs[p][0], (((1,), (1,)), ((), ())), preferred_element_type=F32
        )
        total = term if total is None else total + term
    acc[...] = total
    for b in range(blocks):
        at = BLOCKS + 4 * b
        row = meta[at + 2] - base
        for p in range(n):
            col = meta[at + 3] - firsts[p]
            inside = (row >= 0) & (row < size) & (col >= 0) & (col < slopes[p].shape[1])

            @pl.when(inside & (meta[at + 1] == slot))
            def _():
                ds = slopes[p][:, pl.ds(pl.multiple_of(col, bs), bs)]
                acc[:, pl.ds(pl.multiple_of(row, bs), bs)] += lax.dot_general(
                    ds, delta_ref[b], (((1,), (1,)), ((), ())), preferred_element_type=F32
                )

    if len(outs) == 1:
        outs[0][0] = acc[...]
        return
    cut = outs[0].shape[0]
    for at_step in range(2):

        @pl.when(step == at_step)
        def _():
            outs[2 * at_step][...] = acc[:cut].astype(BF)
            outs[2 * at_step + 1][...] = acc[cut:].astype(BF)


def backward(meta, slopes, ws, delta, firsts, acc, bit):
    rows = slopes[0].shape[0]
    slots, feats = ws[0].shape[0], ws[0].shape[1]
    blocks, bs = delta.shape[0], delta.shape[1]
    every = bit is None
    tiles = 4 if every else 2
    size = feats // tiles
    width = sum(s.shape[1] for s in slopes)
    steps = slots if every else 2

    def slot_of(step, meta):
        return step if every else meta[PARTS + bit - step]

    whole = pl.BlockSpec((1, rows, size), lambda s, i, m: (slot_of(s, m), 0, i))
    give = pl.BlockSpec((rows // 2, size), lambda s, i, m: (0, jnp.where(s == 0, i, tiles - 1)))
    keep = pl.BlockSpec((rows // 2, size), lambda s, i, m: (0, jnp.where(s == 0, 0, i)))
    if every:
        out_specs = [whole]
        out_shape = [jax.ShapeDtypeStruct((slots, rows, feats), F32)]
    else:
        out_specs = [give, give, keep, keep]
        out_shape = [jax.ShapeDtypeStruct((rows // 2, feats), BF)] * 4
    return pl.pallas_call(
        functools.partial(backward_kernel, firsts, blocks, bs, acc is not None, bit),
        grid_spec=pltpu.PrefetchScalarGridSpec(
            num_scalar_prefetch=1,
            grid=(steps, tiles),
            in_specs=[
                pl.BlockSpec(s.shape, lambda s, i, m: (0, 0), pipeline_mode=pl.Buffered(1))
                for s in slopes
            ]
            + [
                pl.BlockSpec((1, size, w.shape[2]), lambda s, i, m: (slot_of(s, m), i, 0))
                for w in ws
            ]
            + [pl.BlockSpec(delta.shape, lambda s, i, m: (0, 0, 0))]
            + ([] if acc is None else [whole]),
            out_specs=out_specs,
            scratch_shapes=[pltpu.VMEM((rows, size), F32)],
        ),
        out_shape=out_shape,
        compiler_params=params(),
        cost_estimate=pl.CostEstimate(
            flops=2 * rows * feats * width * steps if every else 1,
            bytes_accessed=2 * (rows + feats) * width * steps if every else 1,
            transcendentals=0,
        ),
    )(meta, *slopes, *ws, delta, *([] if acc is None else [acc]))


def slot_ranks(owners):
    owner_ids = owners[:, 0]
    order = jnp.arange(owner_ids.shape[0], dtype=jnp.int32)
    earlier = (owner_ids[None, :] == owner_ids[:, None]) & (order[None, :] < order[:, None])
    rank = jnp.sum(earlier.astype(jnp.int32), axis=1)
    return (owner_ids[None, :] == lax.axis_index("dp")) & (
        rank[None, :] == jnp.arange(CAP, dtype=jnp.int32)[:, None]
    )


def pick_slots(owners, total):
    wanted = slot_ranks(owners)
    return jnp.sum(jnp.where(wanted[:, :, None, None], total[None], 0.0), axis=1)[None]


def tie(value, *after):
    return lax.optimization_barrier((value,) + after)[0]


def piece_sizes(half, bs):
    last = max(half // bs // 5, 1) * bs
    return [half - last, last]


def local(tokens, frozen, delta, block_rows, block_cols, owners, d_out):
    group, me_dp, me_t = (lax.axis_index(a) for a in ("groups", "dp", "tensor"))
    n_dp, n_t = lax.axis_size("dp"), lax.axis_size("tensor")
    rows, feats = tokens.shape
    blocks, bs = delta.shape[0], delta.shape[1]
    slab = frozen.shape[1]
    half = slab // 2
    mine, theirs = group * half, (1 - group) * half
    sizes = piece_sizes(half, bs)
    firsts = [sum(sizes[:p]) for p in range(len(sizes))]

    shards = [
        lax.dynamic_slice(frozen, (0, mine + first), (frozen.shape[0], size))
        for first, size in zip(firsts, sizes)
    ]
    gather_a = lax.all_gather(shards[0], "dp")
    gather_b = lax.all_gather(tie(shards[1], gather_a), "dp")
    gathered = [gather_a, gather_b]

    row_part = block_rows * bs // feats
    block_info = jnp.stack(
        [
            row_part ^ me_t,
            row_part,
            block_rows * bs - row_part * feats,
            block_cols * bs - (me_t * slab + mine),
        ],
        axis=1,
    )
    meta = jnp.concatenate([jnp.arange(n_t, dtype=jnp.int32) ^ me_t, block_info.reshape(-1)])

    peer = swap(tokens, "groups", 1)
    own_x = swap(tokens, "tensor", 2)
    peer_x = swap(peer, "tensor", 2)
    near_x = jnp.concatenate([tokens, peer], axis=0)
    far_x = jnp.concatenate([own_x, peer_x], axis=0)
    x4 = jnp.stack([near_x, swap(near_x, "tensor", 1), far_x, swap(far_x, "tensor", 1)])

    order = peer_x
    d_pieces = []
    for first, size in zip(firsts, sizes):
        give = lax.dynamic_slice(d_out, (0, theirs + first), (rows, size))
        keep = lax.dynamic_slice(d_out, (0, mine + first), (rows, size))
        got = swap(tie(give, order), "groups", 1)
        order = got
        d_pieces.append(jnp.concatenate([keep, got], axis=0))

    act_a, slope_a, sums_a = forward(meta, x4, gather_a, delta, d_pieces[0], firsts[0], 2)
    back_a = swap(act_a[1], "groups", 1)
    (early,) = backward(meta, [slope_a], [gather_a], delta, firsts[:1], None, None)
    activated = jnp.zeros((rows, slab), BF)
    activated = lax.dynamic_update_slice(activated, act_a[0], (0, mine + firsts[0]))
    activated = lax.dynamic_update_slice(activated, back_a, (0, theirs + firsts[0]))

    delta_b = tie(delta, early)
    act_b, slope_b, sums_b = forward(meta, x4, gather_b, delta_b, d_pieces[1], firsts[1], 2)
    back_b = swap(act_b[1], "groups", 1)
    activated = lax.dynamic_update_slice(activated, act_b[0], (0, mine + firsts[1]))
    activated = lax.dynamic_update_slice(activated, back_b, (0, theirs + firsts[1]))

    def back_of(bit, *wait):
        d = tie(delta_b, *wait) if wait else delta_b
        return backward(meta, [slope_b], [gather_b], d, firsts[1:], early, bit)

    sums = sums_a + sums_b
    sums = sums[0] + swap(sums[1].astype(BF), "groups", 1).astype(F32)
    shares = [swap(sums.astype(BF), "dp", bit) for bit in range(1, n_dp)]
    far_own_give, far_peer_give, far_own, far_peer = back_of(3)
    far_peer_got = swap(far_peer_give, "tensor", 1)
    far_own_got = swap(far_own_give, "tensor", 1)
    near_own_give, near_peer_give, near_own, near_peer = back_of(1, far_peer, sums)
    near_peer_got = swap(near_peer_give, "tensor", 1)
    near_own_got = swap(near_own_give, "tensor", 1)
    far_peer, far_own = tie(far_peer, near_peer, back_b, *shares), tie(far_own, near_peer)
    far_peer = (far_peer.astype(F32) + far_peer_got.astype(F32)).astype(BF)
    diagonal = [(i, i ^ (n_t + 2)) for i in range(2 * n_t)]
    from_xy = lax.ppermute(far_peer, ("groups", "tensor"), diagonal)
    far_own = (far_own.astype(F32) + far_own_got.astype(F32)).astype(BF)
    from_x = swap(far_own, "tensor", 2)
    near_peer = (near_peer.astype(F32) + near_peer_got.astype(F32)).astype(BF)
    from_y = swap(near_peer, "groups", 1)
    near_own = near_own.astype(F32) + near_own_got.astype(F32)
    d_tokens = near_own + from_y.astype(F32) + from_x.astype(F32) + from_xy.astype(F32)
    for share in shares:
        sums = sums + share.astype(F32)
    norm = float(rows * n_dp) ** (-0.5)
    return (activated, d_tokens.astype(BF), pick_slots(owners, sums * norm))


def local_any(tokens, frozen, delta, block_rows, block_cols, owners, d_out):
    me_dp, me_t, n_dp = lax.axis_index("dp"), lax.axis_index("tensor"), lax.axis_size("dp")
    rows = tokens.shape[0]
    blocks, bs = delta.shape[0], delta.shape[1]
    slab = frozen.shape[1]
    x_full = lax.all_gather(tokens, "tensor", axis=1, tiled=True)
    weight = lax.all_gather(frozen, "dp", axis=0, tiled=True)
    width = x_full.shape[1]
    row_pick = (block_rows[:, None] == jnp.arange(width // bs)[None, :]).astype(F32)
    cols_here = block_cols - me_t * (slab // bs)
    col_pick = (cols_here[:, None] == jnp.arange(slab // bs)[None, :]).astype(F32)
    highest = lax.Precision.HIGHEST
    xb = jnp.take(x_full.reshape(rows, width // bs, bs), block_rows, axis=1)
    contrib = jnp.einsum("tnk,nkc->tnc", xb, delta, preferred_element_type=F32)
    add = jnp.einsum("tnc,nm->tmc", contrib, col_pick, precision=highest).reshape(rows, slab)
    preact = jnp.dot(x_full, weight, preferred_element_type=F32) + add
    squash = jax.nn.sigmoid(preact)
    activated = (preact * squash).astype(BF)
    d_pre = (d_out.astype(F32) * squash * (1.0 + preact * (1.0 - squash))).astype(BF)
    d_rows = lax.dot_general(
        d_pre, weight, (((1,), (1,)), ((), ())), preferred_element_type=F32
    )
    dy = jnp.take(d_pre.reshape(rows, slab // bs, bs), cols_here, axis=1)
    back = jnp.einsum("tnc,nkc->tnk", dy, delta, preferred_element_type=F32)
    back = jnp.einsum("tnk,nr->trk", back, row_pick, precision=highest).reshape(rows, width)
    d_tokens = lax.psum_scatter(
        (d_rows + back).astype(BF), "tensor", scatter_dimension=1, tiled=True
    )
    grads = jnp.einsum("tnk,tnc->nkc", xb, dy, preferred_element_type=F32)
    everyone = lax.all_gather(grads.astype(BF), "dp", axis=0).astype(F32)
    norm = float(rows * n_dp) ** (-0.5)
    return (activated, d_tokens, pick_slots(owners, jnp.sum(everyone, axis=0) * norm))


def solution(mesh):
    sizes = dict(mesh.shape)
    small = sizes["groups"] == 2 and sizes["dp"] == 4 and sizes["tensor"] == 4
    body = local if small else local_any
    in_specs = (
        P(("groups", "dp"), "tensor"),
        P("dp", "tensor"),
        P("tensor", None, None),
        P("tensor"),
        P("tensor"),
        P("tensor", None),
        P(("groups", "dp"), "tensor"),
    )
    out_specs = (
        P(("groups", "dp"), "tensor"),
        P(("groups", "dp"), "tensor"),
        P("tensor", ("groups", "dp"), None, None),
    )
    return jax.shard_map(body, mesh=mesh, in_specs=in_specs, out_specs=out_specs, check_vma=False)
```

```python
import functools

import jax
import jax.numpy as jnp
from jax import lax
from jax.experimental import pallas as pl
from jax.experimental.pallas import tpu as pltpu
from jax.sharding import PartitionSpec as P

CAP = 2
BF = jnp.bfloat16
F32 = jnp.float32
VMEM_BYTES = 56 * 2**20


def swap(array, axis, bit):
    size = lax.axis_size(axis)
    return lax.ppermute(array, axis, [(i, i ^ bit) for i in range(size)])


def params():
    return pltpu.CompilerParams(vmem_limit_bytes=VMEM_BYTES)


PARTS, BLOCKS = 0, 4


def forward_kernel(
    first, blocks, bs, cuts, meta, x_ref, w_ref, delta_ref, d_ref, act_ref, slope_ref, sum_ref, acc
):
    width = acc.shape[1]
    group = pl.program_id(1) // cuts

    @pl.when((pl.program_id(0) == 0) & (pl.program_id(1) == 0))
    def _():
        sum_ref[...] = jnp.zeros_like(sum_ref)

    total = None
    for s in range(w_ref.shape[0]):
        term = jnp.dot(x_ref[meta[PARTS + s]], w_ref[s], preferred_element_type=F32)
        total = term if total is None else total + term
    acc[...] = total
    start = first + pl.program_id(0) * width
    for n in range(blocks):
        at = BLOCKS + 4 * n
        col = meta[at + 3] - start

        @pl.when((col >= 0) & (col < width))
        def _():
            cols = pl.ds(pl.multiple_of(col, bs), bs)
            rows = pl.ds(pl.multiple_of(meta[at + 2], bs), bs)
            xs = x_ref[meta[at], :, rows]
            acc[:, cols] += jnp.dot(xs, delta_ref[n], preferred_element_type=F32)

    preact = acc[...]
    squash = jax.nn.sigmoid(preact)
    act_ref[0] = (preact * squash).astype(BF)
    slope_ref[...] = (
        d_ref[...].astype(F32) * squash * (1.0 + preact * (1.0 - squash))
    ).astype(BF)
    for n in range(blocks):
        at = BLOCKS + 4 * n
        col = meta[at + 3] - start

        @pl.when((col >= 0) & (col < width))
        def _():
            rows = pl.ds(pl.multiple_of(meta[at + 2], bs), bs)
            ds = slope_ref[:, pl.ds(pl.multiple_of(col, bs), bs)]
            sum_ref[group, n] += lax.dot_general(
                x_ref[meta[at], :, rows], ds, (((0,), (0,)), ((), ())), preferred_element_type=F32
            )


def forward(meta, x4, w4, delta, d_piece, first, groups_of):
    rows, width = d_piece.shape
    slots, feats = w4.shape[0], w4.shape[1]
    cuts = 2
    tile = rows // groups_of // cuts
    blocks, bs = delta.shape[0], delta.shape[1]
    wide = next(c for c in (512, 384, 256, 128, width) if width % c == 0)
    return pl.pallas_call(
        functools.partial(forward_kernel, first, blocks, bs, cuts),
        grid_spec=pltpu.PrefetchScalarGridSpec(
            num_scalar_prefetch=1,
            grid=(width // wide, groups_of * cuts),
            in_specs=[
                pl.BlockSpec((slots, tile, feats), lambda j, i, m: (0, i, 0)),
                pl.BlockSpec((slots, feats, wide), lambda j, i, m: (0, 0, j)),
                pl.BlockSpec(delta.shape, lambda j, i, m: (0, 0, 0)),
                pl.BlockSpec((tile, wide), lambda j, i, m: (i, j)),
            ],
            out_specs=[
                pl.BlockSpec((1, tile, wide), lambda j, i, m: (i // cuts, i % cuts, j)),
                pl.BlockSpec((tile, wide), lambda j, i, m: (i, j)),
                pl.BlockSpec((groups_of, blocks, bs, bs), lambda j, i, m: (0, 0, 0, 0)),
            ],
            scratch_shapes=[pltpu.VMEM((tile, wide), F32)],
        ),
        out_shape=[
            jax.ShapeDtypeStruct((groups_of, rows // groups_of, width), BF),
            jax.ShapeDtypeStruct((rows, width), BF),
            jax.ShapeDtypeStruct((groups_of, blocks, bs, bs), F32),
        ],
        compiler_params=params(),
        cost_estimate=pl.CostEstimate(
            flops=2 * rows * feats * slots * width,
            bytes_accessed=2 * (rows + width) * feats * slots,
            transcendentals=0,
        ),
    )(meta, x4, w4, delta, d_piece)


def backward_kernel(firsts, blocks, bs, has_acc, bit, meta, *refs):
    n = len(firsts)
    slopes, w_refs = refs[:n], refs[n : 2 * n]
    delta_ref = refs[2 * n]
    acc_in = refs[2 * n + 1] if has_acc else None
    outs, acc = refs[2 * n + 1 + has_acc : -1], refs[-1]
    size = acc.shape[1]
    step = pl.program_id(0)
    slot = step if bit is None else meta[PARTS + bit - step]
    base = pl.program_id(1) * size
    total = acc_in[0] if has_acc else None
    for p in range(n):
        term = lax.dot_general(
            slopes[p][...], w_refs[p][0], (((1,), (1,)), ((), ())), preferred_element_type=F32
        )
        total = term if total is None else total + term
    acc[...] = total
    for b in range(blocks):
        at = BLOCKS + 4 * b
        row = meta[at + 2] - base
        for p in range(n):
            col = meta[at + 3] - firsts[p]
            inside = (row >= 0) & (row < size) & (col >= 0) & (col < slopes[p].shape[1])

            @pl.when(inside & (meta[at + 1] == slot))
            def _():
                ds = slopes[p][:, pl.ds(pl.multiple_of(col, bs), bs)]
                acc[:, pl.ds(pl.multiple_of(row, bs), bs)] += lax.dot_general(
                    ds, delta_ref[b], (((1,), (1,)), ((), ())), preferred_element_type=F32
                )

    if len(outs) == 1:
        outs[0][0] = acc[...]
        return
    cut = outs[0].shape[0]
    for at_step in range(2):

        @pl.when(step == at_step)
        def _():
            outs[2 * at_step][...] = acc[:cut].astype(BF)
            outs[2 * at_step + 1][...] = acc[cut:].astype(BF)


def backward(meta, slopes, ws, delta, firsts, acc, bit):
    rows = slopes[0].shape[0]
    slots, feats = ws[0].shape[0], ws[0].shape[1]
    blocks, bs = delta.shape[0], delta.shape[1]
    every = bit is None
    tiles = 4 if every else 2
    size = feats // tiles
    width = sum(s.shape[1] for s in slopes)
    steps = slots if every else 2

    def slot_of(step, meta):
        return step if every else meta[PARTS + bit - step]

    whole = pl.BlockSpec((1, rows, size), lambda s, i, m: (slot_of(s, m), 0, i))
    give = pl.BlockSpec((rows // 2, size), lambda s, i, m: (0, jnp.where(s == 0, i, tiles - 1)))
    keep = pl.BlockSpec((rows // 2, size), lambda s, i, m: (0, jnp.where(s == 0, 0, i)))
    if every:
        out_specs = [whole]
        out_shape = [jax.ShapeDtypeStruct((slots, rows, feats), F32)]
    else:
        out_specs = [give, give, keep, keep]
        out_shape = [jax.ShapeDtypeStruct((rows // 2, feats), BF)] * 4
    return pl.pallas_call(
        functools.partial(backward_kernel, firsts, blocks, bs, acc is not None, bit),
        grid_spec=pltpu.PrefetchScalarGridSpec(
            num_scalar_prefetch=1,
            grid=(steps, tiles),
            in_specs=[
                pl.BlockSpec(s.shape, lambda s, i, m: (0, 0), pipeline_mode=pl.Buffered(1))
                for s in slopes
            ]
            + [
                pl.BlockSpec((1, size, w.shape[2]), lambda s, i, m: (slot_of(s, m), i, 0))
                for w in ws
            ]
            + [pl.BlockSpec(delta.shape, lambda s, i, m: (0, 0, 0))]
            + ([] if acc is None else [whole]),
            out_specs=out_specs,
            scratch_shapes=[pltpu.VMEM((rows, size), F32)],
        ),
        out_shape=out_shape,
        compiler_params=params(),
        cost_estimate=pl.CostEstimate(
            flops=2 * rows * feats * width * steps if every else 1,
            bytes_accessed=2 * (rows + feats) * width * steps if every else 1,
            transcendentals=0,
        ),
    )(meta, *slopes, *ws, delta, *([] if acc is None else [acc]))


def slot_ranks(owners):
    owner_ids = owners[:, 0]
    order = jnp.arange(owner_ids.shape[0], dtype=jnp.int32)
    earlier = (owner_ids[None, :] == owner_ids[:, None]) & (order[None, :] < order[:, None])
    rank = jnp.sum(earlier.astype(jnp.int32), axis=1)
    return (owner_ids[None, :] == lax.axis_index("dp")) & (
        rank[None, :] == jnp.arange(CAP, dtype=jnp.int32)[:, None]
    )


def pick_slots(owners, total):
    wanted = slot_ranks(owners)
    return jnp.sum(jnp.where(wanted[:, :, None, None], total[None], 0.0), axis=1)[None]


def tie(value, *after):
    return lax.optimization_barrier((value,) + after)[0]


def piece_sizes(half, bs):
    last = max(half // bs // 5, 1) * bs
    return [half - last, last]


def local(tokens, frozen, delta, block_rows, block_cols, owners, d_out):
    group, me_dp, me_t = (lax.axis_index(a) for a in ("groups", "dp", "tensor"))
    n_dp, n_t = lax.axis_size("dp"), lax.axis_size("tensor")
    rows, feats = tokens.shape
    blocks, bs = delta.shape[0], delta.shape[1]
    slab = frozen.shape[1]
    half = slab // 2
    mine, theirs = group * half, (1 - group) * half
    sizes = piece_sizes(half, bs)
    firsts = [sum(sizes[:p]) for p in range(len(sizes))]

    shards = [
        lax.dynamic_slice(frozen, (0, mine + first), (frozen.shape[0], size))
        for first, size in zip(firsts, sizes)
    ]
    gather_a = lax.all_gather(shards[0], "dp")

    row_part = block_rows * bs // feats
    block_info = jnp.stack(
        [
            row_part ^ me_t,
            row_part,
            block_rows * bs - row_part * feats,
            block_cols * bs - (me_t * slab + mine),
        ],
        axis=1,
    )
    meta = jnp.concatenate([jnp.arange(n_t, dtype=jnp.int32) ^ me_t, block_info.reshape(-1)])

    peer = swap(tokens, "groups", 1)
    own_x = swap(tokens, "tensor", 2)
    peer_x = swap(peer, "tensor", 2)
    near_x = jnp.concatenate([tokens, peer], axis=0)
    far_x = jnp.concatenate([own_x, peer_x], axis=0)
    x4 = jnp.stack([near_x, swap(near_x, "tensor", 1), far_x, swap(far_x, "tensor", 1)])

    order = peer_x
    d_pieces = []
    for first, size in zip(firsts, sizes):
        give = lax.dynamic_slice(d_out, (0, theirs + first), (rows, size))
        keep = lax.dynamic_slice(d_out, (0, mine + first), (rows, size))
        got = swap(tie(give, order), "groups", 1)
        order = got
        d_pieces.append(jnp.concatenate([keep, got], axis=0))

    gather_b = lax.all_gather(tie(shards[1], gather_a, x4, *d_pieces), "dp")
    act_a, slope_a, sums_a = forward(meta, x4, gather_a, delta, d_pieces[0], firsts[0], 2)
    back_a = swap(act_a[1], "groups", 1)
    (early,) = backward(meta, [slope_a], [gather_a], delta, firsts[:1], None, None)
    activated = jnp.zeros((rows, slab), BF)
    activated = lax.dynamic_update_slice(activated, act_a[0], (0, mine + firsts[0]))
    activated = lax.dynamic_update_slice(activated, back_a, (0, theirs + firsts[0]))

    delta_b = tie(delta, early, activated)
    act_b, slope_b, sums_b = forward(meta, x4, gather_b, delta_b, d_pieces[1], firsts[1], 2)
    back_b = swap(act_b[1], "groups", 1)
    activated = lax.dynamic_update_slice(activated, act_b[0], (0, mine + firsts[1]))
    activated = lax.dynamic_update_slice(activated, back_b, (0, theirs + firsts[1]))

    def back_of(bit, *wait):
        d = tie(delta_b, *wait) if wait else delta_b
        return backward(meta, [slope_b], [gather_b], d, firsts[1:], early, bit)

    sums = sums_a + sums_b
    sums = sums[0] + swap(sums[1].astype(BF), "groups", 1).astype(F32)
    shares = [swap(sums.astype(BF), "dp", bit) for bit in range(1, n_dp)]
    far_own_give, far_peer_give, far_own, far_peer = back_of(3)
    far_peer_got = swap(far_peer_give, "tensor", 1)
    far_own_got = swap(far_own_give, "tensor", 1)
    near_own_give, near_peer_give, near_own, near_peer = back_of(1, far_peer, sums)
    near_peer_got = swap(near_peer_give, "tensor", 1)
    near_own_got = swap(near_own_give, "tensor", 1)
    far_peer, far_own = tie(far_peer, near_peer, back_b, *shares), tie(far_own, near_peer)
    far_peer = (far_peer.astype(F32) + far_peer_got.astype(F32)).astype(BF)
    diagonal = [(i, i ^ (n_t + 2)) for i in range(2 * n_t)]
    from_xy = lax.ppermute(far_peer, ("groups", "tensor"), diagonal)
    far_own = (far_own.astype(F32) + far_own_got.astype(F32)).astype(BF)
    from_x = swap(far_own, "tensor", 2)
    near_peer = (near_peer.astype(F32) + near_peer_got.astype(F32)).astype(BF)
    from_y = swap(near_peer, "groups", 1)
    near_own = near_own.astype(F32) + near_own_got.astype(F32)
    d_tokens = near_own + from_y.astype(F32) + from_x.astype(F32) + from_xy.astype(F32)
    for share in shares:
        sums = sums + share.astype(F32)
    norm = float(rows * n_dp) ** (-0.5)
    return (activated, d_tokens.astype(BF), pick_slots(owners, sums * norm))


def local_any(tokens, frozen, delta, block_rows, block_cols, owners, d_out):
    me_dp, me_t, n_dp = lax.axis_index("dp"), lax.axis_index("tensor"), lax.axis_size("dp")
    rows = tokens.shape[0]
    blocks, bs = delta.shape[0], delta.shape[1]
    slab = frozen.shape[1]
    x_full = lax.all_gather(tokens, "tensor", axis=1, tiled=True)
    weight = lax.all_gather(frozen, "dp", axis=0, tiled=True)
    width = x_full.shape[1]
    row_pick = (block_rows[:, None] == jnp.arange(width // bs)[None, :]).astype(F32)
    cols_here = block_cols - me_t * (slab // bs)
    col_pick = (cols_here[:, None] == jnp.arange(slab // bs)[None, :]).astype(F32)
    highest = lax.Precision.HIGHEST
    xb = jnp.take(x_full.reshape(rows, width // bs, bs), block_rows, axis=1)
    contrib = jnp.einsum("tnk,nkc->tnc", xb, delta, preferred_element_type=F32)
    add = jnp.einsum("tnc,nm->tmc", contrib, col_pick, precision=highest).reshape(rows, slab)
    preact = jnp.dot(x_full, weight, preferred_element_type=F32) + add
    squash = jax.nn.sigmoid(preact)
    activated = (preact * squash).astype(BF)
    d_pre = (d_out.astype(F32) * squash * (1.0 + preact * (1.0 - squash))).astype(BF)
    d_rows = lax.dot_general(
        d_pre, weight, (((1,), (1,)), ((), ())), preferred_element_type=F32
    )
    dy = jnp.take(d_pre.reshape(rows, slab // bs, bs), cols_here, axis=1)
    back = jnp.einsum("tnc,nkc->tnk", dy, delta, preferred_element_type=F32)
    back = jnp.einsum("tnk,nr->trk", back, row_pick, precision=highest).reshape(rows, width)
    d_tokens = lax.psum_scatter(
        (d_rows + back).astype(BF), "tensor", scatter_dimension=1, tiled=True
    )
    grads = jnp.einsum("tnk,tnc->nkc", xb, dy, preferred_element_type=F32)
    everyone = lax.all_gather(grads.astype(BF), "dp", axis=0).astype(F32)
    norm = float(rows * n_dp) ** (-0.5)
    return (activated, d_tokens, pick_slots(owners, jnp.sum(everyone, axis=0) * norm))


def solution(mesh):
    sizes = dict(mesh.shape)
    small = sizes["groups"] == 2 and sizes["dp"] == 4 and sizes["tensor"] == 4
    body = local if small else local_any
    in_specs = (
        P(("groups", "dp"), "tensor"),
        P("dp", "tensor"),
        P("tensor", None, None),
        P("tensor"),
        P("tensor"),
        P("tensor", None),
        P(("groups", "dp"), "tensor"),
    )
    out_specs = (
        P(("groups", "dp"), "tensor"),
        P(("groups", "dp"), "tensor"),
        P("tensor", ("groups", "dp"), None, None),
    )
    return jax.shard_map(body, mesh=mesh, in_specs=in_specs, out_specs=out_specs, check_vma=False)
```

```python
import functools

import jax
import jax.numpy as jnp
from jax import lax
from jax.experimental import pallas as pl
from jax.experimental.pallas import tpu as pltpu
from jax.sharding import PartitionSpec as P

CAP = 2
BF = jnp.bfloat16
F32 = jnp.float32
VMEM_BYTES = 56 * 2**20


def swap(array, axis, bit):
    size = lax.axis_size(axis)
    return lax.ppermute(array, axis, [(i, i ^ bit) for i in range(size)])


def params():
    return pltpu.CompilerParams(vmem_limit_bytes=VMEM_BYTES)


PARTS, FOLDED, LIVE, MASK, BLOCKS = 0, 4, 8, 9, 10


def forward_kernel(
    first, blocks, bs, cuts, folded, meta, x_ref, w_ref, delta_ref, d_ref, act_ref, slope_ref, sum_ref, acc
):
    width = acc.shape[1]
    group = pl.program_id(1) // cuts % 2
    parts = FOLDED if folded else PARTS

    @pl.when((pl.program_id(0) == 0) & (pl.program_id(1) == 0))
    def _():
        sum_ref[...] = jnp.zeros_like(sum_ref)

    total = None
    for s in range(w_ref.shape[0]):
        term = jnp.dot(x_ref[meta[parts + s]], w_ref[s], preferred_element_type=F32)
        total = term if total is None else total + term
    acc[...] = total
    start = first + pl.program_id(0) * width
    for n in range(blocks):
        at = BLOCKS + 4 * n
        col = meta[at + 3] - start

        @pl.when((col >= 0) & (col < width))
        def _():
            cols = pl.ds(pl.multiple_of(col, bs), bs)
            rows = pl.ds(pl.multiple_of(meta[at + 2], bs), bs)
            xs = x_ref[meta[at], :, rows]
            acc[:, cols] += jnp.dot(xs, delta_ref[n], preferred_element_type=F32)

    preact = acc[...]
    squash = jax.nn.sigmoid(preact)
    act_ref[0] = (preact * squash).astype(BF)
    slope = d_ref[...].astype(F32) * squash * (1.0 + preact * (1.0 - squash))
    if folded:
        slope = jnp.where(meta[LIVE] != 0, slope, 0.0)
    slope_ref[...] = slope.astype(BF)
    for n in range(blocks):
        at = BLOCKS + 4 * n
        col = meta[at + 3] - start

        @pl.when((col >= 0) & (col < width))
        def _():
            rows = pl.ds(pl.multiple_of(meta[at + 2], bs), bs)
            ds = slope_ref[:, pl.ds(pl.multiple_of(col, bs), bs)]
            sum_ref[group, n] += lax.dot_general(
                x_ref[meta[at], :, rows], ds, (((0,), (0,)), ((), ())), preferred_element_type=F32
            )


def forward(meta, x4, w4, delta, d_piece, first, groups_of, folded=False):
    rows, width = d_piece.shape
    slots, feats = w4.shape[0], w4.shape[1]
    cuts = 2
    tile = rows // groups_of // cuts
    blocks, bs = delta.shape[0], delta.shape[1]
    wide = next(c for c in (896, 640, 512, 384, 256, 128, width) if width % c == 0)
    return pl.pallas_call(
        functools.partial(forward_kernel, first, blocks, bs, cuts, folded),
        grid_spec=pltpu.PrefetchScalarGridSpec(
            num_scalar_prefetch=1,
            grid=(width // wide, groups_of * cuts),
            in_specs=[
                pl.BlockSpec((slots, tile, feats), lambda j, i, m: (0, i, 0)),
                pl.BlockSpec((slots, feats, wide), lambda j, i, m: (0, 0, j)),
                pl.BlockSpec(delta.shape, lambda j, i, m: (0, 0, 0)),
                pl.BlockSpec((tile, wide), lambda j, i, m: (i, j)),
            ],
            out_specs=[
                pl.BlockSpec((1, tile, wide), lambda j, i, m: (i // cuts, i % cuts, j)),
                pl.BlockSpec((tile, wide), lambda j, i, m: (i, j)),
                pl.BlockSpec((2, blocks, bs, bs), lambda j, i, m: (0, 0, 0, 0)),
            ],
            scratch_shapes=[pltpu.VMEM((tile, wide), F32)],
        ),
        out_shape=[
            jax.ShapeDtypeStruct((groups_of, rows // groups_of, width), BF),
            jax.ShapeDtypeStruct((rows, width), BF),
            jax.ShapeDtypeStruct((2, blocks, bs, bs), F32),
        ],
        compiler_params=params(),
        cost_estimate=pl.CostEstimate(
            flops=2 * rows * feats * slots * width,
            bytes_accessed=2 * (rows + width) * feats * slots,
            transcendentals=0,
        ),
    )(meta, x4, w4, delta, d_piece)


def backward_kernel(firsts, blocks, bs, has_acc, bit, meta, *refs):
    n = len(firsts)
    slopes, w_refs = refs[:n], refs[n : 2 * n]
    delta_ref = refs[2 * n]
    acc_in = refs[2 * n + 1] if has_acc else None
    outs, acc = refs[2 * n + 1 + has_acc : -1], refs[-1]
    size = acc.shape[1]
    step = pl.program_id(0)
    slot = step if bit is None else meta[PARTS + bit - step]
    base = pl.program_id(1) * size
    total = acc_in[0] if has_acc else None
    for p in range(n):
        term = lax.dot_general(
            slopes[p][...], w_refs[p][0], (((1,), (1,)), ((), ())), preferred_element_type=F32
        )
        total = term if total is None else total + term
    acc[...] = total
    for b in range(blocks):
        at = BLOCKS + 4 * b
        row = meta[at + 2] - base
        for p in range(n):
            col = meta[at + 3] - firsts[p]
            inside = (row >= 0) & (row < size) & (col >= 0) & (col < slopes[p].shape[1])

            @pl.when(inside & (meta[at + 1] == slot))
            def _():
                ds = slopes[p][:, pl.ds(pl.multiple_of(col, bs), bs)]
                acc[:, pl.ds(pl.multiple_of(row, bs), bs)] += lax.dot_general(
                    ds, delta_ref[b], (((1,), (1,)), ((), ())), preferred_element_type=F32
                )

    if len(outs) == 1:
        outs[0][0] = acc[...]
        return
    cut = outs[0].shape[0]
    for at_step in range(2):

        @pl.when(step == at_step)
        def _():
            outs[2 * at_step][...] = acc[:cut].astype(BF)
            outs[2 * at_step + 1][...] = acc[cut:].astype(BF)


def weight_block(piece_folded, slot_of, step, tile, meta):
    slot = slot_of(step, meta)
    return jnp.bitwise_xor(slot, meta[MASK]) if piece_folded else slot, tile, 0


def backward(meta, rows, slopes, ws, delta, firsts, acc, bit, folded, at_rows=0):
    slots, feats = ws[0].shape[0], ws[0].shape[1]
    blocks, bs = delta.shape[0], delta.shape[1]
    every = bit is None
    tiles = 4 if every else 2
    size = feats // tiles
    width = sum(s.shape[1] for s in slopes)
    steps = slots if every else 2

    def slot_of(step, meta):
        return step if every else meta[PARTS + bit - step]

    whole = pl.BlockSpec((1, rows, size), lambda s, i, m: (slot_of(s, m), 0, i))
    give = pl.BlockSpec((rows // 2, size), lambda s, i, m: (0, jnp.where(s == 0, i, tiles - 1)))
    keep = pl.BlockSpec((rows // 2, size), lambda s, i, m: (0, jnp.where(s == 0, 0, i)))
    if every:
        out_specs = [whole]
        out_shape = [jax.ShapeDtypeStruct((slots, rows, feats), F32)]
    else:
        out_specs = [give, give, keep, keep]
        out_shape = [jax.ShapeDtypeStruct((rows // 2, feats), BF)] * 4
    return pl.pallas_call(
        functools.partial(backward_kernel, firsts, blocks, bs, acc is not None, bit),
        grid_spec=pltpu.PrefetchScalarGridSpec(
            num_scalar_prefetch=1,
            grid=(steps, tiles),
            in_specs=[
                pl.BlockSpec(
                    (rows, s.shape[1]),
                    lambda s, i, m: (at_rows, 0),
                    pipeline_mode=pl.Buffered(1),
                )
                for s in slopes
            ]
            + [
                pl.BlockSpec(
                    (1, size, w.shape[2]), functools.partial(weight_block, f, slot_of)
                )
                for w, f in zip(ws, folded)
            ]
            + [pl.BlockSpec(delta.shape, lambda s, i, m: (0, 0, 0))]
            + ([] if acc is None else [whole]),
            out_specs=out_specs,
            scratch_shapes=[pltpu.VMEM((rows, size), F32)],
        ),
        out_shape=out_shape,
        compiler_params=params(),
        cost_estimate=pl.CostEstimate(
            flops=2 * rows * feats * width * steps if every else 1,
            bytes_accessed=2 * (rows + feats) * width * steps if every else 1,
            transcendentals=0,
        ),
    )(meta, *slopes, *ws, delta, *([] if acc is None else [acc]))


def slot_ranks(owners):
    owner_ids = owners[:, 0]
    order = jnp.arange(owner_ids.shape[0], dtype=jnp.int32)
    earlier = (owner_ids[None, :] == owner_ids[:, None]) & (order[None, :] < order[:, None])
    rank = jnp.sum(earlier.astype(jnp.int32), axis=1)
    return (owner_ids[None, :] == lax.axis_index("dp")) & (
        rank[None, :] == jnp.arange(CAP, dtype=jnp.int32)[:, None]
    )


def pick_slots(owners, total):
    wanted = slot_ranks(owners)
    return jnp.sum(jnp.where(wanted[:, :, None, None], total[None], 0.0), axis=1)[None]


def tie(value, *after):
    return lax.optimization_barrier((value,) + after)[0]


def piece_sizes(half, bs):
    blocks = half // bs
    fold, last = max(blocks // 3, 1), max(blocks // 5, 1)
    return [fold * bs, (blocks - fold - last) * bs, last * bs]


MIDDLE = [(1, 2), (2, 1)]
INWARD = [(0, 1), (3, 2)]
OUTWARD = [(1, 0), (2, 3)]


def to_dp(array, route):
    return lax.ppermute(array, "dp", route)


def gather_x(tokens):
    peer = swap(tokens, "groups", 1)
    own_far = swap(tokens, "tensor", 2)
    peer_far = swap(peer, "tensor", 2)
    near = jnp.concatenate([tokens, peer], axis=0)
    far = jnp.concatenate([own_far, peer_far], axis=0)
    return [near, swap(near, "tensor", 1), far, swap(far, "tensor", 1)]


def add_bf(left, right):
    return (left.astype(F32) + right.astype(F32)).astype(BF)


def local(tokens, frozen, delta, block_rows, block_cols, owners, d_out):
    group, me_dp, me_t = (lax.axis_index(a) for a in ("groups", "dp", "tensor"))
    n_dp, n_t = lax.axis_size("dp"), lax.axis_size("tensor")
    middle = (me_dp == 1) | (me_dp == 2)
    rows, feats = tokens.shape
    both = 2 * rows
    blocks, bs = delta.shape[0], delta.shape[1]
    slab = frozen.shape[1]
    half = slab // 2
    mine, theirs = group * half, (1 - group) * half
    sizes = piece_sizes(half, bs)
    firsts = [sum(sizes[:p]) for p in range(len(sizes))]

    shards = [
        lax.dynamic_slice(frozen, (0, mine + first), (frozen.shape[0], size))
        for first, size in zip(firsts, sizes)
    ]
    gather_a = lax.all_gather(shards[1], "dp")
    outer = to_dp(shards[0], INWARD)
    inner = to_dp(shards[0], MIDDLE)
    w_fold = jnp.stack([shards[0], outer, to_dp(outer, MIDDLE), inner])

    row_part = block_rows * bs // feats
    block_info = jnp.stack(
        [
            row_part ^ me_t,
            row_part,
            block_rows * bs - row_part * feats,
            block_cols * bs - (me_t * slab + mine),
        ],
        axis=1,
    )
    slots = jnp.arange(n_t, dtype=jnp.int32)
    meta = jnp.concatenate(
        [
            slots ^ me_t,
            slots ^ (me_t ^ me_dp),
            jnp.where(jnp.arange(2) == 0, middle.astype(jnp.int32), me_dp),
            block_info.reshape(-1),
        ]
    )

    end_tokens = to_dp(tokens, INWARD)
    own_parts = gather_x(tokens)
    end_parts = gather_x(tie(end_tokens, own_parts[0]))
    x4 = jnp.stack([jnp.concatenate(pair, axis=0) for pair in zip(own_parts, end_parts)])

    order = own_parts[2]
    d_pieces = []
    for first, size in zip(firsts, sizes):
        give = lax.dynamic_slice(d_out, (0, theirs + first), (rows, size))
        keep = lax.dynamic_slice(d_out, (0, mine + first), (rows, size))
        got = swap(tie(give, order), "groups", 1)
        order = got
        d_pieces.append(jnp.concatenate([keep, got], axis=0))
    d_fold = jnp.concatenate([d_pieces[0], to_dp(d_pieces[0], INWARD)], axis=0)
    gather_b = lax.all_gather(
        tie(shards[2], gather_a, x4, d_fold, w_fold, *d_pieces[1:]), "dp"
    )

    act_f, slope_f, sums_f = forward(meta, x4, w_fold, delta, d_fold, firsts[0], 4, True)
    over = swap(jnp.concatenate([act_f[1:2], act_f[3:4]], axis=0), "groups", 1)
    home = to_dp(jnp.concatenate([act_f[2:3], over[1:2]], axis=0), OUTWARD)
    activated = jnp.zeros((rows, slab), BF)
    kept = jnp.where(middle, act_f[0], home[0])
    activated = lax.dynamic_update_slice(activated, kept, (0, mine + firsts[0]))
    kept = jnp.where(middle, over[0], home[1])
    activated = lax.dynamic_update_slice(activated, kept, (0, theirs + firsts[0]))

    diagonal = [(i, i ^ (n_t + 2)) for i in range(2 * n_t)]

    def spread(far, near):
        far_peer = add_bf(far[3], swap(far[1], "tensor", 1))
        far_own = add_bf(far[2], swap(far[0], "tensor", 1))
        from_xy = lax.ppermute(far_peer, ("groups", "tensor"), diagonal)
        from_x = swap(far_own, "tensor", 2)
        near_peer = add_bf(near[3], swap(near[1], "tensor", 1))
        from_y = swap(near_peer, "groups", 1)
        near_own = near[2].astype(F32) + swap(near[0], "tensor", 1).astype(F32)
        return near_own + from_y.astype(F32) + from_x.astype(F32) + from_xy.astype(F32)

    def end_back(bit, wait):
        return backward(
            meta, both, [slope_f], [w_fold], tie(delta, wait), firsts[:1], None, bit, [True], 1
        )

    end_far = end_back(3, slope_f)
    end_near = end_back(1, end_far[1])
    end_sum = spread(end_far, end_near).astype(BF)
    end_home = to_dp(end_sum, OUTWARD)

    delta_a = tie(delta, end_near[1])
    act_a, slope_a, sums_a = forward(meta, x4, gather_a, delta_a, d_pieces[1], firsts[1], 2)
    back_a = swap(act_a[1], "groups", 1)
    (early,) = backward(
        meta, both, [slope_f, slope_a], [w_fold, gather_a], tie(delta, over), firsts[:2], None,
        None, [True, False],
    )
    activated = lax.dynamic_update_slice(activated, act_a[0], (0, mine + firsts[1]))
    activated = lax.dynamic_update_slice(activated, back_a, (0, theirs + firsts[1]))

    delta_b = tie(delta, early, activated, end_sum)
    act_b, slope_b, sums_b = forward(meta, x4, gather_b, delta_b, d_pieces[2], firsts[2], 2)
    back_b = swap(act_b[1], "groups", 1)
    activated = lax.dynamic_update_slice(activated, act_b[0], (0, mine + firsts[2]))
    activated = lax.dynamic_update_slice(activated, back_b, (0, theirs + firsts[2]))

    sums = sums_f + sums_a + sums_b
    sums = sums[0] + swap(sums[1].astype(BF), "groups", 1).astype(F32)
    shares = [swap(sums.astype(BF), "dp", bit) for bit in range(1, n_dp)]

    def last_back(bit, *wait):
        return backward(
            meta, both, [slope_b], [gather_b], tie(delta_b, *wait), firsts[2:], early, bit, [False]
        )

    far = list(last_back(3, slope_b))
    near = last_back(1, far[1], sums)
    far[2], far[3] = tie(far[2], near[1]), tie(far[3], near[1], back_b, end_home, *shares)
    d_tokens = spread(far, near) + end_home.astype(F32)
    for share in shares:
        sums = sums + share.astype(F32)
    norm = float(rows * n_dp) ** (-0.5)
    return (activated, d_tokens.astype(BF), pick_slots(owners, sums * norm))


def local_any(tokens, frozen, delta, block_rows, block_cols, owners, d_out):
    me_dp, me_t, n_dp = lax.axis_index("dp"), lax.axis_index("tensor"), lax.axis_size("dp")
    rows = tokens.shape[0]
    blocks, bs = delta.shape[0], delta.shape[1]
    slab = frozen.shape[1]
    x_full = lax.all_gather(tokens, "tensor", axis=1, tiled=True)
    weight = lax.all_gather(frozen, "dp", axis=0, tiled=True)
    width = x_full.shape[1]
    row_pick = (block_rows[:, None] == jnp.arange(width // bs)[None, :]).astype(F32)
    cols_here = block_cols - me_t * (slab // bs)
    col_pick = (cols_here[:, None] == jnp.arange(slab // bs)[None, :]).astype(F32)
    highest = lax.Precision.HIGHEST
    xb = jnp.take(x_full.reshape(rows, width // bs, bs), block_rows, axis=1)
    contrib = jnp.einsum("tnk,nkc->tnc", xb, delta, preferred_element_type=F32)
    add = jnp.einsum("tnc,nm->tmc", contrib, col_pick, precision=highest).reshape(rows, slab)
    preact = jnp.dot(x_full, weight, preferred_element_type=F32) + add
    squash = jax.nn.sigmoid(preact)
    activated = (preact * squash).astype(BF)
    d_pre = (d_out.astype(F32) * squash * (1.0 + preact * (1.0 - squash))).astype(BF)
    d_rows = lax.dot_general(
        d_pre, weight, (((1,), (1,)), ((), ())), preferred_element_type=F32
    )
    dy = jnp.take(d_pre.reshape(rows, slab // bs, bs), cols_here, axis=1)
    back = jnp.einsum("tnc,nkc->tnk", dy, delta, preferred_element_type=F32)
    back = jnp.einsum("tnk,nr->trk", back, row_pick, precision=highest).reshape(rows, width)
    d_tokens = lax.psum_scatter(
        (d_rows + back).astype(BF), "tensor", scatter_dimension=1, tiled=True
    )
    grads = jnp.einsum("tnk,tnc->nkc", xb, dy, preferred_element_type=F32)
    everyone = lax.all_gather(grads.astype(BF), "dp", axis=0).astype(F32)
    norm = float(rows * n_dp) ** (-0.5)
    return (activated, d_tokens, pick_slots(owners, jnp.sum(everyone, axis=0) * norm))


def solution(mesh):
    sizes = dict(mesh.shape)
    small = sizes["groups"] == 2 and sizes["dp"] == 4 and sizes["tensor"] == 4
    body = local if small else local_any
    in_specs = (
        P(("groups", "dp"), "tensor"),
        P("dp", "tensor"),
        P("tensor", None, None),
        P("tensor"),
        P("tensor"),
        P("tensor", None),
        P(("groups", "dp"), "tensor"),
    )
    out_specs = (
        P(("groups", "dp"), "tensor"),
        P(("groups", "dp"), "tensor"),
        P("tensor", ("groups", "dp"), None, None),
    )
    return jax.shard_map(body, mesh=mesh, in_specs=in_specs, out_specs=out_specs, check_vma=False)
```

```python
import functools

import jax
import jax.numpy as jnp
from jax import lax
from jax.experimental import pallas as pl
from jax.experimental.pallas import tpu as pltpu
from jax.sharding import PartitionSpec as P

CAP = 2
BF = jnp.bfloat16
F32 = jnp.float32
VMEM_BYTES = 56 * 2**20


def swap(array, axis, bit):
    size = lax.axis_size(axis)
    return lax.ppermute(array, axis, [(i, i ^ bit) for i in range(size)])


def params():
    return pltpu.CompilerParams(vmem_limit_bytes=VMEM_BYTES)


PARTS, FOLDED, LIVE, MASK, BLOCKS = 0, 4, 8, 9, 10


def forward_kernel(
    first, blocks, bs, cuts, folded, meta, x_ref, w_ref, delta_ref, d_ref, act_ref, slope_ref, sum_ref, acc
):
    width = acc.shape[1]
    group = pl.program_id(1) // cuts % 2
    parts = FOLDED if folded else PARTS

    @pl.when((pl.program_id(0) == 0) & (pl.program_id(1) == 0))
    def _():
        sum_ref[...] = jnp.zeros_like(sum_ref)

    total = None
    for s in range(w_ref.shape[0]):
        term = jnp.dot(x_ref[meta[parts + s]], w_ref[s], preferred_element_type=F32)
        total = term if total is None else total + term
    acc[...] = total
    start = first + pl.program_id(0) * width
    for n in range(blocks):
        at = BLOCKS + 4 * n
        col = meta[at + 3] - start

        @pl.when((col >= 0) & (col < width))
        def _():
            cols = pl.ds(pl.multiple_of(col, bs), bs)
            rows = pl.ds(pl.multiple_of(meta[at + 2], bs), bs)
            xs = x_ref[meta[at], :, rows]
            acc[:, cols] += jnp.dot(xs, delta_ref[n], preferred_element_type=F32)

    preact = acc[...]
    squash = jax.nn.sigmoid(preact)
    act_ref[0] = (preact * squash).astype(BF)
    slope = d_ref[...].astype(F32) * squash * (1.0 + preact * (1.0 - squash))
    if folded:
        slope = jnp.where(meta[LIVE] != 0, slope, 0.0)
    slope_ref[...] = slope.astype(BF)
    for n in range(blocks):
        at = BLOCKS + 4 * n
        col = meta[at + 3] - start

        @pl.when((col >= 0) & (col < width))
        def _():
            rows = pl.ds(pl.multiple_of(meta[at + 2], bs), bs)
            ds = slope_ref[:, pl.ds(pl.multiple_of(col, bs), bs)]
            sum_ref[group, n] += lax.dot_general(
                x_ref[meta[at], :, rows], ds, (((0,), (0,)), ((), ())), preferred_element_type=F32
            )


def forward(meta, x4, w4, delta, d_piece, first, groups_of, folded=False):
    rows, width = d_piece.shape
    slots, feats = w4.shape[0], w4.shape[1]
    cuts = 2
    tile = rows // groups_of // cuts
    blocks, bs = delta.shape[0], delta.shape[1]
    wide = next(c for c in (768, 640, 512, 384, 256, 128, width) if width % c == 0)
    return pl.pallas_call(
        functools.partial(forward_kernel, first, blocks, bs, cuts, folded),
        grid_spec=pltpu.PrefetchScalarGridSpec(
            num_scalar_prefetch=1,
            grid=(width // wide, groups_of * cuts),
            in_specs=[
                pl.BlockSpec((slots, tile, feats), lambda j, i, m: (0, i, 0)),
                pl.BlockSpec((slots, feats, wide), lambda j, i, m: (0, 0, j)),
                pl.BlockSpec(delta.shape, lambda j, i, m: (0, 0, 0)),
                pl.BlockSpec((tile, wide), lambda j, i, m: (i, j)),
            ],
            out_specs=[
                pl.BlockSpec((1, tile, wide), lambda j, i, m: (i // cuts, i % cuts, j)),
                pl.BlockSpec((tile, wide), lambda j, i, m: (i, j)),
                pl.BlockSpec((2, blocks, bs, bs), lambda j, i, m: (0, 0, 0, 0)),
            ],
            scratch_shapes=[pltpu.VMEM((tile, wide), F32)],
        ),
        out_shape=[
            jax.ShapeDtypeStruct((groups_of, rows // groups_of, width), BF),
            jax.ShapeDtypeStruct((rows, width), BF),
            jax.ShapeDtypeStruct((2, blocks, bs, bs), F32),
        ],
        compiler_params=params(),
        cost_estimate=pl.CostEstimate(flops=1, bytes_accessed=1, transcendentals=0),
    )(meta, x4, w4, delta, d_piece)


def backward_kernel(firsts, blocks, bs, has_acc, bit, meta, *refs):
    n = len(firsts)
    slopes, w_refs = refs[:n], refs[n : 2 * n]
    delta_ref = refs[2 * n]
    acc_in = refs[2 * n + 1] if has_acc else None
    outs, acc = refs[2 * n + 1 + has_acc : -1], refs[-1]
    size = acc.shape[1]
    step = pl.program_id(0)
    slot = step if bit is None else meta[PARTS + bit - step]
    base = pl.program_id(1) * size
    total = acc_in[0] if has_acc else None
    for p in range(n):
        term = lax.dot_general(
            slopes[p][...], w_refs[p][0], (((1,), (1,)), ((), ())), preferred_element_type=F32
        )
        total = term if total is None else total + term
    acc[...] = total
    for b in range(blocks):
        at = BLOCKS + 4 * b
        row = meta[at + 2] - base
        for p in range(n):
            col = meta[at + 3] - firsts[p]
            inside = (row >= 0) & (row < size) & (col >= 0) & (col < slopes[p].shape[1])

            @pl.when(inside & (meta[at + 1] == slot))
            def _():
                ds = slopes[p][:, pl.ds(pl.multiple_of(col, bs), bs)]
                acc[:, pl.ds(pl.multiple_of(row, bs), bs)] += lax.dot_general(
                    ds, delta_ref[b], (((1,), (1,)), ((), ())), preferred_element_type=F32
                )

    if len(outs) == 1:
        outs[0][0] = acc[...]
        return
    cut = outs[0].shape[0]
    for at_step in range(2):

        @pl.when(step == at_step)
        def _():
            outs[2 * at_step][...] = acc[:cut].astype(BF)
            outs[2 * at_step + 1][...] = acc[cut:].astype(BF)


def weight_block(piece_folded, slot_of, step, tile, meta):
    slot = slot_of(step, meta)
    return jnp.bitwise_xor(slot, meta[MASK]) if piece_folded else slot, tile, 0


def backward(meta, rows, slopes, ws, delta, firsts, acc, bit, folded, at_rows=0):
    slots, feats = ws[0].shape[0], ws[0].shape[1]
    blocks, bs = delta.shape[0], delta.shape[1]
    every = bit is None
    tiles = 4 if every else 2
    size = feats // tiles
    width = sum(s.shape[1] for s in slopes)
    steps = slots if every else 2

    def slot_of(step, meta):
        return step if every else meta[PARTS + bit - step]

    whole = pl.BlockSpec((1, rows, size), lambda s, i, m: (slot_of(s, m), 0, i))
    give = pl.BlockSpec((rows // 2, size), lambda s, i, m: (0, jnp.where(s == 0, i, tiles - 1)))
    keep = pl.BlockSpec((rows // 2, size), lambda s, i, m: (0, jnp.where(s == 0, 0, i)))
    if every:
        out_specs = [whole]
        out_shape = [jax.ShapeDtypeStruct((slots, rows, feats), F32)]
    else:
        out_specs = [give, give, keep, keep]
        out_shape = [jax.ShapeDtypeStruct((rows // 2, feats), BF)] * 4
    return pl.pallas_call(
        functools.partial(backward_kernel, firsts, blocks, bs, acc is not None, bit),
        grid_spec=pltpu.PrefetchScalarGridSpec(
            num_scalar_prefetch=1,
            grid=(steps, tiles),
            in_specs=[
                pl.BlockSpec(
                    (rows, s.shape[1]),
                    lambda s, i, m: (at_rows, 0),
                    pipeline_mode=pl.Buffered(1),
                )
                for s in slopes
            ]
            + [
                pl.BlockSpec(
                    (1, size, w.shape[2]), functools.partial(weight_block, f, slot_of)
                )
                for w, f in zip(ws, folded)
            ]
            + [pl.BlockSpec(delta.shape, lambda s, i, m: (0, 0, 0))]
            + ([] if acc is None else [whole]),
            out_specs=out_specs,
            scratch_shapes=[pltpu.VMEM((rows, size), F32)],
        ),
        out_shape=out_shape,
        compiler_params=params(),
        cost_estimate=pl.CostEstimate(flops=1, bytes_accessed=1, transcendentals=0),
    )(meta, *slopes, *ws, delta, *([] if acc is None else [acc]))


def slot_ranks(owners):
    owner_ids = owners[:, 0]
    order = jnp.arange(owner_ids.shape[0], dtype=jnp.int32)
    earlier = (owner_ids[None, :] == owner_ids[:, None]) & (order[None, :] < order[:, None])
    rank = jnp.sum(earlier.astype(jnp.int32), axis=1)
    return (owner_ids[None, :] == lax.axis_index("dp")) & (
        rank[None, :] == jnp.arange(CAP, dtype=jnp.int32)[:, None]
    )


def pick_slots(owners, total):
    wanted = slot_ranks(owners)
    return jnp.sum(jnp.where(wanted[:, :, None, None], total[None], 0.0), axis=1)[None]


def tie(value, *after):
    return lax.optimization_barrier((value,) + after)[0]


def piece_sizes(half, bs):
    blocks = half // bs
    last = max(blocks // 5, 1)
    fold = blocks - last
    return [(fold - fold // 2) * bs, fold // 2 * bs, last * bs]


MIDDLE = [(1, 2), (2, 1)]
INWARD = [(0, 1), (3, 2)]
OUTWARD = [(1, 0), (2, 3)]


def to_dp(array, route):
    return lax.ppermute(array, "dp", route)


def gather_x(tokens):
    peer = swap(tokens, "groups", 1)
    own_far = swap(tokens, "tensor", 2)
    peer_far = swap(peer, "tensor", 2)
    near = jnp.concatenate([tokens, peer], axis=0)
    far = jnp.concatenate([own_far, peer_far], axis=0)
    return [near, swap(near, "tensor", 1), far, swap(far, "tensor", 1)]


def add_bf(left, right):
    return (left.astype(F32) + right.astype(F32)).astype(BF)


def local(tokens, frozen, delta, block_rows, block_cols, owners, d_out):
    group, me_dp, me_t = (lax.axis_index(a) for a in ("groups", "dp", "tensor"))
    n_dp, n_t = lax.axis_size("dp"), lax.axis_size("tensor")
    middle = (me_dp == 1) | (me_dp == 2)
    rows, feats = tokens.shape
    both = 2 * rows
    blocks, bs = delta.shape[0], delta.shape[1]
    slab = frozen.shape[1]
    half = slab // 2
    mine, theirs = group * half, (1 - group) * half
    sizes = piece_sizes(half, bs)
    firsts = [sum(sizes[:p]) for p in range(len(sizes))]

    shards = [
        lax.dynamic_slice(frozen, (0, mine + first), (frozen.shape[0], size))
        for first, size in zip(firsts, sizes)
    ]
    outer = to_dp(shards[0], INWARD)
    inner = to_dp(shards[0], MIDDLE)
    far_end = to_dp(outer, MIDDLE)
    w_0 = jnp.stack([shards[0], outer, far_end, inner])
    outer = to_dp(tie(shards[1], outer), INWARD)
    inner = to_dp(tie(shards[1], inner), MIDDLE)
    far_end = to_dp(outer, MIDDLE)
    w_1 = jnp.stack([shards[1], outer, far_end, inner])
    gather_b = lax.all_gather(tie(shards[2], far_end, inner), "dp")

    row_part = block_rows * bs // feats
    block_info = jnp.stack(
        [
            row_part ^ me_t,
            row_part,
            block_rows * bs - row_part * feats,
            block_cols * bs - (me_t * slab + mine),
        ],
        axis=1,
    )
    slots = jnp.arange(n_t, dtype=jnp.int32)
    meta = jnp.concatenate(
        [
            slots ^ me_t,
            slots ^ (me_t ^ me_dp),
            jnp.where(jnp.arange(2) == 0, middle.astype(jnp.int32), me_dp),
            block_info.reshape(-1),
        ]
    )

    end_tokens = to_dp(tokens, INWARD)
    own_parts = gather_x(tokens)
    end_parts = gather_x(tie(end_tokens, own_parts[0]))
    x4 = jnp.stack([jnp.concatenate(pair, axis=0) for pair in zip(own_parts, end_parts)])

    order = own_parts[2]
    d_pieces = []
    for first, size in zip(firsts, sizes):
        give = lax.dynamic_slice(d_out, (0, theirs + first), (rows, size))
        keep = lax.dynamic_slice(d_out, (0, mine + first), (rows, size))
        got = swap(tie(give, order), "groups", 1)
        order = got
        d_pieces.append(jnp.concatenate([keep, got], axis=0))
    d_fold = [jnp.concatenate([d, to_dp(d, INWARD)], axis=0) for d in d_pieces[:2]]

    def fold(weight, piece, wait):
        return forward(meta, x4, weight, tie(delta, wait), d_fold[piece], firsts[piece], 4, True)

    def send_home(act):
        over = swap(jnp.concatenate([act[1:2], act[3:4]], axis=0), "groups", 1)
        return over, to_dp(jnp.concatenate([act[2:3], over[1:2]], axis=0), OUTWARD)

    def place(activated, act, over, home, first):
        kept = jnp.where(middle, act[0], home[0])
        activated = lax.dynamic_update_slice(activated, kept, (0, mine + first))
        kept = jnp.where(middle, over[0], home[1])
        return lax.dynamic_update_slice(activated, kept, (0, theirs + first))

    act_0, slope_0, sums_0 = fold(w_0, 0, d_pieces[2])
    over_0, home_0 = send_home(act_0)
    act_1, slope_1, sums_1 = fold(w_1, 1, slope_0)
    over_1, home_1 = send_home(act_1)
    slopes, weights = [slope_0, slope_1], [w_0, w_1]

    diagonal = [(i, i ^ (n_t + 2)) for i in range(2 * n_t)]

    def spread(far, near):
        far_peer = add_bf(far[3], swap(far[1], "tensor", 1))
        far_own = add_bf(far[2], swap(far[0], "tensor", 1))
        from_xy = lax.ppermute(far_peer, ("groups", "tensor"), diagonal)
        from_x = swap(far_own, "tensor", 2)
        near_peer = add_bf(near[3], swap(near[1], "tensor", 1))
        from_y = swap(near_peer, "groups", 1)
        near_own = near[2].astype(F32) + swap(near[0], "tensor", 1).astype(F32)
        return near_own + from_y.astype(F32) + from_x.astype(F32) + from_xy.astype(F32)

    def end_back(bit, wait):
        return backward(
            meta, both, slopes, weights, tie(delta, wait), firsts[:2], None, bit, [True, True], 1
        )

    end_far = end_back(3, slope_1)
    end_near = end_back(1, end_far[1])
    end_sum = spread(end_far, end_near).astype(BF)
    end_home = to_dp(end_sum, OUTWARD)
    (early,) = backward(
        meta, both, slopes, weights, tie(delta, end_near[1], over_1, gather_b), firsts[:2], None, None,
        [True, True],
    )
    activated = jnp.zeros((rows, slab), BF)
    activated = place(activated, act_0, over_0, home_0, firsts[0])

    delta_b = tie(delta, early)
    act_b, slope_b, sums_b = forward(meta, x4, gather_b, delta_b, d_pieces[2], firsts[2], 2)
    back_b = swap(act_b[1], "groups", 1)
    activated = place(activated, act_1, over_1, home_1, firsts[1])
    activated = lax.dynamic_update_slice(activated, act_b[0], (0, mine + firsts[2]))
    activated = lax.dynamic_update_slice(activated, back_b, (0, theirs + firsts[2]))

    sums = sums_0 + sums_1 + sums_b
    sums = sums[0] + swap(sums[1].astype(BF), "groups", 1).astype(F32)
    shares = [swap(sums.astype(BF), "dp", bit) for bit in range(1, n_dp)]

    def last_back(bit, *wait):
        return backward(
            meta, both, [slope_b], [gather_b], tie(delta_b, *wait), firsts[2:], early, bit, [False]
        )

    far = list(last_back(3, slope_b, home_0, end_sum))
    near = last_back(1, far[1], sums, home_1)
    far[2], far[3] = tie(far[2], near[1]), tie(far[3], near[1], back_b, end_home, *shares)
    d_tokens = spread(far, near) + end_home.astype(F32)
    for share in shares:
        sums = sums + share.astype(F32)
    norm = float(rows * n_dp) ** (-0.5)
    return (activated, d_tokens.astype(BF), pick_slots(owners, sums * norm))


def local_any(tokens, frozen, delta, block_rows, block_cols, owners, d_out):
    me_dp, me_t, n_dp = lax.axis_index("dp"), lax.axis_index("tensor"), lax.axis_size("dp")
    rows = tokens.shape[0]
    blocks, bs = delta.shape[0], delta.shape[1]
    slab = frozen.shape[1]
    x_full = lax.all_gather(tokens, "tensor", axis=1, tiled=True)
    weight = lax.all_gather(frozen, "dp", axis=0, tiled=True)
    width = x_full.shape[1]
    row_pick = (block_rows[:, None] == jnp.arange(width // bs)[None, :]).astype(F32)
    cols_here = block_cols - me_t * (slab // bs)
    col_pick = (cols_here[:, None] == jnp.arange(slab // bs)[None, :]).astype(F32)
    highest = lax.Precision.HIGHEST
    xb = jnp.take(x_full.reshape(rows, width // bs, bs), block_rows, axis=1)
    contrib = jnp.einsum("tnk,nkc->tnc", xb, delta, preferred_element_type=F32)
    add = jnp.einsum("tnc,nm->tmc", contrib, col_pick, precision=highest).reshape(rows, slab)
    preact = jnp.dot(x_full, weight, preferred_element_type=F32) + add
    squash = jax.nn.sigmoid(preact)
    activated = (preact * squash).astype(BF)
    d_pre = (d_out.astype(F32) * squash * (1.0 + preact * (1.0 - squash))).astype(BF)
    d_rows = lax.dot_general(
        d_pre, weight, (((1,), (1,)), ((), ())), preferred_element_type=F32
    )
    dy = jnp.take(d_pre.reshape(rows, slab // bs, bs), cols_here, axis=1)
    back = jnp.einsum("tnc,nkc->tnk", dy, delta, preferred_element_type=F32)
    back = jnp.einsum("tnk,nr->trk", back, row_pick, precision=highest).reshape(rows, width)
    d_tokens = lax.psum_scatter(
        (d_rows + back).astype(BF), "tensor", scatter_dimension=1, tiled=True
    )
    grads = jnp.einsum("tnk,tnc->nkc", xb, dy, preferred_element_type=F32)
    everyone = lax.all_gather(grads.astype(BF), "dp", axis=0).astype(F32)
    norm = float(rows * n_dp) ** (-0.5)
    return (activated, d_tokens, pick_slots(owners, jnp.sum(everyone, axis=0) * norm))


def solution(mesh):
    sizes = dict(mesh.shape)
    small = sizes["groups"] == 2 and sizes["dp"] == 4 and sizes["tensor"] == 4
    body = local if small else local_any
    in_specs = (
        P(("groups", "dp"), "tensor"),
        P("dp", "tensor"),
        P("tensor", None, None),
        P("tensor"),
        P("tensor"),
        P("tensor", None),
        P(("groups", "dp"), "tensor"),
    )
    out_specs = (
        P(("groups", "dp"), "tensor"),
        P(("groups", "dp"), "tensor"),
        P("tensor", ("groups", "dp"), None, None),
    )
    return jax.shard_map(body, mesh=mesh, in_specs=in_specs, out_specs=out_specs, check_vma=False)
```

```python
import functools

import jax
import jax.numpy as jnp
from jax import lax
from jax.experimental import pallas as pl
from jax.experimental.pallas import tpu as pltpu
from jax.sharding import PartitionSpec as P

CAP = 2
BF = jnp.bfloat16
F32 = jnp.float32
VMEM_BYTES = 56 * 2**20


def swap(array, axis, bit):
    size = lax.axis_size(axis)
    return lax.ppermute(array, axis, [(i, i ^ bit) for i in range(size)])


def params():
    return pltpu.CompilerParams(vmem_limit_bytes=VMEM_BYTES)


PARTS, BLOCKS = 0, 4


def forward_kernel(
    first, blocks, bs, cuts, meta, x_ref, w_ref, delta_ref, d_ref, act_ref, slope_ref, sum_ref, acc
):
    width = acc.shape[1]
    group = pl.program_id(1) // cuts

    @pl.when((pl.program_id(0) == 0) & (pl.program_id(1) == 0))
    def _():
        sum_ref[...] = jnp.zeros_like(sum_ref)

    total = None
    for s in range(w_ref.shape[0]):
        term = jnp.dot(x_ref[meta[PARTS + s]], w_ref[s], preferred_element_type=F32)
        total = term if total is None else total + term
    acc[...] = total
    start = first + pl.program_id(0) * width
    for n in range(blocks):
        at = BLOCKS + 4 * n
        col = meta[at + 3] - start

        @pl.when((col >= 0) & (col < width))
        def _():
            cols = pl.ds(pl.multiple_of(col, bs), bs)
            rows = pl.ds(pl.multiple_of(meta[at + 2], bs), bs)
            xs = x_ref[meta[at], :, rows]
            acc[:, cols] += jnp.dot(xs, delta_ref[n], preferred_element_type=F32)

    preact = acc[...]
    squash = jax.nn.sigmoid(preact)
    act_ref[0] = (preact * squash).astype(BF)
    slope_ref[...] = (
        d_ref[...].astype(F32) * squash * (1.0 + preact * (1.0 - squash))
    ).astype(BF)
    for n in range(blocks):
        at = BLOCKS + 4 * n
        col = meta[at + 3] - start

        @pl.when((col >= 0) & (col < width))
        def _():
            rows = pl.ds(pl.multiple_of(meta[at + 2], bs), bs)
            ds = slope_ref[:, pl.ds(pl.multiple_of(col, bs), bs)]
            sum_ref[group, n] += lax.dot_general(
                x_ref[meta[at], :, rows], ds, (((0,), (0,)), ((), ())), preferred_element_type=F32
            )


def forward(meta, x4, w4, delta, d_piece, first, groups_of):
    rows, width = d_piece.shape
    slots, feats = w4.shape[0], w4.shape[1]
    cuts = 1
    tile = rows // groups_of // cuts
    blocks, bs = delta.shape[0], delta.shape[1]
    wide = next(c for c in (512, 384, 256, 128, width) if width % c == 0)
    return pl.pallas_call(
        functools.partial(forward_kernel, first, blocks, bs, cuts),
        grid_spec=pltpu.PrefetchScalarGridSpec(
            num_scalar_prefetch=1,
            grid=(width // wide, groups_of * cuts),
            in_specs=[
                pl.BlockSpec((slots, tile, feats), lambda j, i, m: (0, i, 0)),
                pl.BlockSpec((slots, feats, wide), lambda j, i, m: (0, 0, j)),
                pl.BlockSpec(delta.shape, lambda j, i, m: (0, 0, 0)),
                pl.BlockSpec((tile, wide), lambda j, i, m: (i, j)),
            ],
            out_specs=[
                pl.BlockSpec((1, tile, wide), lambda j, i, m: (i // cuts, i % cuts, j)),
                pl.BlockSpec((tile, wide), lambda j, i, m: (i, j)),
                pl.BlockSpec((groups_of, blocks, bs, bs), lambda j, i, m: (0, 0, 0, 0)),
            ],
            scratch_shapes=[pltpu.VMEM((tile, wide), F32)],
        ),
        out_shape=[
            jax.ShapeDtypeStruct((groups_of, rows // groups_of, width), BF),
            jax.ShapeDtypeStruct((rows, width), BF),
            jax.ShapeDtypeStruct((groups_of, blocks, bs, bs), F32),
        ],
        compiler_params=params(),
        cost_estimate=pl.CostEstimate(flops=1, bytes_accessed=1, transcendentals=0),
    )(meta, x4, w4, delta, d_piece)


def backward_kernel(firsts, blocks, bs, has_acc, bit, meta, *refs):
    n = len(firsts)
    slopes, w_refs = refs[:n], refs[n : 2 * n]
    delta_ref = refs[2 * n]
    acc_in = refs[2 * n + 1] if has_acc else None
    outs, acc = refs[2 * n + 1 + has_acc : -1], refs[-1]
    size = acc.shape[1]
    step = pl.program_id(0)
    slot = step if bit is None else meta[PARTS + bit - step]
    base = pl.program_id(1) * size
    total = acc_in[0] if has_acc else None
    for p in range(n):
        term = lax.dot_general(
            slopes[p][...], w_refs[p][0], (((1,), (1,)), ((), ())), preferred_element_type=F32
        )
        total = term if total is None else total + term
    acc[...] = total
    for b in range(blocks):
        at = BLOCKS + 4 * b
        row = meta[at + 2] - base
        for p in range(n):
            col = meta[at + 3] - firsts[p]
            inside = (row >= 0) & (row < size) & (col >= 0) & (col < slopes[p].shape[1])

            @pl.when(inside & (meta[at + 1] == slot))
            def _():
                ds = slopes[p][:, pl.ds(pl.multiple_of(col, bs), bs)]
                acc[:, pl.ds(pl.multiple_of(row, bs), bs)] += lax.dot_general(
                    ds, delta_ref[b], (((1,), (1,)), ((), ())), preferred_element_type=F32
                )

    if len(outs) == 1:
        outs[0][0] = acc[...]
        return
    cut = outs[0].shape[0]
    for at_step in range(2):

        @pl.when(step == at_step)
        def _():
            outs[2 * at_step][...] = acc[:cut].astype(BF)
            outs[2 * at_step + 1][...] = acc[cut:].astype(BF)


def backward(meta, slopes, ws, delta, firsts, acc, bit):
    rows = slopes[0].shape[0]
    slots, feats = ws[0].shape[0], ws[0].shape[1]
    blocks, bs = delta.shape[0], delta.shape[1]
    every = bit is None
    tiles = 4 if every else 2
    size = feats // tiles
    width = sum(s.shape[1] for s in slopes)
    steps = slots if every else 2

    def slot_of(step, meta):
        return step if every else meta[PARTS + bit - step]

    whole = pl.BlockSpec((1, rows, size), lambda s, i, m: (slot_of(s, m), 0, i))
    give = pl.BlockSpec((rows // 2, size), lambda s, i, m: (0, jnp.where(s == 0, i, tiles - 1)))
    keep = pl.BlockSpec((rows // 2, size), lambda s, i, m: (0, jnp.where(s == 0, 0, i)))
    if every:
        out_specs = [whole]
        out_shape = [jax.ShapeDtypeStruct((slots, rows, feats), F32)]
    else:
        out_specs = [give, give, keep, keep]
        out_shape = [jax.ShapeDtypeStruct((rows // 2, feats), BF)] * 4
    return pl.pallas_call(
        functools.partial(backward_kernel, firsts, blocks, bs, acc is not None, bit),
        grid_spec=pltpu.PrefetchScalarGridSpec(
            num_scalar_prefetch=1,
            grid=(steps, tiles),
            in_specs=[
                pl.BlockSpec(s.shape, lambda s, i, m: (0, 0), pipeline_mode=pl.Buffered(1))
                for s in slopes
            ]
            + [
                pl.BlockSpec((1, size, w.shape[2]), lambda s, i, m: (slot_of(s, m), i, 0))
                for w in ws
            ]
            + [pl.BlockSpec(delta.shape, lambda s, i, m: (0, 0, 0))]
            + ([] if acc is None else [whole]),
            out_specs=out_specs,
            scratch_shapes=[pltpu.VMEM((rows, size), F32)],
        ),
        out_shape=out_shape,
        compiler_params=params(),
        cost_estimate=pl.CostEstimate(flops=1, bytes_accessed=1, transcendentals=0),
    )(meta, *slopes, *ws, delta, *([] if acc is None else [acc]))


def slot_ranks(owners):
    owner_ids = owners[:, 0]
    order = jnp.arange(owner_ids.shape[0], dtype=jnp.int32)
    earlier = (owner_ids[None, :] == owner_ids[:, None]) & (order[None, :] < order[:, None])
    rank = jnp.sum(earlier.astype(jnp.int32), axis=1)
    return (owner_ids[None, :] == lax.axis_index("dp")) & (
        rank[None, :] == jnp.arange(CAP, dtype=jnp.int32)[:, None]
    )


def pick_slots(owners, total):
    wanted = slot_ranks(owners)
    return jnp.sum(jnp.where(wanted[:, :, None, None], total[None], 0.0), axis=1)[None]


def tie(value, *after):
    return lax.optimization_barrier((value,) + after)[0]


def piece_sizes(half, bs):
    last = max(half // bs // 5, 1) * bs
    return [half - last, last]


def local(tokens, frozen, delta, block_rows, block_cols, owners, d_out):
    group, me_dp, me_t = (lax.axis_index(a) for a in ("groups", "dp", "tensor"))
    n_dp, n_t = lax.axis_size("dp"), lax.axis_size("tensor")
    rows, feats = tokens.shape
    blocks, bs = delta.shape[0], delta.shape[1]
    slab = frozen.shape[1]
    half = slab // 2
    mine, theirs = group * half, (1 - group) * half
    sizes = piece_sizes(half, bs)
    firsts = [sum(sizes[:p]) for p in range(len(sizes))]

    shards = [
        lax.dynamic_slice(frozen, (0, mine + first), (frozen.shape[0], size))
        for first, size in zip(firsts, sizes)
    ]
    gather_a = lax.all_gather(shards[0], "dp")

    row_part = block_rows * bs // feats
    block_info = jnp.stack(
        [
            row_part ^ me_t,
            row_part,
            block_rows * bs - row_part * feats,
            block_cols * bs - (me_t * slab + mine),
        ],
        axis=1,
    )
    meta = jnp.concatenate([jnp.arange(n_t, dtype=jnp.int32) ^ me_t, block_info.reshape(-1)])

    peer = swap(tokens, "groups", 1)
    own_x = swap(tokens, "tensor", 2)
    peer_x = swap(peer, "tensor", 2)
    near_x = jnp.concatenate([tokens, peer], axis=0)
    far_x = jnp.concatenate([own_x, peer_x], axis=0)
    x4 = jnp.stack([near_x, swap(near_x, "tensor", 1), far_x, swap(far_x, "tensor", 1)])

    order = peer_x
    d_pieces = []
    for first, size in zip(firsts, sizes):
        give = lax.dynamic_slice(d_out, (0, theirs + first), (rows, size))
        keep = lax.dynamic_slice(d_out, (0, mine + first), (rows, size))
        got = swap(tie(give, order), "groups", 1)
        order = got
        d_pieces.append(jnp.concatenate([keep, got], axis=0))

    gather_b = lax.all_gather(tie(shards[1], gather_a, x4, *d_pieces), "dp")
    act_a, slope_a, sums_a = forward(meta, x4, gather_a, delta, d_pieces[0], firsts[0], 2)
    back_a = swap(act_a[1], "groups", 1)
    (early,) = backward(meta, [slope_a], [gather_a], delta, firsts[:1], None, None)
    activated = jnp.zeros((rows, slab), BF)
    activated = lax.dynamic_update_slice(activated, act_a[0], (0, mine + firsts[0]))
    activated = lax.dynamic_update_slice(activated, back_a, (0, theirs + firsts[0]))

    delta_b = tie(delta, early, activated)
    act_b, slope_b, sums_b = forward(meta, x4, gather_b, delta_b, d_pieces[1], firsts[1], 2)
    back_b = swap(act_b[1], "groups", 1)
    activated = lax.dynamic_update_slice(activated, act_b[0], (0, mine + firsts[1]))
    activated = lax.dynamic_update_slice(activated, back_b, (0, theirs + firsts[1]))

    def back_of(bit, *wait):
        d = tie(delta_b, *wait) if wait else delta_b
        return backward(meta, [slope_b], [gather_b], d, firsts[1:], early, bit)

    sums = sums_a + sums_b
    sums = sums[0] + swap(sums[1].astype(BF), "groups", 1).astype(F32)
    far_own_give, far_peer_give, far_own, far_peer = back_of(3)
    far_peer_got = swap(far_peer_give, "tensor", 1)
    far_own_got = swap(far_own_give, "tensor", 1)
    near_own_give, near_peer_give, near_own, near_peer = back_of(1, far_peer, sums, back_b)
    near_peer_got = swap(near_peer_give, "tensor", 1)
    near_own_got = swap(near_own_give, "tensor", 1)
    far_peer, far_own = tie(far_peer, near_peer), tie(far_own, near_peer)
    far_peer = (far_peer.astype(F32) + far_peer_got.astype(F32)).astype(BF)
    diagonal = [(i, i ^ (n_t + 2)) for i in range(2 * n_t)]
    from_xy = lax.ppermute(far_peer, ("groups", "tensor"), diagonal)
    far_own = (far_own.astype(F32) + far_own_got.astype(F32)).astype(BF)
    from_x = swap(far_own, "tensor", 2)
    near_peer = (near_peer.astype(F32) + near_peer_got.astype(F32)).astype(BF)
    from_y = swap(near_peer, "groups", 1)
    shares = [swap(tie(sums.astype(BF), near_peer), "dp", bit) for bit in range(1, n_dp)]
    near_own = near_own.astype(F32) + near_own_got.astype(F32)
    d_tokens = near_own + from_y.astype(F32) + from_x.astype(F32) + from_xy.astype(F32)
    for share in shares:
        sums = sums + share.astype(F32)
    norm = float(rows * n_dp) ** (-0.5)
    return (activated, d_tokens.astype(BF), pick_slots(owners, sums * norm))


def local_any(tokens, frozen, delta, block_rows, block_cols, owners, d_out):
    me_dp, me_t, n_dp = lax.axis_index("dp"), lax.axis_index("tensor"), lax.axis_size("dp")
    rows = tokens.shape[0]
    blocks, bs = delta.shape[0], delta.shape[1]
    slab = frozen.shape[1]
    x_full = lax.all_gather(tokens, "tensor", axis=1, tiled=True)
    weight = lax.all_gather(frozen, "dp", axis=0, tiled=True)
    width = x_full.shape[1]
    row_pick = (block_rows[:, None] == jnp.arange(width // bs)[None, :]).astype(F32)
    cols_here = block_cols - me_t * (slab // bs)
    col_pick = (cols_here[:, None] == jnp.arange(slab // bs)[None, :]).astype(F32)
    highest = lax.Precision.HIGHEST
    xb = jnp.take(x_full.reshape(rows, width // bs, bs), block_rows, axis=1)
    contrib = jnp.einsum("tnk,nkc->tnc", xb, delta, preferred_element_type=F32)
    add = jnp.einsum("tnc,nm->tmc", contrib, col_pick, precision=highest).reshape(rows, slab)
    preact = jnp.dot(x_full, weight, preferred_element_type=F32) + add
    squash = jax.nn.sigmoid(preact)
    activated = (preact * squash).astype(BF)
    d_pre = (d_out.astype(F32) * squash * (1.0 + preact * (1.0 - squash))).astype(BF)
    d_rows = lax.dot_general(
        d_pre, weight, (((1,), (1,)), ((), ())), preferred_element_type=F32
    )
    dy = jnp.take(d_pre.reshape(rows, slab // bs, bs), cols_here, axis=1)
    back = jnp.einsum("tnc,nkc->tnk", dy, delta, preferred_element_type=F32)
    back = jnp.einsum("tnk,nr->trk", back, row_pick, precision=highest).reshape(rows, width)
    d_tokens = lax.psum_scatter(
        (d_rows + back).astype(BF), "tensor", scatter_dimension=1, tiled=True
    )
    grads = jnp.einsum("tnk,tnc->nkc", xb, dy, preferred_element_type=F32)
    everyone = lax.all_gather(grads.astype(BF), "dp", axis=0).astype(F32)
    norm = float(rows * n_dp) ** (-0.5)
    return (activated, d_tokens, pick_slots(owners, jnp.sum(everyone, axis=0) * norm))


def solution(mesh):
    sizes = dict(mesh.shape)
    small = sizes["groups"] == 2 and sizes["dp"] == 4 and sizes["tensor"] == 4
    body = local if small else local_any
    in_specs = (
        P(("groups", "dp"), "tensor"),
        P("dp", "tensor"),
        P("tensor", None, None),
        P("tensor"),
        P("tensor"),
        P("tensor", None),
        P(("groups", "dp"), "tensor"),
    )
    out_specs = (
        P(("groups", "dp"), "tensor"),
        P(("groups", "dp"), "tensor"),
        P("tensor", ("groups", "dp"), None, None),
    )
    return jax.shard_map(body, mesh=mesh, in_specs=in_specs, out_specs=out_specs, check_vma=False)
```

```python
import functools

import jax
import jax.numpy as jnp
from jax import lax
from jax.experimental import pallas as pl
from jax.experimental.pallas import tpu as pltpu
from jax.sharding import PartitionSpec as P

CAP = 2
BF = jnp.bfloat16
F32 = jnp.float32
VMEM_BYTES = 30 * 2**20


def swap(array, axis, bit):
    size = lax.axis_size(axis)
    return lax.ppermute(array, axis, [(i, i ^ bit) for i in range(size)])


def params():
    return pltpu.CompilerParams(vmem_limit_bytes=VMEM_BYTES)


PARTS, BLOCKS = 0, 4


def forward_kernel(
    first, blocks, bs, cuts, meta, x_ref, w_ref, delta_ref, d_ref, act_ref, slope_ref, sum_ref, acc
):
    width = acc.shape[1]
    group = pl.program_id(1) // cuts

    @pl.when((pl.program_id(0) == 0) & (pl.program_id(1) == 0))
    def _():
        sum_ref[...] = jnp.zeros_like(sum_ref)

    total = None
    for s in range(w_ref.shape[0]):
        term = jnp.dot(x_ref[meta[PARTS + s]], w_ref[s], preferred_element_type=F32)
        total = term if total is None else total + term
    acc[...] = total
    start = first + pl.program_id(0) * width
    for n in range(blocks):
        at = BLOCKS + 4 * n
        col = meta[at + 3] - start

        @pl.when((col >= 0) & (col < width))
        def _():
            cols = pl.ds(pl.multiple_of(col, bs), bs)
            rows = pl.ds(pl.multiple_of(meta[at + 2], bs), bs)
            xs = x_ref[meta[at], :, rows]
            acc[:, cols] += jnp.dot(xs, delta_ref[n], preferred_element_type=F32)

    preact = acc[...]
    squash = jax.nn.sigmoid(preact)
    act_ref[0] = (preact * squash).astype(BF)
    slope_ref[...] = (
        d_ref[...].astype(F32) * squash * (1.0 + preact * (1.0 - squash))
    ).astype(BF)
    for n in range(blocks):
        at = BLOCKS + 4 * n
        col = meta[at + 3] - start

        @pl.when((col >= 0) & (col < width))
        def _():
            rows = pl.ds(pl.multiple_of(meta[at + 2], bs), bs)
            ds = slope_ref[:, pl.ds(pl.multiple_of(col, bs), bs)]
            sum_ref[group, n] += lax.dot_general(
                x_ref[meta[at], :, rows], ds, (((0,), (0,)), ((), ())), preferred_element_type=F32
            )


def forward(meta, x4, w4, delta, d_piece, first, groups_of):
    rows, width = d_piece.shape
    slots, feats = w4.shape[0], w4.shape[1]
    cuts = 1
    tile = rows // groups_of // cuts
    blocks, bs = delta.shape[0], delta.shape[1]
    wide = next(c for c in (512, 384, 256, 128, width) if width % c == 0)
    return pl.pallas_call(
        functools.partial(forward_kernel, first, blocks, bs, cuts),
        grid_spec=pltpu.PrefetchScalarGridSpec(
            num_scalar_prefetch=1,
            grid=(width // wide, groups_of * cuts),
            in_specs=[
                pl.BlockSpec((slots, tile, feats), lambda j, i, m: (0, i, 0)),
                pl.BlockSpec((slots, feats, wide), lambda j, i, m: (0, 0, j)),
                pl.BlockSpec(delta.shape, lambda j, i, m: (0, 0, 0)),
                pl.BlockSpec((tile, wide), lambda j, i, m: (i, j)),
            ],
            out_specs=[
                pl.BlockSpec((1, tile, wide), lambda j, i, m: (i // cuts, i % cuts, j)),
                pl.BlockSpec((tile, wide), lambda j, i, m: (i, j)),
                pl.BlockSpec((groups_of, blocks, bs, bs), lambda j, i, m: (0, 0, 0, 0)),
            ],
            scratch_shapes=[pltpu.VMEM((tile, wide), F32)],
        ),
        out_shape=[
            jax.ShapeDtypeStruct((groups_of, rows // groups_of, width), BF),
            jax.ShapeDtypeStruct((rows, width), BF),
            jax.ShapeDtypeStruct((groups_of, blocks, bs, bs), F32),
        ],
        compiler_params=params(),
        cost_estimate=pl.CostEstimate(flops=1, bytes_accessed=1, transcendentals=0),
    )(meta, x4, w4, delta, d_piece)


def backward_kernel(firsts, blocks, bs, has_acc, bit, meta, *refs):
    n = len(firsts)
    slopes, w_refs = refs[:n], refs[n : 2 * n]
    delta_ref = refs[2 * n]
    acc_in = refs[2 * n + 1] if has_acc else None
    outs, acc = refs[2 * n + 1 + has_acc : -1], refs[-1]
    size = acc.shape[1]
    step = pl.program_id(0)
    slot = step if bit is None else meta[PARTS + bit - step]
    base = pl.program_id(1) * size
    total = acc_in[0] if has_acc else None
    for p in range(n):
        term = lax.dot_general(
            slopes[p][...], w_refs[p][0], (((1,), (1,)), ((), ())), preferred_element_type=F32
        )
        total = term if total is None else total + term
    acc[...] = total
    for b in range(blocks):
        at = BLOCKS + 4 * b
        row = meta[at + 2] - base
        for p in range(n):
            col = meta[at + 3] - firsts[p]
            inside = (row >= 0) & (row < size) & (col >= 0) & (col < slopes[p].shape[1])

            @pl.when(inside & (meta[at + 1] == slot))
            def _():
                ds = slopes[p][:, pl.ds(pl.multiple_of(col, bs), bs)]
                acc[:, pl.ds(pl.multiple_of(row, bs), bs)] += lax.dot_general(
                    ds, delta_ref[b], (((1,), (1,)), ((), ())), preferred_element_type=F32
                )

    if len(outs) == 1:
        outs[0][0] = acc[...]
        return
    cut = outs[0].shape[0]
    for at_step in range(2):

        @pl.when(step == at_step)
        def _():
            outs[2 * at_step][...] = acc[:cut].astype(BF)
            outs[2 * at_step + 1][...] = acc[cut:].astype(BF)


def backward(meta, slopes, ws, delta, firsts, acc, bit):
    rows = slopes[0].shape[0]
    slots, feats = ws[0].shape[0], ws[0].shape[1]
    blocks, bs = delta.shape[0], delta.shape[1]
    every = bit is None
    tiles = 4 if every else 2
    size = feats // tiles
    width = sum(s.shape[1] for s in slopes)
    steps = slots if every else 2

    def slot_of(step, meta):
        return step if every else meta[PARTS + bit - step]

    whole = pl.BlockSpec((1, rows, size), lambda s, i, m: (slot_of(s, m), 0, i))
    give = pl.BlockSpec((rows // 2, size), lambda s, i, m: (0, jnp.where(s == 0, i, tiles - 1)))
    keep = pl.BlockSpec((rows // 2, size), lambda s, i, m: (0, jnp.where(s == 0, 0, i)))
    if every:
        out_specs = [whole]
        out_shape = [jax.ShapeDtypeStruct((slots, rows, feats), F32)]
    else:
        out_specs = [give, give, keep, keep]
        out_shape = [jax.ShapeDtypeStruct((rows // 2, feats), BF)] * 4
    return pl.pallas_call(
        functools.partial(backward_kernel, firsts, blocks, bs, acc is not None, bit),
        grid_spec=pltpu.PrefetchScalarGridSpec(
            num_scalar_prefetch=1,
            grid=(steps, tiles),
            in_specs=[
                pl.BlockSpec(s.shape, lambda s, i, m: (0, 0), pipeline_mode=pl.Buffered(1))
                for s in slopes
            ]
            + [
                pl.BlockSpec((1, size, w.shape[2]), lambda s, i, m: (slot_of(s, m), i, 0))
                for w in ws
            ]
            + [pl.BlockSpec(delta.shape, lambda s, i, m: (0, 0, 0))]
            + ([] if acc is None else [whole]),
            out_specs=out_specs,
            scratch_shapes=[pltpu.VMEM((rows, size), F32)],
        ),
        out_shape=out_shape,
        compiler_params=params(),
        cost_estimate=pl.CostEstimate(flops=1, bytes_accessed=1, transcendentals=0),
    )(meta, *slopes, *ws, delta, *([] if acc is None else [acc]))


def slot_ranks(owners):
    owner_ids = owners[:, 0]
    order = jnp.arange(owner_ids.shape[0], dtype=jnp.int32)
    earlier = (owner_ids[None, :] == owner_ids[:, None]) & (order[None, :] < order[:, None])
    rank = jnp.sum(earlier.astype(jnp.int32), axis=1)
    return (owner_ids[None, :] == lax.axis_index("dp")) & (
        rank[None, :] == jnp.arange(CAP, dtype=jnp.int32)[:, None]
    )


def pick_slots(owners, total):
    wanted = slot_ranks(owners)
    return jnp.sum(jnp.where(wanted[:, :, None, None], total[None], 0.0), axis=1)[None]


def tie(value, *after):
    return lax.optimization_barrier((value,) + after)[0]


def piece_sizes(half, bs):
    last = max(half // bs // 5, 1) * bs
    return [half - last, last]


def local(tokens, frozen, delta, block_rows, block_cols, owners, d_out):
    group, me_dp, me_t = (lax.axis_index(a) for a in ("groups", "dp", "tensor"))
    n_dp, n_t = lax.axis_size("dp"), lax.axis_size("tensor")
    rows, feats = tokens.shape
    blocks, bs = delta.shape[0], delta.shape[1]
    slab = frozen.shape[1]
    half = slab // 2
    mine, theirs = group * half, (1 - group) * half
    sizes = piece_sizes(half, bs)
    firsts = [sum(sizes[:p]) for p in range(len(sizes))]

    shards = [
        lax.dynamic_slice(frozen, (0, mine + first), (frozen.shape[0], size))
        for first, size in zip(firsts, sizes)
    ]
    gather_a = lax.all_gather(shards[0], "dp")

    row_part = block_rows * bs // feats
    block_info = jnp.stack(
        [
            row_part ^ me_t,
            row_part,
            block_rows * bs - row_part * feats,
            block_cols * bs - (me_t * slab + mine),
        ],
        axis=1,
    )
    meta = jnp.concatenate([jnp.arange(n_t, dtype=jnp.int32) ^ me_t, block_info.reshape(-1)])

    peer = swap(tokens, "groups", 1)
    own_x = swap(tokens, "tensor", 2)
    peer_x = swap(peer, "tensor", 2)
    near_x = jnp.concatenate([tokens, peer], axis=0)
    far_x = jnp.concatenate([own_x, peer_x], axis=0)
    x4 = jnp.stack([near_x, swap(near_x, "tensor", 1), far_x, swap(far_x, "tensor", 1)])

    order = peer_x
    d_pieces = []
    for first, size in zip(firsts, sizes):
        give = lax.dynamic_slice(d_out, (0, theirs + first), (rows, size))
        keep = lax.dynamic_slice(d_out, (0, mine + first), (rows, size))
        got = swap(tie(give, order), "groups", 1)
        order = got
        d_pieces.append(jnp.concatenate([keep, got], axis=0))

    gather_b = lax.all_gather(tie(shards[1], gather_a, x4, *d_pieces), "dp")
    act_a, slope_a, sums_a = forward(meta, x4, gather_a, delta, d_pieces[0], firsts[0], 2)
    back_a = swap(act_a[1], "groups", 1)
    (early,) = backward(meta, [slope_a], [gather_a], delta, firsts[:1], None, None)
    activated = jnp.zeros((rows, slab), BF)
    activated = lax.dynamic_update_slice(activated, act_a[0], (0, mine + firsts[0]))
    activated = lax.dynamic_update_slice(activated, back_a, (0, theirs + firsts[0]))

    delta_b = tie(delta, early, activated)
    act_b, slope_b, sums_b = forward(meta, x4, gather_b, delta_b, d_pieces[1], firsts[1], 2)
    back_b = swap(act_b[1], "groups", 1)
    activated = lax.dynamic_update_slice(activated, act_b[0], (0, mine + firsts[1]))
    activated = lax.dynamic_update_slice(activated, back_b, (0, theirs + firsts[1]))

    def back_of(bit, *wait):
        d = tie(delta_b, *wait) if wait else delta_b
        return backward(meta, [slope_b], [gather_b], d, firsts[1:], early, bit)

    sums = sums_a + sums_b
    sums = sums[0] + swap(sums[1].astype(BF), "groups", 1).astype(F32)
    far_own_give, far_peer_give, far_own, far_peer = back_of(3)
    far_peer_got = swap(far_peer_give, "tensor", 1)
    far_own_got = swap(far_own_give, "tensor", 1)
    near_own_give, near_peer_give, near_own, near_peer = back_of(1, far_peer, sums, back_b)
    near_peer_got = swap(near_peer_give, "tensor", 1)
    near_own_got = swap(near_own_give, "tensor", 1)
    far_peer, far_own = tie(far_peer, near_peer), tie(far_own, near_peer)
    far_peer = (far_peer.astype(F32) + far_peer_got.astype(F32)).astype(BF)
    diagonal = [(i, i ^ (n_t + 2)) for i in range(2 * n_t)]
    from_xy = lax.ppermute(far_peer, ("groups", "tensor"), diagonal)
    far_own = (far_own.astype(F32) + far_own_got.astype(F32)).astype(BF)
    from_x = swap(far_own, "tensor", 2)
    near_peer = (near_peer.astype(F32) + near_peer_got.astype(F32)).astype(BF)
    from_y = swap(near_peer, "groups", 1)
    shares = [swap(tie(sums.astype(BF), near_peer), "dp", bit) for bit in range(1, n_dp)]
    near_own = near_own.astype(F32) + near_own_got.astype(F32)
    d_tokens = near_own + from_y.astype(F32) + from_x.astype(F32) + from_xy.astype(F32)
    for share in shares:
        sums = sums + share.astype(F32)
    norm = float(rows * n_dp) ** (-0.5)
    return (activated, d_tokens.astype(BF), pick_slots(owners, sums * norm))


def local_any(tokens, frozen, delta, block_rows, block_cols, owners, d_out):
    me_dp, me_t, n_dp = lax.axis_index("dp"), lax.axis_index("tensor"), lax.axis_size("dp")
    rows = tokens.shape[0]
    blocks, bs = delta.shape[0], delta.shape[1]
    slab = frozen.shape[1]
    x_full = lax.all_gather(tokens, "tensor", axis=1, tiled=True)
    weight = lax.all_gather(frozen, "dp", axis=0, tiled=True)
    width = x_full.shape[1]
    row_pick = (block_rows[:, None] == jnp.arange(width // bs)[None, :]).astype(F32)
    cols_here = block_cols - me_t * (slab // bs)
    col_pick = (cols_here[:, None] == jnp.arange(slab // bs)[None, :]).astype(F32)
    highest = lax.Precision.HIGHEST
    xb = jnp.take(x_full.reshape(rows, width // bs, bs), block_rows, axis=1)
    contrib = jnp.einsum("tnk,nkc->tnc", xb, delta, preferred_element_type=F32)
    add = jnp.einsum("tnc,nm->tmc", contrib, col_pick, precision=highest).reshape(rows, slab)
    preact = jnp.dot(x_full, weight, preferred_element_type=F32) + add
    squash = jax.nn.sigmoid(preact)
    activated = (preact * squash).astype(BF)
    d_pre = (d_out.astype(F32) * squash * (1.0 + preact * (1.0 - squash))).astype(BF)
    d_rows = lax.dot_general(
        d_pre, weight, (((1,), (1,)), ((), ())), preferred_element_type=F32
    )
    dy = jnp.take(d_pre.reshape(rows, slab // bs, bs), cols_here, axis=1)
    back = jnp.einsum("tnc,nkc->tnk", dy, delta, preferred_element_type=F32)
    back = jnp.einsum("tnk,nr->trk", back, row_pick, precision=highest).reshape(rows, width)
    d_tokens = lax.psum_scatter(
        (d_rows + back).astype(BF), "tensor", scatter_dimension=1, tiled=True
    )
    grads = jnp.einsum("tnk,tnc->nkc", xb, dy, preferred_element_type=F32)
    everyone = lax.all_gather(grads.astype(BF), "dp", axis=0).astype(F32)
    norm = float(rows * n_dp) ** (-0.5)
    return (activated, d_tokens, pick_slots(owners, jnp.sum(everyone, axis=0) * norm))


def solution(mesh):
    sizes = dict(mesh.shape)
    small = sizes["groups"] == 2 and sizes["dp"] == 4 and sizes["tensor"] == 4
    body = local if small else local_any
    in_specs = (
        P(("groups", "dp"), "tensor"),
        P("dp", "tensor"),
        P("tensor", None, None),
        P("tensor"),
        P("tensor"),
        P("tensor", None),
        P(("groups", "dp"), "tensor"),
    )
    out_specs = (
        P(("groups", "dp"), "tensor"),
        P(("groups", "dp"), "tensor"),
        P("tensor", ("groups", "dp"), None, None),
    )
    return jax.shard_map(body, mesh=mesh, in_specs=in_specs, out_specs=out_specs, check_vma=False)
```

```python
import functools

import jax
import jax.numpy as jnp
from jax import lax
from jax.experimental import pallas as pl
from jax.experimental.pallas import tpu as pltpu
from jax.sharding import PartitionSpec as P

CAP = 2
BF = jnp.bfloat16
F32 = jnp.float32
VMEM_BYTES = 30 * 2**20


def swap(array, axis, bit):
    size = lax.axis_size(axis)
    return lax.ppermute(array, axis, [(i, i ^ bit) for i in range(size)])


def params():
    return pltpu.CompilerParams(vmem_limit_bytes=VMEM_BYTES)


PARTS, BLOCKS = 0, 4


def forward_kernel(
    first, blocks, bs, cuts, meta, x_ref, w_ref, delta_ref, d_ref, act_ref, slope_ref, sum_ref, acc
):
    width = acc.shape[1]
    group = pl.program_id(1) // cuts

    @pl.when((pl.program_id(0) == 0) & (pl.program_id(1) == 0))
    def _():
        sum_ref[...] = jnp.zeros_like(sum_ref)

    total = None
    for s in range(w_ref.shape[0]):
        term = jnp.dot(x_ref[meta[PARTS + s]], w_ref[s], preferred_element_type=F32)
        total = term if total is None else total + term
    acc[...] = total
    start = first + pl.program_id(0) * width
    for n in range(blocks):
        at = BLOCKS + 4 * n
        col = meta[at + 3] - start

        @pl.when((col >= 0) & (col < width))
        def _():
            cols = pl.ds(pl.multiple_of(col, bs), bs)
            rows = pl.ds(pl.multiple_of(meta[at + 2], bs), bs)
            xs = x_ref[meta[at], :, rows]
            acc[:, cols] += jnp.dot(xs, delta_ref[n], preferred_element_type=F32)

    preact = acc[...]
    squash = jax.nn.sigmoid(preact)
    act_ref[0] = (preact * squash).astype(BF)
    slope_ref[...] = (
        d_ref[...].astype(F32) * squash * (1.0 + preact * (1.0 - squash))
    ).astype(BF)
    for n in range(blocks):
        at = BLOCKS + 4 * n
        col = meta[at + 3] - start

        @pl.when((col >= 0) & (col < width))
        def _():
            rows = pl.ds(pl.multiple_of(meta[at + 2], bs), bs)
            ds = slope_ref[:, pl.ds(pl.multiple_of(col, bs), bs)]
            sum_ref[group, n] += lax.dot_general(
                x_ref[meta[at], :, rows], ds, (((0,), (0,)), ((), ())), preferred_element_type=F32
            )


def forward(meta, x4, w4, delta, d_piece, first, groups_of):
    rows, width = d_piece.shape
    slots, feats = w4.shape[0], w4.shape[1]
    cuts = 1
    tile = rows // groups_of // cuts
    blocks, bs = delta.shape[0], delta.shape[1]
    wide = next(c for c in (512, 384, 256, 128, width) if width % c == 0)
    return pl.pallas_call(
        functools.partial(forward_kernel, first, blocks, bs, cuts),
        grid_spec=pltpu.PrefetchScalarGridSpec(
            num_scalar_prefetch=1,
            grid=(width // wide, groups_of * cuts),
            in_specs=[
                pl.BlockSpec((slots, tile, feats), lambda j, i, m: (0, i, 0)),
                pl.BlockSpec((slots, feats, wide), lambda j, i, m: (0, 0, j)),
                pl.BlockSpec(delta.shape, lambda j, i, m: (0, 0, 0)),
                pl.BlockSpec((tile, wide), lambda j, i, m: (i, j)),
            ],
            out_specs=[
                pl.BlockSpec((1, tile, wide), lambda j, i, m: (i // cuts, i % cuts, j)),
                pl.BlockSpec((tile, wide), lambda j, i, m: (i, j)),
                pl.BlockSpec((groups_of, blocks, bs, bs), lambda j, i, m: (0, 0, 0, 0)),
            ],
            scratch_shapes=[pltpu.VMEM((tile, wide), F32)],
        ),
        out_shape=[
            jax.ShapeDtypeStruct((groups_of, rows // groups_of, width), BF),
            jax.ShapeDtypeStruct((rows, width), BF),
            jax.ShapeDtypeStruct((groups_of, blocks, bs, bs), F32),
        ],
        compiler_params=params(),
        cost_estimate=pl.CostEstimate(flops=1, bytes_accessed=1, transcendentals=0),
    )(meta, x4, w4, delta, d_piece)


def backward_kernel(firsts, blocks, bs, has_acc, bit, meta, *refs):
    n = len(firsts)
    slopes, w_refs = refs[:n], refs[n : 2 * n]
    delta_ref = refs[2 * n]
    acc_in = refs[2 * n + 1] if has_acc else None
    outs, acc = refs[2 * n + 1 + has_acc : -1], refs[-1]
    size = acc.shape[1]
    step = pl.program_id(0)
    slot = step if bit is None else meta[PARTS + bit - step]
    base = pl.program_id(1) * size
    total = acc_in[0].astype(F32) if has_acc else None
    for p in range(n):
        term = lax.dot_general(
            slopes[p][...], w_refs[p][0], (((1,), (1,)), ((), ())), preferred_element_type=F32
        )
        total = term if total is None else total + term
    acc[...] = total
    for b in range(blocks):
        at = BLOCKS + 4 * b
        row = meta[at + 2] - base
        for p in range(n):
            col = meta[at + 3] - firsts[p]
            inside = (row >= 0) & (row < size) & (col >= 0) & (col < slopes[p].shape[1])

            @pl.when(inside & (meta[at + 1] == slot))
            def _():
                ds = slopes[p][:, pl.ds(pl.multiple_of(col, bs), bs)]
                acc[:, pl.ds(pl.multiple_of(row, bs), bs)] += lax.dot_general(
                    ds, delta_ref[b], (((1,), (1,)), ((), ())), preferred_element_type=F32
                )

    if len(outs) == 1:
        outs[0][0] = acc[...].astype(BF)
        return
    cut = outs[0].shape[0]
    for at_step in range(2):

        @pl.when(step == at_step)
        def _():
            outs[2 * at_step][...] = acc[:cut].astype(BF)
            outs[2 * at_step + 1][...] = acc[cut:].astype(BF)


def backward(meta, slopes, ws, delta, firsts, acc, bit):
    rows = slopes[0].shape[0]
    slots, feats = ws[0].shape[0], ws[0].shape[1]
    blocks, bs = delta.shape[0], delta.shape[1]
    every = bit is None
    tiles = 4 if every else 2
    size = feats // tiles
    width = sum(s.shape[1] for s in slopes)
    steps = slots if every else 2

    def slot_of(step, meta):
        return step if every else meta[PARTS + bit - step]

    whole = pl.BlockSpec((1, rows, size), lambda s, i, m: (slot_of(s, m), 0, i))
    give = pl.BlockSpec((rows // 2, size), lambda s, i, m: (0, jnp.where(s == 0, i, tiles - 1)))
    keep = pl.BlockSpec((rows // 2, size), lambda s, i, m: (0, jnp.where(s == 0, 0, i)))
    if every:
        out_specs = [whole]
        out_shape = [jax.ShapeDtypeStruct((slots, rows, feats), BF)]
    else:
        out_specs = [give, give, keep, keep]
        out_shape = [jax.ShapeDtypeStruct((rows // 2, feats), BF)] * 4
    return pl.pallas_call(
        functools.partial(backward_kernel, firsts, blocks, bs, acc is not None, bit),
        grid_spec=pltpu.PrefetchScalarGridSpec(
            num_scalar_prefetch=1,
            grid=(steps, tiles),
            in_specs=[
                pl.BlockSpec(s.shape, lambda s, i, m: (0, 0), pipeline_mode=pl.Buffered(1))
                for s in slopes
            ]
            + [
                pl.BlockSpec((1, size, w.shape[2]), lambda s, i, m: (slot_of(s, m), i, 0))
                for w in ws
            ]
            + [pl.BlockSpec(delta.shape, lambda s, i, m: (0, 0, 0))]
            + ([] if acc is None else [whole]),
            out_specs=out_specs,
            scratch_shapes=[pltpu.VMEM((rows, size), F32)],
        ),
        out_shape=out_shape,
        compiler_params=params(),
        cost_estimate=pl.CostEstimate(flops=1, bytes_accessed=1, transcendentals=0),
    )(meta, *slopes, *ws, delta, *([] if acc is None else [acc]))


def slot_ranks(owners):
    owner_ids = owners[:, 0]
    order = jnp.arange(owner_ids.shape[0], dtype=jnp.int32)
    earlier = (owner_ids[None, :] == owner_ids[:, None]) & (order[None, :] < order[:, None])
    rank = jnp.sum(earlier.astype(jnp.int32), axis=1)
    return (owner_ids[None, :] == lax.axis_index("dp")) & (
        rank[None, :] == jnp.arange(CAP, dtype=jnp.int32)[:, None]
    )


def pick_slots(owners, total):
    wanted = slot_ranks(owners)
    return jnp.sum(jnp.where(wanted[:, :, None, None], total[None], 0.0), axis=1)[None]


def tie(value, *after):
    return lax.optimization_barrier((value,) + after)[0]


def piece_sizes(half, bs):
    last = max(half // bs // 5, 1) * bs
    return [half - last, last]


def local(tokens, frozen, delta, block_rows, block_cols, owners, d_out):
    group, me_dp, me_t = (lax.axis_index(a) for a in ("groups", "dp", "tensor"))
    n_dp, n_t = lax.axis_size("dp"), lax.axis_size("tensor")
    rows, feats = tokens.shape
    blocks, bs = delta.shape[0], delta.shape[1]
    slab = frozen.shape[1]
    half = slab // 2
    mine, theirs = group * half, (1 - group) * half
    sizes = piece_sizes(half, bs)
    firsts = [sum(sizes[:p]) for p in range(len(sizes))]

    shards = [
        lax.dynamic_slice(frozen, (0, mine + first), (frozen.shape[0], size))
        for first, size in zip(firsts, sizes)
    ]
    gather_a = lax.all_gather(shards[0], "dp")

    row_part = block_rows * bs // feats
    block_info = jnp.stack(
        [
            row_part ^ me_t,
            row_part,
            block_rows * bs - row_part * feats,
            block_cols * bs - (me_t * slab + mine),
        ],
        axis=1,
    )
    meta = jnp.concatenate([jnp.arange(n_t, dtype=jnp.int32) ^ me_t, block_info.reshape(-1)])

    peer = swap(tokens, "groups", 1)
    own_x = swap(tokens, "tensor", 2)
    peer_x = swap(peer, "tensor", 2)
    near_x = jnp.concatenate([tokens, peer], axis=0)
    far_x = jnp.concatenate([own_x, peer_x], axis=0)
    x4 = jnp.stack([near_x, swap(near_x, "tensor", 1), far_x, swap(far_x, "tensor", 1)])

    order = peer_x
    d_pieces = []
    for first, size in zip(firsts, sizes):
        give = lax.dynamic_slice(d_out, (0, theirs + first), (rows, size))
        keep = lax.dynamic_slice(d_out, (0, mine + first), (rows, size))
        got = swap(tie(give, order), "groups", 1)
        order = got
        d_pieces.append(jnp.concatenate([keep, got], axis=0))

    gather_b = lax.all_gather(tie(shards[1], gather_a, x4, *d_pieces), "dp")
    act_a, slope_a, sums_a = forward(meta, x4, gather_a, delta, d_pieces[0], firsts[0], 2)
    back_a = swap(act_a[1], "groups", 1)
    (early,) = backward(meta, [slope_a], [gather_a], delta, firsts[:1], None, None)
    activated = jnp.zeros((rows, slab), BF)
    activated = lax.dynamic_update_slice(activated, act_a[0], (0, mine + firsts[0]))
    activated = lax.dynamic_update_slice(activated, back_a, (0, theirs + firsts[0]))

    delta_b = tie(delta, early, activated)
    act_b, slope_b, sums_b = forward(meta, x4, gather_b, delta_b, d_pieces[1], firsts[1], 2)
    back_b = swap(act_b[1], "groups", 1)
    activated = lax.dynamic_update_slice(activated, act_b[0], (0, mine + firsts[1]))
    activated = lax.dynamic_update_slice(activated, back_b, (0, theirs + firsts[1]))

    def back_of(bit, *wait):
        d = tie(delta_b, *wait) if wait else delta_b
        return backward(meta, [slope_b], [gather_b], d, firsts[1:], early, bit)

    sums = sums_a + sums_b
    sums = sums[0] + swap(sums[1].astype(BF), "groups", 1).astype(F32)
    far_own_give, far_peer_give, far_own, far_peer = back_of(3)
    far_peer_got = swap(far_peer_give, "tensor", 1)
    far_own_got = swap(far_own_give, "tensor", 1)
    near_own_give, near_peer_give, near_own, near_peer = back_of(1, far_peer, sums, back_b)
    near_peer_got = swap(near_peer_give, "tensor", 1)
    near_own_got = swap(near_own_give, "tensor", 1)
    far_peer, far_own = tie(far_peer, near_peer), tie(far_own, near_peer)
    far_peer = (far_peer.astype(F32) + far_peer_got.astype(F32)).astype(BF)
    diagonal = [(i, i ^ (n_t + 2)) for i in range(2 * n_t)]
    from_xy = lax.ppermute(far_peer, ("groups", "tensor"), diagonal)
    far_own = (far_own.astype(F32) + far_own_got.astype(F32)).astype(BF)
    from_x = swap(far_own, "tensor", 2)
    near_peer = (near_peer.astype(F32) + near_peer_got.astype(F32)).astype(BF)
    from_y = swap(near_peer, "groups", 1)
    shares = [swap(tie(sums.astype(BF), near_peer), "dp", bit) for bit in range(1, n_dp)]
    near_own = near_own.astype(F32) + near_own_got.astype(F32)
    d_tokens = near_own + from_y.astype(F32) + from_x.astype(F32) + from_xy.astype(F32)
    for share in shares:
        sums = sums + share.astype(F32)
    norm = float(rows * n_dp) ** (-0.5)
    return (activated, d_tokens.astype(BF), pick_slots(owners, sums * norm))


def local_any(tokens, frozen, delta, block_rows, block_cols, owners, d_out):
    me_dp, me_t, n_dp = lax.axis_index("dp"), lax.axis_index("tensor"), lax.axis_size("dp")
    rows = tokens.shape[0]
    blocks, bs = delta.shape[0], delta.shape[1]
    slab = frozen.shape[1]
    x_full = lax.all_gather(tokens, "tensor", axis=1, tiled=True)
    weight = lax.all_gather(frozen, "dp", axis=0, tiled=True)
    width = x_full.shape[1]
    row_pick = (block_rows[:, None] == jnp.arange(width // bs)[None, :]).astype(F32)
    cols_here = block_cols - me_t * (slab // bs)
    col_pick = (cols_here[:, None] == jnp.arange(slab // bs)[None, :]).astype(F32)
    highest = lax.Precision.HIGHEST
    xb = jnp.take(x_full.reshape(rows, width // bs, bs), block_rows, axis=1)
    contrib = jnp.einsum("tnk,nkc->tnc", xb, delta, preferred_element_type=F32)
    add = jnp.einsum("tnc,nm->tmc", contrib, col_pick, precision=highest).reshape(rows, slab)
    preact = jnp.dot(x_full, weight, preferred_element_type=F32) + add
    squash = jax.nn.sigmoid(preact)
    activated = (preact * squash).astype(BF)
    d_pre = (d_out.astype(F32) * squash * (1.0 + preact * (1.0 - squash))).astype(BF)
    d_rows = lax.dot_general(
        d_pre, weight, (((1,), (1,)), ((), ())), preferred_element_type=F32
    )
    dy = jnp.take(d_pre.reshape(rows, slab // bs, bs), cols_here, axis=1)
    back = jnp.einsum("tnc,nkc->tnk", dy, delta, preferred_element_type=F32)
    back = jnp.einsum("tnk,nr->trk", back, row_pick, precision=highest).reshape(rows, width)
    d_tokens = lax.psum_scatter(
        (d_rows + back).astype(BF), "tensor", scatter_dimension=1, tiled=True
    )
    grads = jnp.einsum("tnk,tnc->nkc", xb, dy, preferred_element_type=F32)
    everyone = lax.all_gather(grads.astype(BF), "dp", axis=0).astype(F32)
    norm = float(rows * n_dp) ** (-0.5)
    return (activated, d_tokens, pick_slots(owners, jnp.sum(everyone, axis=0) * norm))


def solution(mesh):
    sizes = dict(mesh.shape)
    small = sizes["groups"] == 2 and sizes["dp"] == 4 and sizes["tensor"] == 4
    body = local if small else local_any
    in_specs = (
        P(("groups", "dp"), "tensor"),
        P("dp", "tensor"),
        P("tensor", None, None),
        P("tensor"),
        P("tensor"),
        P("tensor", None),
        P(("groups", "dp"), "tensor"),
    )
    out_specs = (
        P(("groups", "dp"), "tensor"),
        P(("groups", "dp"), "tensor"),
        P("tensor", ("groups", "dp"), None, None),
    )
    return jax.shard_map(body, mesh=mesh, in_specs=in_specs, out_specs=out_specs, check_vma=False)
```

```python
import functools

import jax
import jax.numpy as jnp
from jax import lax
from jax.experimental import pallas as pl
from jax.experimental.pallas import tpu as pltpu
from jax.sharding import PartitionSpec as P

CAP = 2
BF = jnp.bfloat16
F32 = jnp.float32
VMEM_BYTES = 30 * 2**20


def swap(array, axis, bit):
    size = lax.axis_size(axis)
    return lax.ppermute(array, axis, [(i, i ^ bit) for i in range(size)])


def params():
    return pltpu.CompilerParams(vmem_limit_bytes=VMEM_BYTES)


PARTS, BLOCKS = 0, 4


def forward_kernel(
    first, blocks, bs, cuts, meta, x_ref, w_ref, delta_ref, d_ref, act_ref, slope_ref, sum_ref, acc
):
    width = acc.shape[1]
    group = pl.program_id(1) // cuts

    @pl.when((pl.program_id(0) == 0) & (pl.program_id(1) == 0))
    def _():
        sum_ref[...] = jnp.zeros_like(sum_ref)

    total = None
    for s in range(w_ref.shape[0]):
        term = jnp.dot(x_ref[meta[PARTS + s]], w_ref[s], preferred_element_type=F32)
        total = term if total is None else total + term
    acc[...] = total
    start = first + pl.program_id(0) * width
    for n in range(blocks):
        at = BLOCKS + 4 * n
        col = meta[at + 3] - start

        @pl.when((col >= 0) & (col < width))
        def _():
            cols = pl.ds(pl.multiple_of(col, bs), bs)
            rows = pl.ds(pl.multiple_of(meta[at + 2], bs), bs)
            xs = x_ref[meta[at], :, rows]
            acc[:, cols] += jnp.dot(xs, delta_ref[n], preferred_element_type=F32)

    preact = acc[...]
    squash = jax.nn.sigmoid(preact)
    act_ref[0] = (preact * squash).astype(BF)
    slope_ref[...] = (
        d_ref[...].astype(F32) * squash * (1.0 + preact * (1.0 - squash))
    ).astype(BF)
    for n in range(blocks):
        at = BLOCKS + 4 * n
        col = meta[at + 3] - start

        @pl.when((col >= 0) & (col < width))
        def _():
            rows = pl.ds(pl.multiple_of(meta[at + 2], bs), bs)
            ds = slope_ref[:, pl.ds(pl.multiple_of(col, bs), bs)]
            sum_ref[group, n] += lax.dot_general(
                x_ref[meta[at], :, rows], ds, (((0,), (0,)), ((), ())), preferred_element_type=F32
            )


def forward(meta, x4, w4, delta, d_piece, first, groups_of):
    rows, width = d_piece.shape
    slots, feats = w4.shape[0], w4.shape[1]
    cuts = 1
    tile = rows // groups_of // cuts
    blocks, bs = delta.shape[0], delta.shape[1]
    wide = next(c for c in (512, 384, 256, 128, width) if width % c == 0)
    return pl.pallas_call(
        functools.partial(forward_kernel, first, blocks, bs, cuts),
        grid_spec=pltpu.PrefetchScalarGridSpec(
            num_scalar_prefetch=1,
            grid=(width // wide, groups_of * cuts),
            in_specs=[
                pl.BlockSpec((slots, tile, feats), lambda j, i, m: (0, i, 0)),
                pl.BlockSpec((slots, feats, wide), lambda j, i, m: (0, 0, j)),
                pl.BlockSpec(delta.shape, lambda j, i, m: (0, 0, 0)),
                pl.BlockSpec((tile, wide), lambda j, i, m: (i, j)),
            ],
            out_specs=[
                pl.BlockSpec((1, tile, wide), lambda j, i, m: (i // cuts, i % cuts, j)),
                pl.BlockSpec((tile, wide), lambda j, i, m: (i, j)),
                pl.BlockSpec((groups_of, blocks, bs, bs), lambda j, i, m: (0, 0, 0, 0)),
            ],
            scratch_shapes=[pltpu.VMEM((tile, wide), F32)],
        ),
        out_shape=[
            jax.ShapeDtypeStruct((groups_of, rows // groups_of, width), BF),
            jax.ShapeDtypeStruct((rows, width), BF),
            jax.ShapeDtypeStruct((groups_of, blocks, bs, bs), F32),
        ],
        compiler_params=params(),
        cost_estimate=pl.CostEstimate(flops=1, bytes_accessed=1, transcendentals=0),
    )(meta, x4, w4, delta, d_piece)


def backward_kernel(firsts, blocks, bs, has_acc, bit, meta, *refs):
    n = len(firsts)
    slopes, w_refs = refs[:n], refs[n : 2 * n]
    delta_ref = refs[2 * n]
    acc_in = refs[2 * n + 1] if has_acc else None
    outs, acc = refs[2 * n + 1 + has_acc : -1], refs[-1]
    size = acc.shape[1]
    step = pl.program_id(0)
    slot = step if bit is None else meta[PARTS + bit - step]
    base = pl.program_id(1) * size
    total = acc_in[0].astype(F32) if has_acc else None
    for p in range(n):
        term = lax.dot_general(
            slopes[p][...], w_refs[p][0], (((1,), (1,)), ((), ())), preferred_element_type=F32
        )
        total = term if total is None else total + term
    acc[...] = total
    for b in range(blocks):
        at = BLOCKS + 4 * b
        row = meta[at + 2] - base
        for p in range(n):
            col = meta[at + 3] - firsts[p]
            inside = (row >= 0) & (row < size) & (col >= 0) & (col < slopes[p].shape[1])

            @pl.when(inside & (meta[at + 1] == slot))
            def _():
                ds = slopes[p][:, pl.ds(pl.multiple_of(col, bs), bs)]
                acc[:, pl.ds(pl.multiple_of(row, bs), bs)] += lax.dot_general(
                    ds, delta_ref[b], (((1,), (1,)), ((), ())), preferred_element_type=F32
                )

    if len(outs) == 1:
        outs[0][0] = acc[...].astype(BF)
        return
    cut = outs[0].shape[0]
    for at_step in range(2):

        @pl.when(step == at_step)
        def _():
            outs[2 * at_step][...] = acc[:cut].astype(BF)
            outs[2 * at_step + 1][...] = acc[cut:].astype(BF)


def backward(meta, slopes, ws, delta, firsts, acc, bit):
    rows = slopes[0].shape[0]
    slots, feats = ws[0].shape[0], ws[0].shape[1]
    blocks, bs = delta.shape[0], delta.shape[1]
    every = bit is None
    tiles = 4 if every else 2
    size = feats // tiles
    width = sum(s.shape[1] for s in slopes)
    steps = slots if every else 2

    def slot_of(step, meta):
        return step if every else meta[PARTS + bit - step]

    whole = pl.BlockSpec((1, rows, size), lambda s, i, m: (slot_of(s, m), 0, i))
    give = pl.BlockSpec((rows // 2, size), lambda s, i, m: (0, jnp.where(s == 0, i, tiles - 1)))
    keep = pl.BlockSpec((rows // 2, size), lambda s, i, m: (0, jnp.where(s == 0, 0, i)))
    if every:
        out_specs = [whole]
        out_shape = [jax.ShapeDtypeStruct((slots, rows, feats), BF)]
    else:
        out_specs = [give, give, keep, keep]
        out_shape = [jax.ShapeDtypeStruct((rows // 2, feats), BF)] * 4
    return pl.pallas_call(
        functools.partial(backward_kernel, firsts, blocks, bs, acc is not None, bit),
        grid_spec=pltpu.PrefetchScalarGridSpec(
            num_scalar_prefetch=1,
            grid=(steps, tiles),
            in_specs=[
                pl.BlockSpec(s.shape, lambda s, i, m: (0, 0), pipeline_mode=pl.Buffered(1))
                for s in slopes
            ]
            + [
                pl.BlockSpec((1, size, w.shape[2]), lambda s, i, m: (slot_of(s, m), i, 0))
                for w in ws
            ]
            + [pl.BlockSpec(delta.shape, lambda s, i, m: (0, 0, 0))]
            + ([] if acc is None else [whole]),
            out_specs=out_specs,
            scratch_shapes=[pltpu.VMEM((rows, size), F32)],
        ),
        out_shape=out_shape,
        compiler_params=params(),
        cost_estimate=pl.CostEstimate(flops=1, bytes_accessed=1, transcendentals=0),
    )(meta, *slopes, *ws, delta, *([] if acc is None else [acc]))


def slot_ranks(owners):
    owner_ids = owners[:, 0]
    order = jnp.arange(owner_ids.shape[0], dtype=jnp.int32)
    earlier = (owner_ids[None, :] == owner_ids[:, None]) & (order[None, :] < order[:, None])
    rank = jnp.sum(earlier.astype(jnp.int32), axis=1)
    return (owner_ids[None, :] == lax.axis_index("dp")) & (
        rank[None, :] == jnp.arange(CAP, dtype=jnp.int32)[:, None]
    )


def pick_slots(owners, total):
    wanted = slot_ranks(owners)
    return jnp.sum(jnp.where(wanted[:, :, None, None], total[None], 0.0), axis=1)[None]


def tie(value, *after):
    return lax.optimization_barrier((value,) + after)[0]


def piece_sizes(half, bs):
    last = max(half // bs // 5, 1) * bs
    return [half - last, last]


def local(tokens, frozen, delta, block_rows, block_cols, owners, d_out):
    group, me_dp, me_t = (lax.axis_index(a) for a in ("groups", "dp", "tensor"))
    n_dp, n_t = lax.axis_size("dp"), lax.axis_size("tensor")
    rows, feats = tokens.shape
    blocks, bs = delta.shape[0], delta.shape[1]
    slab = frozen.shape[1]
    half = slab // 2
    mine, theirs = group * half, (1 - group) * half
    sizes = piece_sizes(half, bs)
    firsts = [sum(sizes[:p]) for p in range(len(sizes))]

    shards = [
        lax.dynamic_slice(frozen, (0, mine + first), (frozen.shape[0], size))
        for first, size in zip(firsts, sizes)
    ]
    gather_a = lax.all_gather(shards[0], "dp")

    row_part = block_rows * bs // feats
    block_info = jnp.stack(
        [
            row_part ^ me_t,
            row_part,
            block_rows * bs - row_part * feats,
            block_cols * bs - (me_t * slab + mine),
        ],
        axis=1,
    )
    meta = jnp.concatenate([jnp.arange(n_t, dtype=jnp.int32) ^ me_t, block_info.reshape(-1)])

    peer = swap(tokens, "groups", 1)
    own_x = swap(tokens, "tensor", 2)
    peer_x = swap(peer, "tensor", 2)
    near_x = jnp.concatenate([tokens, peer], axis=0)
    far_x = jnp.concatenate([own_x, peer_x], axis=0)
    x4 = jnp.stack([near_x, swap(near_x, "tensor", 1), far_x, swap(far_x, "tensor", 1)])

    order = peer_x
    d_pieces = []
    for first, size in zip(firsts, sizes):
        give = lax.dynamic_slice(d_out, (0, theirs + first), (rows, size))
        keep = lax.dynamic_slice(d_out, (0, mine + first), (rows, size))
        got = swap(tie(give, order), "groups", 1)
        order = got
        d_pieces.append(jnp.concatenate([keep, got], axis=0))

    gather_b = lax.all_gather(tie(shards[1], gather_a, x4, *d_pieces), "dp")
    act_a, slope_a, sums_a = forward(meta, x4, gather_a, delta, d_pieces[0], firsts[0], 2)
    back_a = swap(act_a[1], "groups", 1)
    (early,) = backward(meta, [slope_a], [gather_a], delta, firsts[:1], None, None)
    activated = jnp.zeros((rows, slab), BF)
    activated = lax.dynamic_update_slice(activated, act_a[0], (0, mine + firsts[0]))
    activated = lax.dynamic_update_slice(activated, back_a, (0, theirs + firsts[0]))

    delta_b = tie(delta, early, activated)
    act_b, slope_b, sums_b = forward(meta, x4, gather_b, delta_b, d_pieces[1], firsts[1], 2)
    back_b = swap(act_b[1], "groups", 1)
    activated = lax.dynamic_update_slice(activated, act_b[0], (0, mine + firsts[1]))
    activated = lax.dynamic_update_slice(activated, back_b, (0, theirs + firsts[1]))

    def back_of(bit, *wait):
        d = tie(delta_b, *wait) if wait else delta_b
        return backward(meta, [slope_b], [gather_b], d, firsts[1:], early, bit)

    sums = sums_a + sums_b
    sums = sums[0] + swap(sums[1].astype(BF), "groups", 1).astype(F32)
    far_own_give, far_peer_give, far_own, far_peer = back_of(3)
    far_peer_got = swap(far_peer_give, "tensor", 1)
    far_own_got = swap(far_own_give, "tensor", 1)
    near_own_give, near_peer_give, near_own, near_peer = back_of(1, far_peer)
    near_peer_got = swap(near_peer_give, "tensor", 1)
    near_own_got = swap(near_own_give, "tensor", 1)
    cut = rows // 2
    far_peer, far_own = tie(far_peer, near_peer), tie(far_own, near_peer)
    far_peer = far_peer.astype(F32) + far_peer_got.astype(F32)
    far_own = far_own.astype(F32) + far_own_got.astype(F32)
    near_peer = near_peer.astype(F32) + near_peer_got.astype(F32)
    over_x = swap(jnp.concatenate([far_peer[:cut], far_own[:cut]], axis=0).astype(BF), "tensor", 2)
    over_y = swap(
        jnp.concatenate([near_peer[cut:], far_peer[cut:]], axis=0).astype(BF), "groups", 1
    )
    shares = [swap(tie(sums.astype(BF), near_peer), "dp", bit) for bit in range(1, n_dp)]
    far_own = (far_own[cut:] + over_y[cut:].astype(F32)).astype(BF)
    near_peer = (near_peer[:cut] + over_x[:cut].astype(F32)).astype(BF)
    last_x = swap(tie(far_own, *shares[:1]), "tensor", 2)
    last_y = swap(tie(near_peer, back_b, *shares[:1]), "groups", 1)
    from_x = jnp.concatenate([over_x[cut:], last_x], axis=0)
    from_y = jnp.concatenate([last_y, over_y[:cut]], axis=0)
    near_own = near_own.astype(F32) + near_own_got.astype(F32)
    d_tokens = near_own + from_y.astype(F32) + from_x.astype(F32)
    for share in shares:
        sums = sums + share.astype(F32)
    norm = float(rows * n_dp) ** (-0.5)
    return (activated, d_tokens.astype(BF), pick_slots(owners, sums * norm))


def local_any(tokens, frozen, delta, block_rows, block_cols, owners, d_out):
    me_dp, me_t, n_dp = lax.axis_index("dp"), lax.axis_index("tensor"), lax.axis_size("dp")
    rows = tokens.shape[0]
    blocks, bs = delta.shape[0], delta.shape[1]
    slab = frozen.shape[1]
    x_full = lax.all_gather(tokens, "tensor", axis=1, tiled=True)
    weight = lax.all_gather(frozen, "dp", axis=0, tiled=True)
    width = x_full.shape[1]
    row_pick = (block_rows[:, None] == jnp.arange(width // bs)[None, :]).astype(F32)
    cols_here = block_cols - me_t * (slab // bs)
    col_pick = (cols_here[:, None] == jnp.arange(slab // bs)[None, :]).astype(F32)
    highest = lax.Precision.HIGHEST
    xb = jnp.take(x_full.reshape(rows, width // bs, bs), block_rows, axis=1)
    contrib = jnp.einsum("tnk,nkc->tnc", xb, delta, preferred_element_type=F32)
    add = jnp.einsum("tnc,nm->tmc", contrib, col_pick, precision=highest).reshape(rows, slab)
    preact = jnp.dot(x_full, weight, preferred_element_type=F32) + add
    squash = jax.nn.sigmoid(preact)
    activated = (preact * squash).astype(BF)
    d_pre = (d_out.astype(F32) * squash * (1.0 + preact * (1.0 - squash))).astype(BF)
    d_rows = lax.dot_general(
        d_pre, weight, (((1,), (1,)), ((), ())), preferred_element_type=F32
    )
    dy = jnp.take(d_pre.reshape(rows, slab // bs, bs), cols_here, axis=1)
    back = jnp.einsum("tnc,nkc->tnk", dy, delta, preferred_element_type=F32)
    back = jnp.einsum("tnk,nr->trk", back, row_pick, precision=highest).reshape(rows, width)
    d_tokens = lax.psum_scatter(
        (d_rows + back).astype(BF), "tensor", scatter_dimension=1, tiled=True
    )
    grads = jnp.einsum("tnk,tnc->nkc", xb, dy, preferred_element_type=F32)
    everyone = lax.all_gather(grads.astype(BF), "dp", axis=0).astype(F32)
    norm = float(rows * n_dp) ** (-0.5)
    return (activated, d_tokens, pick_slots(owners, jnp.sum(everyone, axis=0) * norm))


def solution(mesh):
    sizes = dict(mesh.shape)
    small = sizes["groups"] == 2 and sizes["dp"] == 4 and sizes["tensor"] == 4
    body = local if small else local_any
    in_specs = (
        P(("groups", "dp"), "tensor"),
        P("dp", "tensor"),
        P("tensor", None, None),
        P("tensor"),
        P("tensor"),
        P("tensor", None),
        P(("groups", "dp"), "tensor"),
    )
    out_specs = (
        P(("groups", "dp"), "tensor"),
        P(("groups", "dp"), "tensor"),
        P("tensor", ("groups", "dp"), None, None),
    )
    return jax.shard_map(body, mesh=mesh, in_specs=in_specs, out_specs=out_specs, check_vma=False)
```

```python
import functools

import jax
import jax.numpy as jnp
from jax import lax
from jax.experimental import pallas as pl
from jax.experimental.pallas import tpu as pltpu
from jax.sharding import PartitionSpec as P

CAP = 2
BF = jnp.bfloat16
F32 = jnp.float32
VMEM_BYTES = 30 * 2**20


def swap(array, axis, bit):
    size = lax.axis_size(axis)
    return lax.ppermute(array, axis, [(i, i ^ bit) for i in range(size)])


def params():
    return pltpu.CompilerParams(vmem_limit_bytes=VMEM_BYTES)


PARTS, BLOCKS = 0, 4


def forward_kernel(
    first, blocks, bs, cuts, meta, x_ref, w_ref, delta_ref, d_ref, act_ref, slope_ref, sum_ref, acc
):
    width = acc.shape[1]
    group = pl.program_id(1) // cuts

    @pl.when((pl.program_id(0) == 0) & (pl.program_id(1) == 0))
    def _():
        sum_ref[...] = jnp.zeros_like(sum_ref)

    total = None
    for s in range(w_ref.shape[0]):
        term = jnp.dot(x_ref[meta[PARTS + s]], w_ref[s], preferred_element_type=F32)
        total = term if total is None else total + term
    acc[...] = total
    start = first + pl.program_id(0) * width
    for n in range(blocks):
        at = BLOCKS + 4 * n
        col = meta[at + 3] - start

        @pl.when((col >= 0) & (col < width))
        def _():
            cols = pl.ds(pl.multiple_of(col, bs), bs)
            rows = pl.ds(pl.multiple_of(meta[at + 2], bs), bs)
            xs = x_ref[meta[at], :, rows]
            acc[:, cols] += jnp.dot(xs, delta_ref[n], preferred_element_type=F32)

    preact = acc[...]
    squash = jax.nn.sigmoid(preact)
    act_ref[0] = (preact * squash).astype(BF)
    slope_ref[...] = (
        d_ref[...].astype(F32) * squash * (1.0 + preact * (1.0 - squash))
    ).astype(BF)
    for n in range(blocks):
        at = BLOCKS + 4 * n
        col = meta[at + 3] - start

        @pl.when((col >= 0) & (col < width))
        def _():
            rows = pl.ds(pl.multiple_of(meta[at + 2], bs), bs)
            ds = slope_ref[:, pl.ds(pl.multiple_of(col, bs), bs)]
            sum_ref[group, n] += lax.dot_general(
                x_ref[meta[at], :, rows], ds, (((0,), (0,)), ((), ())), preferred_element_type=F32
            )


def forward(meta, x4, w4, delta, d_piece, first, groups_of):
    rows, width = d_piece.shape
    slots, feats = w4.shape[0], w4.shape[1]
    cuts = 1
    tile = rows // groups_of // cuts
    blocks, bs = delta.shape[0], delta.shape[1]
    wide = next(c for c in (512, 384, 256, 128, width) if width % c == 0)
    return pl.pallas_call(
        functools.partial(forward_kernel, first, blocks, bs, cuts),
        grid_spec=pltpu.PrefetchScalarGridSpec(
            num_scalar_prefetch=1,
            grid=(width // wide, groups_of * cuts),
            in_specs=[
                pl.BlockSpec((slots, tile, feats), lambda j, i, m: (0, i, 0)),
                pl.BlockSpec((slots, feats, wide), lambda j, i, m: (0, 0, j)),
                pl.BlockSpec(delta.shape, lambda j, i, m: (0, 0, 0)),
                pl.BlockSpec((tile, wide), lambda j, i, m: (i, j)),
            ],
            out_specs=[
                pl.BlockSpec((1, tile, wide), lambda j, i, m: (i // cuts, i % cuts, j)),
                pl.BlockSpec((tile, wide), lambda j, i, m: (i, j)),
                pl.BlockSpec((groups_of, blocks, bs, bs), lambda j, i, m: (0, 0, 0, 0)),
            ],
            scratch_shapes=[pltpu.VMEM((tile, wide), F32)],
        ),
        out_shape=[
            jax.ShapeDtypeStruct((groups_of, rows // groups_of, width), BF),
            jax.ShapeDtypeStruct((rows, width), BF),
            jax.ShapeDtypeStruct((groups_of, blocks, bs, bs), F32),
        ],
        compiler_params=params(),
        cost_estimate=pl.CostEstimate(flops=1, bytes_accessed=1, transcendentals=0),
    )(meta, x4, w4, delta, d_piece)


def backward_kernel(firsts, blocks, bs, has_acc, bit, meta, *refs):
    n = len(firsts)
    slopes, w_refs = refs[:n], refs[n : 2 * n]
    delta_ref = refs[2 * n]
    acc_in = refs[2 * n + 1] if has_acc else None
    outs, acc = refs[2 * n + 1 + has_acc : -1], refs[-1]
    size = acc.shape[1]
    step = pl.program_id(0)
    slot = step if bit is None else meta[PARTS + bit - step]
    base = pl.program_id(1) * size
    total = acc_in[0].astype(F32) if has_acc else None
    for p in range(n):
        term = lax.dot_general(
            slopes[p][...], w_refs[p][0], (((1,), (1,)), ((), ())), preferred_element_type=F32
        )
        total = term if total is None else total + term
    acc[...] = total
    for b in range(blocks):
        at = BLOCKS + 4 * b
        row = meta[at + 2] - base
        for p in range(n):
            col = meta[at + 3] - firsts[p]
            inside = (row >= 0) & (row < size) & (col >= 0) & (col < slopes[p].shape[1])

            @pl.when(inside & (meta[at + 1] == slot))
            def _():
                ds = slopes[p][:, pl.ds(pl.multiple_of(col, bs), bs)]
                acc[:, pl.ds(pl.multiple_of(row, bs), bs)] += lax.dot_general(
                    ds, delta_ref[b], (((1,), (1,)), ((), ())), preferred_element_type=F32
                )

    if len(outs) == 1:
        outs[0][0] = acc[...].astype(BF)
        return
    cut = outs[0].shape[0]
    for at_step in range(2):

        @pl.when(step == at_step)
        def _():
            outs[2 * at_step][...] = acc[:cut].astype(BF)
            outs[2 * at_step + 1][...] = acc[cut:].astype(BF)


def backward(meta, slopes, ws, delta, firsts, acc, bit):
    rows = slopes[0].shape[0]
    slots, feats = ws[0].shape[0], ws[0].shape[1]
    blocks, bs = delta.shape[0], delta.shape[1]
    every = bit is None
    tiles = 4 if every else 2
    size = feats // tiles
    width = sum(s.shape[1] for s in slopes)
    steps = slots if every else 2

    def slot_of(step, meta):
        return step if every else meta[PARTS + bit - step]

    whole = pl.BlockSpec((1, rows, size), lambda s, i, m: (slot_of(s, m), 0, i))
    give = pl.BlockSpec((rows // 2, size), lambda s, i, m: (0, jnp.where(s == 0, i, tiles - 1)))
    keep = pl.BlockSpec((rows // 2, size), lambda s, i, m: (0, jnp.where(s == 0, 0, i)))
    if every:
        out_specs = [whole]
        out_shape = [jax.ShapeDtypeStruct((slots, rows, feats), BF)]
    else:
        out_specs = [give, give, keep, keep]
        out_shape = [jax.ShapeDtypeStruct((rows // 2, feats), BF)] * 4
    return pl.pallas_call(
        functools.partial(backward_kernel, firsts, blocks, bs, acc is not None, bit),
        grid_spec=pltpu.PrefetchScalarGridSpec(
            num_scalar_prefetch=1,
            grid=(steps, tiles),
            in_specs=[
                pl.BlockSpec(s.shape, lambda s, i, m: (0, 0), pipeline_mode=pl.Buffered(1))
                for s in slopes
            ]
            + [
                pl.BlockSpec((1, size, w.shape[2]), lambda s, i, m: (slot_of(s, m), i, 0))
                for w in ws
            ]
            + [pl.BlockSpec(delta.shape, lambda s, i, m: (0, 0, 0))]
            + ([] if acc is None else [whole]),
            out_specs=out_specs,
            scratch_shapes=[pltpu.VMEM((rows, size), F32)],
        ),
        out_shape=out_shape,
        compiler_params=params(),
        cost_estimate=pl.CostEstimate(flops=1, bytes_accessed=1, transcendentals=0),
    )(meta, *slopes, *ws, delta, *([] if acc is None else [acc]))


def slot_ranks(owners):
    owner_ids = owners[:, 0]
    order = jnp.arange(owner_ids.shape[0], dtype=jnp.int32)
    earlier = (owner_ids[None, :] == owner_ids[:, None]) & (order[None, :] < order[:, None])
    rank = jnp.sum(earlier.astype(jnp.int32), axis=1)
    return (owner_ids[None, :] == lax.axis_index("dp")) & (
        rank[None, :] == jnp.arange(CAP, dtype=jnp.int32)[:, None]
    )


def pick_slots(owners, total):
    wanted = slot_ranks(owners)
    return jnp.sum(jnp.where(wanted[:, :, None, None], total[None], 0.0), axis=1)[None]


def tie(value, *after):
    return lax.optimization_barrier((value,) + after)[0]


def piece_sizes(half, bs):
    last = max(half // bs // 5, 1) * bs
    return [half - last, last]


def local(tokens, frozen, delta, block_rows, block_cols, owners, d_out):
    group, me_dp, me_t = (lax.axis_index(a) for a in ("groups", "dp", "tensor"))
    n_dp, n_t = lax.axis_size("dp"), lax.axis_size("tensor")
    rows, feats = tokens.shape
    blocks, bs = delta.shape[0], delta.shape[1]
    slab = frozen.shape[1]
    half = slab // 2
    mine, theirs = group * half, (1 - group) * half
    sizes = piece_sizes(half, bs)
    firsts = [sum(sizes[:p]) for p in range(len(sizes))]

    shards = [
        lax.dynamic_slice(frozen, (0, mine + first), (frozen.shape[0], size))
        for first, size in zip(firsts, sizes)
    ]
    gather_a = lax.all_gather(shards[0], "dp")

    row_part = block_rows * bs // feats
    block_info = jnp.stack(
        [
            row_part ^ me_t,
            row_part,
            block_rows * bs - row_part * feats,
            block_cols * bs - (me_t * slab + mine),
        ],
        axis=1,
    )
    meta = jnp.concatenate([jnp.arange(n_t, dtype=jnp.int32) ^ me_t, block_info.reshape(-1)])

    peer = swap(tokens, "groups", 1)
    own_x = swap(tokens, "tensor", 2)
    peer_x = swap(peer, "tensor", 2)
    near_x = jnp.concatenate([tokens, peer], axis=0)
    far_x = jnp.concatenate([own_x, peer_x], axis=0)
    x4 = jnp.stack([near_x, swap(near_x, "tensor", 1), far_x, swap(far_x, "tensor", 1)])

    order = peer_x
    d_pieces = []
    for first, size in zip(firsts, sizes):
        give = lax.dynamic_slice(d_out, (0, theirs + first), (rows, size))
        keep = lax.dynamic_slice(d_out, (0, mine + first), (rows, size))
        got = swap(tie(give, order), "groups", 1)
        order = got
        d_pieces.append(jnp.concatenate([keep, got], axis=0))

    gather_b = lax.all_gather(tie(shards[1], gather_a, x4, *d_pieces), "dp")
    act_a, slope_a, sums_a = forward(meta, x4, gather_a, delta, d_pieces[0], firsts[0], 2)
    back_a = swap(act_a[1], "groups", 1)
    (early,) = backward(meta, [slope_a], [gather_a], delta, firsts[:1], None, None)
    activated = jnp.zeros((rows, slab), BF)
    activated = lax.dynamic_update_slice(activated, act_a[0], (0, mine + firsts[0]))
    activated = lax.dynamic_update_slice(activated, back_a, (0, theirs + firsts[0]))

    delta_b = tie(delta, early, activated)
    act_b, slope_b, sums_b = forward(meta, x4, gather_b, delta_b, d_pieces[1], firsts[1], 2)
    back_b = swap(act_b[1], "groups", 1)
    activated = lax.dynamic_update_slice(activated, act_b[0], (0, mine + firsts[1]))
    activated = lax.dynamic_update_slice(activated, back_b, (0, theirs + firsts[1]))

    def back_of(bit, *wait):
        d = tie(delta_b, *wait) if wait else delta_b
        return backward(meta, [slope_b], [gather_b], d, firsts[1:], early, bit)

    sums = sums_a + sums_b
    sums = sums[0] + swap(sums[1].astype(BF), "groups", 1).astype(F32)
    far_own_give, far_peer_give, far_own, far_peer = back_of(3)
    far_peer_got = swap(far_peer_give, "tensor", 1)
    far_own_got = swap(far_own_give, "tensor", 1)
    near_own_give, near_peer_give, near_own, near_peer = back_of(1, far_peer)
    near_peer_got = swap(near_peer_give, "tensor", 1)
    near_own_got = swap(near_own_give, "tensor", 1)
    cut = rows // 2
    far_peer, far_own = tie(far_peer, near_peer, sums), tie(far_own, near_peer, back_b)
    far_peer = far_peer.astype(F32) + far_peer_got.astype(F32)
    far_own = far_own.astype(F32) + far_own_got.astype(F32)
    near_peer = near_peer.astype(F32) + near_peer_got.astype(F32)
    over_x = swap(jnp.concatenate([far_peer[:cut], far_own[:cut]], axis=0).astype(BF), "tensor", 2)
    over_y = swap(
        jnp.concatenate([near_peer[cut:], far_peer[cut:]], axis=0).astype(BF), "groups", 1
    )
    shares = [swap(tie(sums.astype(BF), near_peer), "dp", bit) for bit in range(1, n_dp)]
    far_own = (far_own[cut:] + over_y[cut:].astype(F32)).astype(BF)
    near_peer = (near_peer[:cut] + over_x[:cut].astype(F32)).astype(BF)
    last_x = swap(tie(far_own, *shares[:1]), "tensor", 2)
    last_y = swap(tie(near_peer, *shares[:1]), "groups", 1)
    from_x = jnp.concatenate([over_x[cut:], last_x], axis=0)
    from_y = jnp.concatenate([last_y, over_y[:cut]], axis=0)
    near_own = near_own.astype(F32) + near_own_got.astype(F32)
    d_tokens = near_own + from_y.astype(F32) + from_x.astype(F32)
    for share in shares:
        sums = sums + share.astype(F32)
    norm = float(rows * n_dp) ** (-0.5)
    return (activated, d_tokens.astype(BF), pick_slots(owners, sums * norm))


def local_any(tokens, frozen, delta, block_rows, block_cols, owners, d_out):
    me_dp, me_t, n_dp = lax.axis_index("dp"), lax.axis_index("tensor"), lax.axis_size("dp")
    rows = tokens.shape[0]
    blocks, bs = delta.shape[0], delta.shape[1]
    slab = frozen.shape[1]
    x_full = lax.all_gather(tokens, "tensor", axis=1, tiled=True)
    weight = lax.all_gather(frozen, "dp", axis=0, tiled=True)
    width = x_full.shape[1]
    row_pick = (block_rows[:, None] == jnp.arange(width // bs)[None, :]).astype(F32)
    cols_here = block_cols - me_t * (slab // bs)
    col_pick = (cols_here[:, None] == jnp.arange(slab // bs)[None, :]).astype(F32)
    highest = lax.Precision.HIGHEST
    xb = jnp.take(x_full.reshape(rows, width // bs, bs), block_rows, axis=1)
    contrib = jnp.einsum("tnk,nkc->tnc", xb, delta, preferred_element_type=F32)
    add = jnp.einsum("tnc,nm->tmc", contrib, col_pick, precision=highest).reshape(rows, slab)
    preact = jnp.dot(x_full, weight, preferred_element_type=F32) + add
    squash = jax.nn.sigmoid(preact)
    activated = (preact * squash).astype(BF)
    d_pre = (d_out.astype(F32) * squash * (1.0 + preact * (1.0 - squash))).astype(BF)
    d_rows = lax.dot_general(
        d_pre, weight, (((1,), (1,)), ((), ())), preferred_element_type=F32
    )
    dy = jnp.take(d_pre.reshape(rows, slab // bs, bs), cols_here, axis=1)
    back = jnp.einsum("tnc,nkc->tnk", dy, delta, preferred_element_type=F32)
    back = jnp.einsum("tnk,nr->trk", back, row_pick, precision=highest).reshape(rows, width)
    d_tokens = lax.psum_scatter(
        (d_rows + back).astype(BF), "tensor", scatter_dimension=1, tiled=True
    )
    grads = jnp.einsum("tnk,tnc->nkc", xb, dy, preferred_element_type=F32)
    everyone = lax.all_gather(grads.astype(BF), "dp", axis=0).astype(F32)
    norm = float(rows * n_dp) ** (-0.5)
    return (activated, d_tokens, pick_slots(owners, jnp.sum(everyone, axis=0) * norm))


def solution(mesh):
    sizes = dict(mesh.shape)
    small = sizes["groups"] == 2 and sizes["dp"] == 4 and sizes["tensor"] == 4
    body = local if small else local_any
    in_specs = (
        P(("groups", "dp"), "tensor"),
        P("dp", "tensor"),
        P("tensor", None, None),
        P("tensor"),
        P("tensor"),
        P("tensor", None),
        P(("groups", "dp"), "tensor"),
    )
    out_specs = (
        P(("groups", "dp"), "tensor"),
        P(("groups", "dp"), "tensor"),
        P("tensor", ("groups", "dp"), None, None),
    )
    return jax.shard_map(body, mesh=mesh, in_specs=in_specs, out_specs=out_specs, check_vma=False)
```

```python
import functools

import jax
import jax.numpy as jnp
from jax import lax
from jax.experimental import pallas as pl
from jax.experimental.pallas import tpu as pltpu
from jax.sharding import PartitionSpec as P

CAP = 2
BF = jnp.bfloat16
F32 = jnp.float32
VMEM_BYTES = 25 * 2**20


def swap(array, axis, bit):
    size = lax.axis_size(axis)
    return lax.ppermute(array, axis, [(i, i ^ bit) for i in range(size)])


def params():
    return pltpu.CompilerParams(vmem_limit_bytes=VMEM_BYTES)


PARTS, BLOCKS = 0, 4


def forward_kernel(
    first, blocks, bs, cuts, meta, x_ref, w_ref, delta_ref, d_ref, act_ref, slope_ref, sum_ref, acc
):
    width = acc.shape[1]
    group = pl.program_id(1) // cuts

    @pl.when((pl.program_id(0) == 0) & (pl.program_id(1) == 0))
    def _():
        sum_ref[...] = jnp.zeros_like(sum_ref)

    total = None
    for s in range(w_ref.shape[0]):
        term = jnp.dot(x_ref[meta[PARTS + s]], w_ref[s], preferred_element_type=F32)
        total = term if total is None else total + term
    acc[...] = total
    start = first + pl.program_id(0) * width
    for n in range(blocks):
        at = BLOCKS + 4 * n
        col = meta[at + 3] - start

        @pl.when((col >= 0) & (col < width))
        def _():
            cols = pl.ds(pl.multiple_of(col, bs), bs)
            rows = pl.ds(pl.multiple_of(meta[at + 2], bs), bs)
            xs = x_ref[meta[at], :, rows]
            acc[:, cols] += jnp.dot(xs, delta_ref[n], preferred_element_type=F32)

    preact = acc[...]
    squash = jax.nn.sigmoid(preact)
    act_ref[0] = (preact * squash).astype(BF)
    slope_ref[...] = (
        d_ref[...].astype(F32) * squash * (1.0 + preact * (1.0 - squash))
    ).astype(BF)
    for n in range(blocks):
        at = BLOCKS + 4 * n
        col = meta[at + 3] - start

        @pl.when((col >= 0) & (col < width))
        def _():
            rows = pl.ds(pl.multiple_of(meta[at + 2], bs), bs)
            ds = slope_ref[:, pl.ds(pl.multiple_of(col, bs), bs)]
            sum_ref[group, n] += lax.dot_general(
                x_ref[meta[at], :, rows], ds, (((0,), (0,)), ((), ())), preferred_element_type=F32
            )


def forward(meta, x4, w4, delta, d_piece, first, groups_of):
    rows, width = d_piece.shape
    slots, feats = w4.shape[0], w4.shape[1]
    cuts = 1
    tile = rows // groups_of // cuts
    blocks, bs = delta.shape[0], delta.shape[1]
    wide = next(c for c in (512, 384, 256, 128, width) if width % c == 0)
    return pl.pallas_call(
        functools.partial(forward_kernel, first, blocks, bs, cuts),
        grid_spec=pltpu.PrefetchScalarGridSpec(
            num_scalar_prefetch=1,
            grid=(width // wide, groups_of * cuts),
            in_specs=[
                pl.BlockSpec((slots, tile, feats), lambda j, i, m: (0, i, 0)),
                pl.BlockSpec((slots, feats, wide), lambda j, i, m: (0, 0, j)),
                pl.BlockSpec(delta.shape, lambda j, i, m: (0, 0, 0)),
                pl.BlockSpec((tile, wide), lambda j, i, m: (i, j)),
            ],
            out_specs=[
                pl.BlockSpec((1, tile, wide), lambda j, i, m: (i // cuts, i % cuts, j)),
                pl.BlockSpec((tile, wide), lambda j, i, m: (i, j)),
                pl.BlockSpec((groups_of, blocks, bs, bs), lambda j, i, m: (0, 0, 0, 0)),
            ],
            scratch_shapes=[pltpu.VMEM((tile, wide), F32)],
        ),
        out_shape=[
            jax.ShapeDtypeStruct((groups_of, rows // groups_of, width), BF),
            jax.ShapeDtypeStruct((rows, width), BF),
            jax.ShapeDtypeStruct((groups_of, blocks, bs, bs), F32),
        ],
        compiler_params=params(),
        cost_estimate=pl.CostEstimate(flops=1, bytes_accessed=1, transcendentals=0),
    )(meta, x4, w4, delta, d_piece)


def backward_kernel(firsts, blocks, bs, has_acc, bit, meta, *refs):
    n = len(firsts)
    slopes, w_refs = refs[:n], refs[n : 2 * n]
    delta_ref = refs[2 * n]
    acc_in = refs[2 * n + 1] if has_acc else None
    outs, acc = refs[2 * n + 1 + has_acc : -1], refs[-1]
    size = acc.shape[1]
    step = pl.program_id(0)
    slot = step if bit is None else meta[PARTS + bit - step]
    base = pl.program_id(1) * size
    total = acc_in[0].astype(F32) if has_acc else None
    for p in range(n):
        term = lax.dot_general(
            slopes[p][...], w_refs[p][0], (((1,), (1,)), ((), ())), preferred_element_type=F32
        )
        total = term if total is None else total + term
    acc[...] = total
    for b in range(blocks):
        at = BLOCKS + 4 * b
        row = meta[at + 2] - base
        for p in range(n):
            col = meta[at + 3] - firsts[p]
            inside = (row >= 0) & (row < size) & (col >= 0) & (col < slopes[p].shape[1])

            @pl.when(inside & (meta[at + 1] == slot))
            def _():
                ds = slopes[p][:, pl.ds(pl.multiple_of(col, bs), bs)]
                acc[:, pl.ds(pl.multiple_of(row, bs), bs)] += lax.dot_general(
                    ds, delta_ref[b], (((1,), (1,)), ((), ())), preferred_element_type=F32
                )

    if len(outs) == 1:
        outs[0][0] = acc[...].astype(BF)
        return
    cut = outs[0].shape[0]
    for at_step in range(2):

        @pl.when(step == at_step)
        def _():
            outs[2 * at_step][...] = acc[:cut].astype(BF)
            outs[2 * at_step + 1][...] = acc[cut:].astype(BF)


def backward(meta, slopes, ws, delta, firsts, acc, bit):
    rows = slopes[0].shape[0]
    slots, feats = ws[0].shape[0], ws[0].shape[1]
    blocks, bs = delta.shape[0], delta.shape[1]
    every = bit is None
    tiles = 4 if every else 2
    size = feats // tiles
    width = sum(s.shape[1] for s in slopes)
    steps = slots if every else 2

    def slot_of(step, meta):
        return step if every else meta[PARTS + bit - step]

    whole = pl.BlockSpec((1, rows, size), lambda s, i, m: (slot_of(s, m), 0, i))
    give = pl.BlockSpec((rows // 2, size), lambda s, i, m: (0, jnp.where(s == 0, i, tiles - 1)))
    keep = pl.BlockSpec((rows // 2, size), lambda s, i, m: (0, jnp.where(s == 0, 0, i)))
    if every:
        out_specs = [whole]
        out_shape = [jax.ShapeDtypeStruct((slots, rows, feats), BF)]
    else:
        out_specs = [give, give, keep, keep]
        out_shape = [jax.ShapeDtypeStruct((rows // 2, feats), BF)] * 4
    return pl.pallas_call(
        functools.partial(backward_kernel, firsts, blocks, bs, acc is not None, bit),
        grid_spec=pltpu.PrefetchScalarGridSpec(
            num_scalar_prefetch=1,
            grid=(steps, tiles),
            in_specs=[
                pl.BlockSpec(s.shape, lambda s, i, m: (0, 0), pipeline_mode=pl.Buffered(1))
                for s in slopes
            ]
            + [
                pl.BlockSpec((1, size, w.shape[2]), lambda s, i, m: (slot_of(s, m), i, 0))
                for w in ws
            ]
            + [pl.BlockSpec(delta.shape, lambda s, i, m: (0, 0, 0))]
            + ([] if acc is None else [whole]),
            out_specs=out_specs,
            scratch_shapes=[pltpu.VMEM((rows, size), F32)],
        ),
        out_shape=out_shape,
        compiler_params=params(),
        cost_estimate=pl.CostEstimate(flops=1, bytes_accessed=1, transcendentals=0),
    )(meta, *slopes, *ws, delta, *([] if acc is None else [acc]))


def slot_ranks(owners):
    owner_ids = owners[:, 0]
    order = jnp.arange(owner_ids.shape[0], dtype=jnp.int32)
    earlier = (owner_ids[None, :] == owner_ids[:, None]) & (order[None, :] < order[:, None])
    rank = jnp.sum(earlier.astype(jnp.int32), axis=1)
    return (owner_ids[None, :] == lax.axis_index("dp")) & (
        rank[None, :] == jnp.arange(CAP, dtype=jnp.int32)[:, None]
    )


def pick_slots(owners, total):
    wanted = slot_ranks(owners)
    return jnp.sum(jnp.where(wanted[:, :, None, None], total[None], 0.0), axis=1)[None]


def tie(value, *after):
    return lax.optimization_barrier((value,) + after)[0]


def piece_sizes(half, bs):
    last = max(half // bs // 5, 1) * bs
    return [half - last, last]


def local(tokens, frozen, delta, block_rows, block_cols, owners, d_out):
    group, me_dp, me_t = (lax.axis_index(a) for a in ("groups", "dp", "tensor"))
    n_dp, n_t = lax.axis_size("dp"), lax.axis_size("tensor")
    rows, feats = tokens.shape
    blocks, bs = delta.shape[0], delta.shape[1]
    slab = frozen.shape[1]
    half = slab // 2
    mine, theirs = group * half, (1 - group) * half
    sizes = piece_sizes(half, bs)
    firsts = [sum(sizes[:p]) for p in range(len(sizes))]

    shards = [
        lax.dynamic_slice(frozen, (0, mine + first), (frozen.shape[0], size))
        for first, size in zip(firsts, sizes)
    ]
    gather_a = lax.all_gather(shards[0], "dp")

    row_part = block_rows * bs // feats
    block_info = jnp.stack(
        [
            row_part ^ me_t,
            row_part,
            block_rows * bs - row_part * feats,
            block_cols * bs - (me_t * slab + mine),
        ],
        axis=1,
    )
    meta = jnp.concatenate([jnp.arange(n_t, dtype=jnp.int32) ^ me_t, block_info.reshape(-1)])

    peer = swap(tokens, "groups", 1)
    own_x = swap(tokens, "tensor", 2)
    peer_x = swap(peer, "tensor", 2)
    near_x = jnp.concatenate([tokens, peer], axis=0)
    far_x = jnp.concatenate([own_x, peer_x], axis=0)
    x4 = jnp.stack([near_x, swap(near_x, "tensor", 1), far_x, swap(far_x, "tensor", 1)])

    order = peer_x
    d_pieces = []
    for first, size in zip(firsts, sizes):
        give = lax.dynamic_slice(d_out, (0, theirs + first), (rows, size))
        keep = lax.dynamic_slice(d_out, (0, mine + first), (rows, size))
        got = swap(tie(give, order), "groups", 1)
        order = got
        d_pieces.append(jnp.concatenate([keep, got], axis=0))

    gather_b = lax.all_gather(tie(shards[1], gather_a, x4, *d_pieces), "dp")
    act_a, slope_a, sums_a = forward(meta, x4, gather_a, delta, d_pieces[0], firsts[0], 2)
    back_a = swap(act_a[1], "groups", 1)
    (early,) = backward(meta, [slope_a], [gather_a], delta, firsts[:1], None, None)
    activated = jnp.zeros((rows, slab), BF)
    activated = lax.dynamic_update_slice(activated, act_a[0], (0, mine + firsts[0]))
    activated = lax.dynamic_update_slice(activated, back_a, (0, theirs + firsts[0]))

    delta_b = tie(delta, early, activated)
    act_b, slope_b, sums_b = forward(meta, x4, gather_b, delta_b, d_pieces[1], firsts[1], 2)
    back_b = swap(act_b[1], "groups", 1)
    activated = lax.dynamic_update_slice(activated, act_b[0], (0, mine + firsts[1]))
    activated = lax.dynamic_update_slice(activated, back_b, (0, theirs + firsts[1]))

    def back_of(bit, *wait):
        d = tie(delta_b, *wait) if wait else delta_b
        return backward(meta, [slope_b], [gather_b], d, firsts[1:], early, bit)

    sums = sums_a + sums_b
    sums = sums[0] + swap(sums[1].astype(BF), "groups", 1).astype(F32)
    far_own_give, far_peer_give, far_own, far_peer = back_of(3)
    far_peer_got = swap(far_peer_give, "tensor", 1)
    far_own_got = swap(far_own_give, "tensor", 1)
    near_own_give, near_peer_give, near_own, near_peer = back_of(1, far_peer)
    near_peer_got = swap(near_peer_give, "tensor", 1)
    near_own_got = swap(near_own_give, "tensor", 1)
    cut = rows // 2
    far_peer, far_own = tie(far_peer, near_peer, sums), tie(far_own, near_peer, back_b)
    far_peer = far_peer.astype(F32) + far_peer_got.astype(F32)
    far_own = far_own.astype(F32) + far_own_got.astype(F32)
    near_peer = near_peer.astype(F32) + near_peer_got.astype(F32)
    over_x = swap(jnp.concatenate([far_peer[:cut], far_own[:cut]], axis=0).astype(BF), "tensor", 2)
    over_y = swap(
        jnp.concatenate([near_peer[cut:], far_peer[cut:]], axis=0).astype(BF), "groups", 1
    )
    shares = [swap(tie(sums.astype(BF), near_peer), "dp", bit) for bit in range(1, n_dp)]
    far_own = (far_own[cut:] + over_y[cut:].astype(F32)).astype(BF)
    near_peer = (near_peer[:cut] + over_x[:cut].astype(F32)).astype(BF)
    last_x = swap(tie(far_own, *shares[:1]), "tensor", 2)
    last_y = swap(tie(near_peer, *shares[:1]), "groups", 1)
    from_x = jnp.concatenate([over_x[cut:], last_x], axis=0)
    from_y = jnp.concatenate([last_y, over_y[:cut]], axis=0)
    near_own = near_own.astype(F32) + near_own_got.astype(F32)
    d_tokens = near_own + from_y.astype(F32) + from_x.astype(F32)
    for share in shares:
        sums = sums + share.astype(F32)
    norm = float(rows * n_dp) ** (-0.5)
    return (activated, d_tokens.astype(BF), pick_slots(owners, sums * norm))


def local_any(tokens, frozen, delta, block_rows, block_cols, owners, d_out):
    me_dp, me_t, n_dp = lax.axis_index("dp"), lax.axis_index("tensor"), lax.axis_size("dp")
    rows = tokens.shape[0]
    blocks, bs = delta.shape[0], delta.shape[1]
    slab = frozen.shape[1]
    x_full = lax.all_gather(tokens, "tensor", axis=1, tiled=True)
    weight = lax.all_gather(frozen, "dp", axis=0, tiled=True)
    width = x_full.shape[1]
    row_pick = (block_rows[:, None] == jnp.arange(width // bs)[None, :]).astype(F32)
    cols_here = block_cols - me_t * (slab // bs)
    col_pick = (cols_here[:, None] == jnp.arange(slab // bs)[None, :]).astype(F32)
    highest = lax.Precision.HIGHEST
    xb = jnp.take(x_full.reshape(rows, width // bs, bs), block_rows, axis=1)
    contrib = jnp.einsum("tnk,nkc->tnc", xb, delta, preferred_element_type=F32)
    add = jnp.einsum("tnc,nm->tmc", contrib, col_pick, precision=highest).reshape(rows, slab)
    preact = jnp.dot(x_full, weight, preferred_element_type=F32) + add
    squash = jax.nn.sigmoid(preact)
    activated = (preact * squash).astype(BF)
    d_pre = (d_out.astype(F32) * squash * (1.0 + preact * (1.0 - squash))).astype(BF)
    d_rows = lax.dot_general(
        d_pre, weight, (((1,), (1,)), ((), ())), preferred_element_type=F32
    )
    dy = jnp.take(d_pre.reshape(rows, slab // bs, bs), cols_here, axis=1)
    back = jnp.einsum("tnc,nkc->tnk", dy, delta, preferred_element_type=F32)
    back = jnp.einsum("tnk,nr->trk", back, row_pick, precision=highest).reshape(rows, width)
    d_tokens = lax.psum_scatter(
        (d_rows + back).astype(BF), "tensor", scatter_dimension=1, tiled=True
    )
    grads = jnp.einsum("tnk,tnc->nkc", xb, dy, preferred_element_type=F32)
    everyone = lax.all_gather(grads.astype(BF), "dp", axis=0).astype(F32)
    norm = float(rows * n_dp) ** (-0.5)
    return (activated, d_tokens, pick_slots(owners, jnp.sum(everyone, axis=0) * norm))


def solution(mesh):
    sizes = dict(mesh.shape)
    small = sizes["groups"] == 2 and sizes["dp"] == 4 and sizes["tensor"] == 4
    body = local if small else local_any
    in_specs = (
        P(("groups", "dp"), "tensor"),
        P("dp", "tensor"),
        P("tensor", None, None),
        P("tensor"),
        P("tensor"),
        P("tensor", None),
        P(("groups", "dp"), "tensor"),
    )
    out_specs = (
        P(("groups", "dp"), "tensor"),
        P(("groups", "dp"), "tensor"),
        P("tensor", ("groups", "dp"), None, None),
    )
    return jax.shard_map(body, mesh=mesh, in_specs=in_specs, out_specs=out_specs, check_vma=False)
```
